32 devices in a mesh: section: 2 (over core), dp: 4 (over z), tensor: 4 (over y, x).
Axes of the slice: x: 2, y: 2, z: 4, core: 2. Of those that a mesh axis runs over, the one named last changes fastest.
Arguments:
- activations: bfloat16 [2, 2, 4096, 1024], P('section', None, ('dp', 'tensor')), may hold values from -6 to 6
- starts: int32 [2, 4, 4], P(None, 'dp'), may hold values from 0 to 1023, as said below
- attention_weights: bfloat16 [2, 3, 1024, 1024], P('section', None, None, 'tensor'), may hold values from -0.1875 to 0.1875
- projection_weight: bfloat16 [2, 1024, 1024], P('section', 'tensor'), may hold values from -0.75 to 0.75
- feedforward_weight: bfloat16 [2, 1024, 4096], P('section', None, 'tensor'), may hold values from -0.1875 to 0.1875
- output_weight: bfloat16 [2, 4096, 1024], P('section', 'tensor'), may hold values from -0.09375 to 0.09375
- norm_gains: float32 [2, 2, 1024], P('section'), may hold values from 0.1 to 1.9
- norm_biases: float32 [2, 2, 1024], P('section'), may hold values from -3 to 3
- output_biases: float32 [2, 2, 1024], P('section'), may hold values from -3 to 3
- query_value_bias: float32 [2, 2, 1024], P('section', None, 'tensor'), may hold values from -3 to 3
- feedforward_bias: float32 [2, 4096], P('section', 'tensor'), may hold values from -3 to 3
- adapter_down_weight: bfloat16 [2, 2, 1024, 4], P('section'), may hold values from -0.1875 to 0.1875
- adapter_up_weight: bfloat16 [2, 2, 4, 1024], P('section', None, None, 'tensor'), may hold values from -0.1875 to 0.1875
Outputs:
- combined: float32 [2, 2, 4096, 1024], P('section', None, ('dp', 'tensor'))
- grad_lora_a: float32 [2, 2, 1024, 4], P('section')
- grad_lora_b: float32 [2, 2, 4, 1024], P('section', None, None, 'tensor')
The draws below stay inside these ranges and needn't reach their ends.
Inputs may be any that keep to these rules, and one draw needn't show every extreme that they name: In each slot the first start is 0 and the 4 starts rise strictly, all below 1024.
All inputs are finite; a program needn't handle non-finite values.
Results may differ from the reference program's by a relative error of at most 0.0173.
Values may be sent and summed in bfloat16 or wider, within the bound.
No kernel may reach another device: no remote copies, remote signals or barrier semaphores. Data moves between devices by JAX's collectives and lax.ppermute only.
A program may use at most 192 MiB of HBM per device.

```python
import jax
import jax.numpy as jnp
from jax import lax

MODEL_WIDTH = 1024
HEADS = 16
HEAD = 64
FF = 4096
ADAPTER_RANK = 4
SEQ_LEN = 1024
DOCS = 4
MB = 2
SEQ_MB = 1
SLOTS = 4
ROWS = 4096
N_DP = 4


def draw_starts(key, part):
    key = jax.random.fold_in(key, 7)
    keys = jax.random.split(key, MB * SLOTS)

    def one_slot(slot_key):
        order = jax.random.permutation(slot_key, SEQ_LEN - 1)
        cuts = jnp.sort(order[:DOCS - 1]) + 1
        return jnp.concatenate([jnp.zeros((1,), jnp.int32), cuts.astype(jnp.int32)])
    drawn = jax.vmap(one_slot)(keys).reshape(MB, SLOTS, DOCS).astype(jnp.int32)
    return drawn.at[0, 0, DOCS - 1].set(SEQ_LEN - 1).astype(jnp.int32)


def block_levels(key, shape, pieces, smallest, largest):
    level, own = 1.0, jax.random.fold_in(key, 6)
    for position, parts in pieces:
        heights = jnp.exp(jax.random.uniform(jax.random.fold_in(own, position), (parts,), jnp.float32, smallest / len(pieces), largest / len(pieces)))
        level = level * jnp.repeat(heights, shape[position] // parts).reshape([-1 if axis == position else 1 for axis in range(len(shape))])
    return level


def gaussian(key, extent, width, most, pieces=(), kind=jnp.bfloat16):
    entries = width * jax.random.normal(key, extent, jnp.float32)
    if pieces:
        entries = entries * block_levels(key, extent, pieces, -0.22, 0.18)
    return jnp.clip(entries, -most, most).astype(kind)


def setup_inputs(seed: int = 0) -> dict:
    arg_keys = jax.random.split(jax.random.key(seed), 14)
    return {
        "activations": gaussian(arg_keys[0], (2, MB, ROWS, MODEL_WIDTH), 1.0, 6.0, ((0, 2), (2, 16))),
        "starts": draw_starts(jax.random.fold_in(arg_keys[13], 71), 0),
        "attention_weights": gaussian(arg_keys[2], (2, 3, MODEL_WIDTH, MODEL_WIDTH), MODEL_WIDTH ** -0.5, 0.1875, ((0, 2), (3, 4))),
        "projection_weight": gaussian(arg_keys[3], (2, MODEL_WIDTH, MODEL_WIDTH), (MODEL_WIDTH // 16) ** -0.5, 0.75, ((0, 2), (1, 4))),
        "feedforward_weight": gaussian(arg_keys[4], (2, MODEL_WIDTH, FF), MODEL_WIDTH ** -0.5, 0.1875, ((0, 2), (2, 4))),
        "output_weight": gaussian(arg_keys[5], (2, FF, MODEL_WIDTH), FF ** -0.5, 0.09375, ((0, 2), (1, 4))),
        "norm_gains": jnp.clip(1.0 + 0.18 * jax.random.normal(arg_keys[6], (2, 2, MODEL_WIDTH), jnp.float32), 0.1, 1.9),
        "norm_biases": gaussian(arg_keys[7], (2, 2, MODEL_WIDTH), 0.5, 3.0, ((0, 2),), jnp.float32),
        "output_biases": gaussian(arg_keys[8], (2, 2, MODEL_WIDTH), 0.5, 3.0, ((0, 2),), jnp.float32),
        "query_value_bias": gaussian(arg_keys[9], (2, 2, MODEL_WIDTH), 0.5, 3.0, ((0, 2), (2, 4)), jnp.float32),
        "feedforward_bias": gaussian(arg_keys[10], (2, FF), 0.5, 3.0, ((0, 2), (1, 4)), jnp.float32),
        "adapter_down_weight": gaussian(arg_keys[11], (2, 2, MODEL_WIDTH, ADAPTER_RANK), MODEL_WIDTH ** -0.5, 0.1875, ((0, 2),)),
        "adapter_up_weight": gaussian(arg_keys[12], (2, 2, ADAPTER_RANK, MODEL_WIDTH), MODEL_WIDTH ** -0.5, 0.1875, ((0, 2), (3, 4))),
    }


@jax.custom_vjp
def reduced_rows(v):
    return lax.optimization_barrier(v.astype(jnp.bfloat16)).astype(jnp.float32)

@jax.custom_vjp
def reduced_gradient(v):
    return v

def low_keep(v):
    return (reduced_rows(v), None)

def low_pass(kept, grad):
    return (grad,)

def back_keep(v):
    return (v, None)

def back_low(kept, grad):
    return (reduced_rows(grad),)
reduced_rows.defvjp(low_keep, low_pass)
reduced_gradient.defvjp(back_keep, back_low)
adapter_scale = 8.0

def matrix_product(left, right):
    return jnp.dot(left, right, precision=lax.Precision.HIGHEST, preferred_element_type=jnp.float32)

def layer_norm(rows, gain, shift):
    mean = lax.optimization_barrier(jnp.mean(rows, axis=-1, keepdims=True))
    centered = rows - mean
    spread = lax.optimization_barrier(jnp.mean(centered * centered, axis=-1, keepdims=True))
    return centered * lax.rsqrt(spread + 1e-05) * gain + shift

def gelu_tanh(value):
    return 0.5 * value * (1.0 + jnp.tanh(0.7978845608028654 * (value + 0.044715 * value * value * value)))

def doc_mask(doc_starts):
    positions = jnp.arange(SEQ_LEN, dtype=jnp.int32)
    labels = lax.optimization_barrier(jnp.sum((doc_starts[None, :] <= positions[:, None]).astype(jnp.int32), axis=1))
    return (positions[None, :] <= positions[:, None]) & (labels[:, None] == labels[None, :])

def attend(items):
    query_rows, keys, value_rows, doc_starts = items
    scores = jnp.einsum('qhd,khd->hqk', query_rows, keys, precision=lax.Precision.HIGHEST) * HEAD ** (-0.5)
    scores = reduced_gradient(scores)
    scores = jnp.where(doc_mask(doc_starts)[None], scores, -1e+30)
    top = lax.optimization_barrier(jnp.max(scores, axis=-1, keepdims=True))
    weights = jnp.exp(scores - top)
    total = lax.optimization_barrier(jnp.sum(weights, axis=-1, keepdims=True))
    probs = reduced_rows(weights / total)
    return jnp.einsum('hqk,khd->qhd', probs, value_rows, precision=lax.Precision.HIGHEST)

def layer(rows, group_starts, params):
    attention_weight, proj_w, fc_w, out_w, gains, shifts, biases, query_value_up, fc_b, down_map, lifting_weight = params
    span = SEQ_MB * SEQ_LEN
    normalized_rows = reduced_rows(layer_norm(rows, gains[0], shifts[0]))
    apply_adapter = reduced_gradient(reduced_rows(matrix_product(normalized_rows, jnp.concatenate([down_map[0], down_map[1]], axis=1))))
    query_rows = reduced_gradient(reduced_rows(matrix_product(normalized_rows, attention_weight[0]) + query_value_up[0] + adapter_scale * matrix_product(apply_adapter[:, :ADAPTER_RANK], lifting_weight[0])))
    keys = reduced_gradient(reduced_rows(matrix_product(normalized_rows, attention_weight[1])))
    value_rows = reduced_gradient(reduced_rows(matrix_product(normalized_rows, attention_weight[2]) + query_value_up[1] + adapter_scale * matrix_product(apply_adapter[:, ADAPTER_RANK:], lifting_weight[1])))
    shaped = (SEQ_MB, SEQ_LEN, HEADS, HEAD)
    mixed = lax.map(jax.checkpoint(attend), (query_rows.reshape(shaped), keys.reshape(shaped), value_rows.reshape(shaped), group_starts))
    heads_out = reduced_gradient(reduced_rows(mixed.reshape(span, MODEL_WIDTH)))
    middle = rows + reduced_gradient(matrix_product(heads_out, proj_w)) + biases[0]
    normed_two = reduced_rows(layer_norm(middle, gains[1], shifts[1]))
    hidden = reduced_gradient(matrix_product(normed_two, fc_w) + fc_b)
    active = reduced_rows(gelu_tanh(hidden))
    return middle + reduced_gradient(matrix_product(active, out_w)) + biases[1]

def reference(activations, starts, attention_weights, projection_weight, feedforward_weight, output_weight, norm_gains, norm_biases, output_biases, query_value_bias, feedforward_bias, adapter_down_weight, adapter_up_weight):
    frozen = tuple((weight.astype(jnp.float32) for weight in (attention_weights, projection_weight, feedforward_weight, output_weight))) + (norm_gains, norm_biases, output_biases, query_value_bias, feedforward_bias)
    input_rows = activations[0].astype(jnp.float32)
    cotangent = activations[1].astype(jnp.float32)
    groups = MB * N_DP
    span = SEQ_MB * SEQ_LEN
    doc_starts = starts.reshape(groups, SEQ_MB, DOCS)

    def forward_relay(input_rows, adapter_a, adapter_b):
        grouped = input_rows.reshape(groups, span, MODEL_WIDTH)

        def one_group(carry, items):
            rows, group_starts = items
            first_params = tuple((weight[0] for weight in frozen)) + (adapter_a[0], adapter_b[0])
            second_params = tuple((weight[1] for weight in frozen)) + (adapter_a[1], adapter_b[1])
            between = reduced_gradient(reduced_rows(layer(rows, group_starts, first_params)))
            return (carry, layer(between, group_starts, second_params))
        _, output_rows = lax.scan(jax.checkpoint(one_group), jnp.zeros((), jnp.float32), (grouped, doc_starts))
        return output_rows.reshape(MB, ROWS, MODEL_WIDTH)
    output_rows, backward_relay = jax.vjp(forward_relay, input_rows, adapter_down_weight.astype(jnp.float32), adapter_up_weight.astype(jnp.float32))
    grad_inputs, grad_a, grad_b = backward_relay(cotangent)
    return (jnp.stack([grad_inputs, output_rows]), grad_a, grad_b)
```

```python
import functools

import jax
import jax.numpy as jnp
from jax import lax
from jax.experimental import pallas as pl
from jax.experimental.pallas import tpu as pltpu
from jax.sharding import PartitionSpec as P

HEAD = 64
ADAPTER_RANK = 4
SEQ_LEN = 1024


adapter_scale = 8.0


def from_behind(block, axis, distance):
    devices = range(lax.axis_size(axis))
    route = [(i - distance, i) for i in devices if i - distance in devices]
    return lax.ppermute(block, axis, route)


def contract_axes(left, right, left_dim, right_dim):
    return lax.dot_general(
        left, right, (((left_dim,), (right_dim,)), ((), ())), preferred_element_type=jnp.float32
    )


def layer_norm(rows, gain, shift):
    mean = jnp.mean(rows, axis=-1, keepdims=True)
    centered = rows - mean
    spread = jnp.mean(centered * centered, axis=-1, keepdims=True)
    return centered * lax.rsqrt(spread + 1e-05) * gain + shift


def gelu_tanh(value):
    return (
        0.5
        * value
        * (1.0 + jnp.tanh(0.7978845608028654 * (value + 0.044715 * value * value * value)))
    )


def doc_mask(doc_starts):
    positions = jnp.arange(SEQ_LEN, dtype=jnp.int32)
    labels = jnp.sum((doc_starts[None, :] <= positions[:, None]).astype(jnp.int32), axis=1)
    return (positions[None, :] <= positions[:, None]) & (labels[:, None] == labels[None, :])


def masked_scores(query_rows, keys, doc_starts):
    scores = jnp.einsum(
        "qhd,khd->hqk", query_rows, keys, preferred_element_type=jnp.float32
    ) * HEAD ** (-0.5)
    return jnp.where(doc_mask(doc_starts)[None], scores, -1e30)


def attend(items):
    query_rows, keys, value_rows, doc_starts = items
    scores = masked_scores(query_rows, keys, doc_starts)
    top = jnp.max(scores, axis=-1, keepdims=True)
    weights = jnp.exp(scores - top)
    total = jnp.sum(weights, axis=-1, keepdims=True)
    mixed = jnp.einsum(
        "hqk,khd->qhd",
        (weights / total).astype(jnp.bfloat16),
        value_rows,
        preferred_element_type=jnp.float32,
    )
    return (mixed.astype(jnp.bfloat16), (top + jnp.log(total))[:, :, 0])


def attend_back(items):
    query_rows, keys, value_rows, doc_starts, log_totals, grad_mixed = items
    scores = masked_scores(query_rows, keys, doc_starts)
    probs = jnp.exp(scores - log_totals[:, :, None])
    grad_probs = jnp.einsum(
        "qhd,khd->hqk", grad_mixed, value_rows, preferred_element_type=jnp.float32
    )
    inner = jnp.sum(probs * grad_probs, axis=-1, keepdims=True)
    grad_scores = (probs * (grad_probs - inner)).astype(jnp.bfloat16)
    query_gradient = jnp.einsum(
        "hqk,khd->qhd", grad_scores, keys, preferred_element_type=jnp.float32
    ) * HEAD ** (-0.5)
    grad_k = jnp.einsum(
        "hqk,qhd->khd", grad_scores, query_rows, preferred_element_type=jnp.float32
    ) * HEAD ** (-0.5)
    value_gradient = jnp.einsum(
        "hqk,qhd->khd", probs.astype(jnp.bfloat16), grad_mixed, preferred_element_type=jnp.float32
    )
    return (
        query_gradient.astype(jnp.bfloat16),
        grad_k.astype(jnp.bfloat16),
        value_gradient.astype(jnp.bfloat16),
    )


def reduce_adapters(part_a, second_portion):
    return (lax.psum(part_a, ("dp", "tensor")), lax.psum(second_portion, "dp"))


def plain_body(
    activations,
    starts,
    attention_weights,
    projection_weight,
    feedforward_weight,
    output_weight,
    norm_gains,
    norm_biases,
    output_biases,
    query_value_bias,
    feedforward_bias,
    adapter_down_weight,
    adapter_up_weight,
):
    section = lax.axis_index("section")
    first = section == 0
    batches = activations.shape[1]
    own_rows = activations.shape[2]
    width = activations.shape[3]
    head_cols = projection_weight.shape[1]
    local_heads = head_cols // HEAD
    shaped = (-1, SEQ_LEN, local_heads, HEAD)
    w_cat = jnp.concatenate(
        [attention_weights[0, 0], attention_weights[0, 1], attention_weights[0, 2]], axis=1
    )
    stacked_down_maps = jnp.concatenate(
        [adapter_down_weight[0, 0], adapter_down_weight[0, 1]], axis=1
    )

    def forward_relay(rows, group_starts):
        normalized_rows = layer_norm(rows, norm_gains[0, 0], norm_biases[0, 0]).astype(jnp.bfloat16)
        gathered = lax.all_gather(normalized_rows, "tensor", axis=0, tiled=True)
        joined = jnp.dot(gathered, w_cat, preferred_element_type=jnp.float32)
        apply_adapter = jnp.dot(
            gathered, stacked_down_maps, preferred_element_type=jnp.float32
        ).astype(jnp.bfloat16)
        query_rows = (
            joined[:, :head_cols]
            + query_value_bias[0, 0]
            + adapter_scale
            * jnp.dot(
                apply_adapter[:, :ADAPTER_RANK],
                adapter_up_weight[0, 0],
                preferred_element_type=jnp.float32,
            )
        ).astype(jnp.bfloat16)
        keys = joined[:, head_cols : 2 * head_cols].astype(jnp.bfloat16)
        value_rows = (
            joined[:, 2 * head_cols :]
            + query_value_bias[0, 1]
            + adapter_scale
            * jnp.dot(
                apply_adapter[:, ADAPTER_RANK:],
                adapter_up_weight[0, 1],
                preferred_element_type=jnp.float32,
            )
        ).astype(jnp.bfloat16)
        mixed, log_totals = lax.map(
            attend,
            (
                query_rows.reshape(shaped),
                keys.reshape(shaped),
                value_rows.reshape(shaped),
                group_starts,
            ),
        )
        mixed = mixed.reshape(-1, head_cols)
        middle = (
            rows
            + lax.psum_scatter(
                jnp.dot(mixed, projection_weight[0], preferred_element_type=jnp.float32),
                "tensor",
                scatter_dimension=0,
                tiled=True,
            )
            + output_biases[0, 0]
        )
        normed_two = layer_norm(middle, norm_gains[0, 1], norm_biases[0, 1]).astype(jnp.bfloat16)
        hidden = (
            jnp.dot(
                lax.all_gather(normed_two, "tensor", axis=0, tiled=True),
                feedforward_weight[0],
                preferred_element_type=jnp.float32,
            )
            + feedforward_bias[0]
        )
        active = gelu_tanh(hidden).astype(jnp.bfloat16)
        output = (
            middle
            + lax.psum_scatter(
                jnp.dot(active, output_weight[0], preferred_element_type=jnp.float32).astype(
                    jnp.bfloat16
                ),
                "tensor",
                scatter_dimension=0,
                tiled=True,
            ).astype(jnp.float32)
            + output_biases[0, 1]
        )
        return (
            output,
            (
                rows,
                middle,
                gathered,
                apply_adapter,
                query_rows,
                keys,
                value_rows,
                log_totals,
                hidden,
            ),
        )

    def backward_relay(grad_rows, cache, group_starts):
        rows, middle, gathered, apply_adapter, query_rows, keys, value_rows, log_totals, hidden = (
            cache
        )
        grad_active = contract_axes(
            lax.all_gather(grad_rows.astype(jnp.bfloat16), "tensor", axis=0, tiled=True),
            output_weight[0],
            1,
            1,
        )
        _, gelu_back = jax.vjp(gelu_tanh, hidden)
        grad_hidden = gelu_back(grad_active)[0].astype(jnp.bfloat16)
        grad_normed_two = lax.psum_scatter(
            contract_axes(grad_hidden, feedforward_weight[0], 1, 1).astype(jnp.bfloat16),
            "tensor",
            scatter_dimension=0,
            tiled=True,
        ).astype(jnp.float32)
        _, norm_two_back = jax.vjp(
            lambda inner_rows: layer_norm(inner_rows, norm_gains[0, 1], norm_biases[0, 1]), middle
        )
        grad_middle = grad_rows + norm_two_back(grad_normed_two)[0]
        grad_mixed = contract_axes(
            lax.all_gather(grad_middle.astype(jnp.bfloat16), "tensor", axis=0, tiled=True),
            projection_weight[0],
            1,
            1,
        ).astype(jnp.bfloat16)
        query_gradient, grad_k, value_gradient = lax.map(
            attend_back,
            (
                query_rows.reshape(shaped),
                keys.reshape(shaped),
                value_rows.reshape(shaped),
                group_starts,
                log_totals,
                grad_mixed.reshape(shaped),
            ),
        )
        query_gradient = query_gradient.reshape(-1, head_cols)
        grad_k = grad_k.reshape(-1, head_cols)
        value_gradient = value_gradient.reshape(-1, head_cols)
        grad_low = jnp.concatenate(
            [
                adapter_scale * contract_axes(query_gradient, adapter_up_weight[0, 0], 1, 1),
                adapter_scale * contract_axes(value_gradient, adapter_up_weight[0, 1], 1, 1),
            ],
            axis=1,
        ).astype(jnp.bfloat16)
        grad_joined = jnp.concatenate([query_gradient, grad_k, value_gradient], axis=1)
        grad_normed = lax.psum_scatter(
            (
                contract_axes(grad_joined, w_cat, 1, 1)
                + contract_axes(grad_low, stacked_down_maps, 1, 1)
            ).astype(jnp.bfloat16),
            "tensor",
            scatter_dimension=0,
            tiled=True,
        ).astype(jnp.float32)
        _, norm_back = jax.vjp(
            lambda inner_rows: layer_norm(inner_rows, norm_gains[0, 0], norm_biases[0, 0]), rows
        )
        grad_in = grad_middle + norm_back(grad_normed)[0]
        grad_down = contract_axes(gathered, grad_low, 0, 0)
        part_a = jnp.stack([grad_down[:, :ADAPTER_RANK], grad_down[:, ADAPTER_RANK:]])
        second_portion = adapter_scale * jnp.stack(
            [
                contract_axes(apply_adapter[:, :ADAPTER_RANK], query_gradient, 0, 0),
                contract_axes(apply_adapter[:, ADAPTER_RANK:], value_gradient, 0, 0),
            ]
        )
        return (grad_in, part_a, second_portion)

    received = jnp.zeros((own_rows, width), jnp.bfloat16)
    finals = []
    stored = []
    for tick in range(batches + 1):
        batch_index = jnp.clip(tick - section, 0, batches - 1)
        own = lax.dynamic_index_in_dim(activations[0], batch_index, 0, keepdims=False)
        rows = jnp.where(first, own, received).astype(jnp.float32)
        group_starts = lax.dynamic_index_in_dim(starts, batch_index, 0, keepdims=False)
        output, cache = forward_relay(rows, group_starts)
        finals.append(output)
        stored.append(rows)
        if tick < batches:
            received = from_behind(output.astype(jnp.bfloat16), "section", 1)
    stacked = jax.tree.map(lambda *items: jnp.stack(items), *stored)
    returned = jnp.zeros((own_rows, width), jnp.bfloat16)
    totals_a = jnp.zeros((2, width, ADAPTER_RANK), jnp.float32)
    totals_b = jnp.zeros((2, ADAPTER_RANK, head_cols), jnp.float32)
    grads_in = []
    for tick in range(batches + 1):
        position = tick - 1 + section
        batch_index = jnp.clip(position, 0, batches - 1)
        valid = ((position >= 0) & (position < batches)).astype(jnp.float32)
        own = lax.dynamic_index_in_dim(activations[0], batch_index, 0, keepdims=False)
        grad_rows = jnp.where(first, returned, own).astype(jnp.float32) * valid
        group_starts = lax.dynamic_index_in_dim(starts, batch_index, 0, keepdims=False)
        slot_index = jnp.clip(tick - 1 + 2 * section, 0, batches)
        picked = lax.dynamic_index_in_dim(stacked, slot_index, 0, keepdims=False)
        _, cache = forward_relay(picked, group_starts)
        grad_in, part_a, second_portion = backward_relay(grad_rows, cache, group_starts)
        grads_in.append(grad_in)
        if tick < batches:
            returned = from_behind(grad_in.astype(jnp.bfloat16), "section", -1)
        part_a, second_portion = reduce_adapters(part_a, second_portion)
        totals_a = totals_a + part_a
        totals_b = totals_b + second_portion
    combined = jnp.stack(
        [jnp.where(first, grads_in[index + 1], finals[index + 1]) for index in range(batches)]
    )
    return (combined[None], totals_a[None], totals_b[None])


LOW = 2 * ADAPTER_RANK
VMEM_SPACE = pl.BlockSpec(memory_space=pltpu.VMEM)
SMEM_SPACE = pl.BlockSpec(memory_space=pltpu.SMEM)
HBM_SPACE = pl.BlockSpec(memory_space=pl.ANY)
BLOCK = 256


def send(block, route):
    pairs = []
    for s in range(2):
        for t in range(4):
            to = route(s, t)
            if to is not None:
                pairs.append((s * 4 + t, to[0] * 4 + to[1]))
    return lax.ppermute(block, ("section", "tensor"), pairs)


def other_core(block):
    return send(block, lambda s, t: (1 - s, t))


def x_swap(block):
    return send(block, lambda s, t: (s, t ^ 1))


def y_swap(block):
    return send(block, lambda s, t: (s, t ^ 2))


def deal(source, same_chip, cross_chip):
    return (
        send(same_chip, lambda s, t: (t >> 1, t) if s == source else None),
        send(cross_chip, lambda s, t: (t >> 1, t ^ 2) if s == source else None),
    )


def collect(target, same_chip, cross_chip):
    return (
        send(same_chip, lambda s, t: (target, t) if s == t >> 1 else None),
        send(cross_chip, lambda s, t: (target, t ^ 2) if s != t >> 1 else None),
    )


def mm(left, right):
    return jnp.dot(left, right, preferred_element_type=jnp.float32)


def mm_nt(left, right):
    return contract_axes(left, right, 1, 1)


def norm_back(rows, gain, grad):
    mean = jnp.mean(rows, axis=-1, keepdims=True)
    centered = rows - mean
    scale = lax.rsqrt(jnp.mean(centered * centered, axis=-1, keepdims=True) + 1e-05)
    unit = centered * scale
    scaled = grad * gain
    return scale * (
        scaled
        - jnp.mean(scaled, axis=-1, keepdims=True)
        - unit * jnp.mean(scaled * unit, axis=-1, keepdims=True)
    )


def gelu_both(value):
    square = value * value
    bent = jnp.tanh(0.7978845608028654 * value * (1.0 + 0.044715 * square))
    half = 0.5 * (1.0 + bent)
    slope = half + 0.5 * value * (1.0 - bent * bent) * (
        0.7978845608028654 * (1.0 + 3.0 * 0.044715 * square)
    )
    return value * half, slope


def cost(flops, read):
    return pl.CostEstimate(flops=int(flops), bytes_accessed=int(read), transcendentals=0)


def kernel_params(mib):
    return pltpu.CompilerParams(vmem_limit_bytes=mib * 1024 * 1024)


def position_mask(meta, query_block, key_block):
    shape = (BLOCK, BLOCK)
    key_pos = key_block * BLOCK + lax.broadcasted_iota(jnp.int32, shape, 0)
    query_pos = query_block * BLOCK + lax.broadcasted_iota(jnp.int32, (1, BLOCK), 1)
    low = jnp.zeros((1, BLOCK), jnp.int32)
    for c in range(4):
        first = meta[4 + c]
        low = jnp.where(first <= query_pos, jnp.maximum(low, first), low)
    valid = key_pos >= low
    if query_block == key_block:
        valid = valid & (key_pos <= query_pos)
    return valid


def head_lanes(half):
    return (lax.broadcasted_iota(jnp.int32, (1, 2 * HEAD), 1) // HEAD) == half


def load_qkv_weight(meta, w_same, w_cross, w_buf, sem):
    home = meta[0] == meta[2]

    @pl.when(home)
    def _():
        pltpu.make_async_copy(w_same, w_buf, sem).start()

    @pl.when(jnp.logical_not(home))
    def _():
        pltpu.make_async_copy(w_cross, w_buf, sem).start()


def block_places(meta):
    s, x = meta[0], meta[1]
    return (x + 2 * s, x + 2 * (1 - s), (1 - x) + 2 * s, (1 - x) + 2 * (1 - s))


def attend_kernel(
    layer, meta, n0, n1, n2, n3, shared, varied, w_same, w_cross,
    q_ref, k_ref, v_ref, lse_ref, mixed_ref, o0, o1, o2, o3,
    w_buf, score_buf, vt_buf, sem,
):
    load_qkv_weight(meta, w_same, w_cross, w_buf, sem)
    s, x = meta[0], meta[1]
    quarter = x + 2 * s
    down = shared[layer, 8:16, :].astype(jnp.bfloat16)
    bias = varied[quarter, layer, 1:2, :]
    up = varied[quarter, layer, 8:16, 0:512].astype(jnp.bfloat16)
    places = block_places(meta)
    pltpu.make_async_copy(w_same, w_buf, sem).wait()
    for place, block in zip(places, (n0, n1, n2, n3)):
        rows = pl.ds(pl.multiple_of(place * BLOCK, BLOCK), BLOCK)
        normed = block[...]
        low = mm_nt(normed, down).astype(jnp.bfloat16)
        lifted = adapter_scale * mm(low, up)
        q_ref[rows, :] = (mm(normed, w_buf[0]) + bias[:, 0:256] + lifted[:, 0:256]).astype(
            jnp.bfloat16
        )
        k_ref[rows, :] = mm(normed, w_buf[1]).astype(jnp.bfloat16)
        v_ref[rows, :] = (mm(normed, w_buf[2]) + bias[:, 256:512] + lifted[:, 256:512]).astype(
            jnp.bfloat16
        )
    for b in range(4):
        vt_buf[:, b * BLOCK : (b + 1) * BLOCK] = v_ref[b * BLOCK : (b + 1) * BLOCK, :].T

    def one_head(head, carry):
        lanes = pl.ds(pl.multiple_of((head // 2) * 128, 128), 128)
        chosen = head_lanes(head % 2)
        deep = pl.ds(pl.multiple_of(head * HEAD, HEAD), HEAD)
        for i in range(4):
            part = q_ref[i * BLOCK : (i + 1) * BLOCK, lanes]
            query = jnp.where(chosen, part * HEAD ** (-0.5), 0.0).astype(jnp.bfloat16)
            top = jnp.full((1, BLOCK), -1e30, jnp.float32)
            for j in range(i + 1):
                scores = mm_nt(k_ref[j * BLOCK : (j + 1) * BLOCK, lanes], query)
                scores = jnp.where(position_mask(meta, i, j), scores, -1e30)
                score_buf[j] = scores
                top = jnp.maximum(top, jnp.max(scores, axis=0, keepdims=True))
            total = jnp.zeros((1, BLOCK), jnp.float32)
            mixed = jnp.zeros((HEAD, BLOCK), jnp.float32)
            for j in range(i + 1):
                weights = jnp.exp(score_buf[j] - top)
                total = total + jnp.sum(weights, axis=0, keepdims=True)
                mixed = mixed + mm(
                    vt_buf[deep, j * BLOCK : (j + 1) * BLOCK], weights.astype(jnp.bfloat16)
                )
            mixed_ref[deep, i * BLOCK : (i + 1) * BLOCK] = mixed / total
            lse_ref[pl.ds(head, 1), i * BLOCK : (i + 1) * BLOCK] = top + jnp.log(total)
        return carry

    lax.fori_loop(0, 4, one_head, 0)
    for place, out in zip(places, (o0, o1, o2, o3)):
        columns = pl.ds(pl.multiple_of(place * BLOCK, BLOCK), BLOCK)
        out[...] = mixed_ref[:, columns].T.astype(jnp.bfloat16)


def attend_call(layer, meta, blocks, shared, varied, w_same, w_cross):
    bf, f32 = jnp.bfloat16, jnp.float32
    wide = jax.ShapeDtypeStruct((SEQ_LEN, 256), bf)
    piece = jax.ShapeDtypeStruct((BLOCK, 256), bf)
    return pl.pallas_call(
        functools.partial(attend_kernel, layer),
        in_specs=[SMEM_SPACE] + [VMEM_SPACE] * 6 + [HBM_SPACE] * 2,
        out_specs=[VMEM_SPACE] * 9,
        out_shape=[wide, wide, wide, jax.ShapeDtypeStruct((8, SEQ_LEN), f32),
                   jax.ShapeDtypeStruct((256, SEQ_LEN), f32)] + [piece] * 4,
        scratch_shapes=[
            pltpu.VMEM((3, 1024, 256), bf),
            pltpu.VMEM((4, BLOCK, BLOCK), f32),
            pltpu.VMEM((256, SEQ_LEN), bf),
            pltpu.SemaphoreType.DMA,
        ],
        compiler_params=kernel_params(40),
        cost_estimate=cost(3.5e9, 8e6),
        name="attention_forward",
    )(meta, *blocks, shared, varied, w_same, w_cross)


def attend_back_kernel(
    layer, meta, n0, n1, n2, n3, g0, g1, g2, g3, q_ref, k_ref, v_ref, lse_ref, mixed_ref,
    shared, varied, w_same, w_cross,
    keep_ref, give_ref, down_ref, up_ref,
    w_buf, kt_buf, do_buf, delta_buf, dqt_buf, dk_buf, dv_buf, dq_buf, sem,
):
    load_qkv_weight(meta, w_same, w_cross, w_buf, sem)
    s, x = meta[0], meta[1]
    quarter = x + 2 * s
    places = block_places(meta)
    for place, block in zip(places, (g0, g1, g2, g3)):
        do_buf[pl.ds(pl.multiple_of(place * BLOCK, BLOCK), BLOCK), :] = block[...]
    for b in range(4):
        span = slice(b * BLOCK, (b + 1) * BLOCK)
        kt_buf[:, span] = k_ref[span, :].T
        product = do_buf[span, :].astype(jnp.float32).T * mixed_ref[:, span]
        for head in range(4):
            delta_buf[head : head + 1, span] = jnp.sum(
                product[head * HEAD : (head + 1) * HEAD], axis=0, keepdims=True
            )
    dk_buf[...] = jnp.zeros_like(dk_buf)
    dv_buf[...] = jnp.zeros_like(dv_buf)

    def one_head(head, carry):
        lanes = pl.ds(pl.multiple_of((head // 2) * 128, 128), 128)
        chosen = head_lanes(head % 2)
        deep = pl.ds(pl.multiple_of(head * HEAD, HEAD), HEAD)
        for i in range(4):
            span = slice(i * BLOCK, (i + 1) * BLOCK)
            query = jnp.where(chosen, q_ref[span, lanes] * HEAD ** (-0.5), 0.0).astype(jnp.bfloat16)
            grad_mixed = jnp.where(chosen, do_buf[span, lanes], 0.0).astype(jnp.bfloat16)
            lse = lse_ref[pl.ds(head, 1), span]
            delta = delta_buf[pl.ds(head, 1), span]
            grad_query = jnp.zeros((HEAD, BLOCK), jnp.float32)
            for j in range(i + 1):
                keys = slice(j * BLOCK, (j + 1) * BLOCK)
                scores = mm_nt(k_ref[keys, lanes], query)
                probs = jnp.where(position_mask(meta, i, j), jnp.exp(scores - lse), 0.0)
                grad_probs = mm_nt(v_ref[keys, lanes], grad_mixed)
                grad_scores = (probs * (grad_probs - delta)).astype(jnp.bfloat16)
                dv_buf[keys, lanes] += mm(probs.astype(jnp.bfloat16), grad_mixed)
                dk_buf[keys, lanes] += mm(grad_scores, query)
                grad_query = grad_query + mm(kt_buf[deep, keys], grad_scores)
            dqt_buf[deep, span] = grad_query * HEAD ** (-0.5)
        return carry

    lax.fori_loop(0, 4, one_head, 0)
    down = shared[layer, 8:16, :].astype(jnp.bfloat16)
    up = varied[quarter, layer, 8:16, 0:512].astype(jnp.bfloat16)
    for b in range(4):
        span = slice(b * BLOCK, (b + 1) * BLOCK)
        dq_buf[span, :] = dqt_buf[:, span].T.astype(jnp.bfloat16)
    pltpu.make_async_copy(w_same, w_buf, sem).wait()
    total_down = jnp.zeros((LOW, 1024), jnp.float32)
    total_up = jnp.zeros((LOW, 512), jnp.float32)
    targets = ((keep_ref, 0), (give_ref, 0), (keep_ref, 1), (give_ref, 1))
    for place, block, (target, slot) in zip(places, (n0, n1, n2, n3), targets):
        rows = pl.ds(pl.multiple_of(place * BLOCK, BLOCK), BLOCK)
        normed = block[...]
        grad_q = dq_buf[rows, :]
        grad_k = dk_buf[rows, :].astype(jnp.bfloat16)
        grad_v = dv_buf[rows, :].astype(jnp.bfloat16)
        both = jnp.concatenate([grad_q, grad_v], axis=1)
        low_grad = (adapter_scale * mm_nt(both, up)).astype(jnp.bfloat16)
        low_grad_t = (adapter_scale * mm_nt(up, both)).astype(jnp.bfloat16)
        low_t = mm_nt(down, normed).astype(jnp.bfloat16)
        grad_normed = (
            mm_nt(grad_q, w_buf[0]) + mm_nt(grad_k, w_buf[1]) + mm_nt(grad_v, w_buf[2])
            + mm(low_grad, down)
        )
        target[slot] = grad_normed.astype(jnp.bfloat16)
        total_down = total_down + mm(low_grad_t, normed)
        total_up = total_up + adapter_scale * mm(low_t, both)
    down_ref[...] = total_down
    up_ref[...] = total_up


def attend_back_call(layer, meta, blocks, grads, saved, shared, varied, w_same, w_cross):
    bf, f32 = jnp.bfloat16, jnp.float32
    pair = jax.ShapeDtypeStruct((2, BLOCK, 1024), bf)
    return pl.pallas_call(
        functools.partial(attend_back_kernel, layer),
        in_specs=[SMEM_SPACE] + [VMEM_SPACE] * 15 + [HBM_SPACE] * 2,
        out_specs=[VMEM_SPACE] * 4,
        out_shape=[pair, pair, jax.ShapeDtypeStruct((LOW, 1024), f32),
                   jax.ShapeDtypeStruct((LOW, 512), f32)],
        scratch_shapes=[
            pltpu.VMEM((3, 1024, 256), bf),
            pltpu.VMEM((256, SEQ_LEN), bf),
            pltpu.VMEM((SEQ_LEN, 256), bf),
            pltpu.VMEM((8, SEQ_LEN), f32),
            pltpu.VMEM((256, SEQ_LEN), f32),
            pltpu.VMEM((SEQ_LEN, 256), f32),
            pltpu.VMEM((SEQ_LEN, 256), f32),
            pltpu.VMEM((SEQ_LEN, 256), bf),
            pltpu.SemaphoreType.DMA,
        ],
        compiler_params=kernel_params(48),
        cost_estimate=cost(6e9, 12e6),
        name="attention_backward",
    )(meta, *blocks, *grads, *saved, shared, varied, w_same, w_cross)


N_WEIGHTS = 18


def weight_plan(layer, meta, refs, wp, w1, w2, sems):
    s = meta[0]
    own, dup, parts = refs[0:3], refs[3:6], refs[6:18]
    plan = {"p": [[] for _ in range(4)], "a": [[] for _ in range(4)], "b": [[] for _ in range(4)]}
    count = 0

    def add(kind, slot, source, target, alternative=None):
        nonlocal count
        plan[kind][slot].append((source, target, sems.at[count], alternative))
        count += 1

    half_p = [pl.ds(pl.multiple_of(h * 128, 128), 128) for h in (s, 1 - s)]
    half_w = [pl.ds(pl.multiple_of(h * 512, 512), 512) for h in (s, 1 - s)]
    add("p", 0, own[0], wp.at[0], dup[0])
    add("a", 0, own[1], w1.at[0], dup[1])
    add("b", 0, own[2], w2.at[0], dup[2])
    for slot in (1, 2, 3):
        for h in range(2):
            first, second = parts[(slot - 1) * 4 + 2 * h : (slot - 1) * 4 + 2 * h + 2]
            add("p", slot, first.at[0:128], wp.at[slot, half_p[h]])
            add("a", slot, first.at[128:640], w1.at[slot, half_w[h]])
            add("b", slot, second, w2.at[slot, half_w[h]])
    return plan


def start_copies(layer, meta, copies):
    for source, target, sem, alternative in copies:
        if alternative is None:
            pltpu.make_async_copy(source, target, sem).start()
        else:
            mine = meta[0] == layer

            @pl.when(mine)
            def _():
                pltpu.make_async_copy(source, target, sem).start()

            @pl.when(jnp.logical_not(mine))
            def _():
                pltpu.make_async_copy(alternative, target, sem).start()


def wait_copies(copies):
    for source, target, sem, _ in copies:
        pltpu.make_async_copy(source, target, sem).wait()


def project(meta, pieces, wp):
    apart = jnp.where(meta[0] == meta[2], 0, 1)
    slots = (2 * apart, 2 * (1 - apart), 2 * apart + 1, 2 * (1 - apart) + 1)
    total = mm(pieces[0][...], wp[slots[0]])
    for piece, slot in zip(pieces[1:], slots[1:]):
        total = total + mm(piece[...], wp[slot])
    return total


def back_to_heads(meta, grad, wp, outs):
    apart = jnp.where(meta[0] == meta[2], 0, 1)
    slots = (2 * apart, 2 * (1 - apart), 2 * apart + 1, 2 * (1 - apart) + 1)
    for out, slot in zip(outs, slots):
        out[...] = mm_nt(grad, wp[slot]).astype(jnp.bfloat16)


def unit_bias(meta, varied, layer, slot):
    return varied[jnp.bitwise_xor(meta[3], slot), layer, 0:1, :]


def rows_forward_kernel(meta, p0, p1, p2, p3, h_ref, shared, varied, *rest):
    refs = rest[:N_WEIGHTS]
    middle_ref, slope_ref, between_ref, normed_ref = rest[N_WEIGHTS : N_WEIGHTS + 4]
    wp, w1, w2, total, sems = rest[N_WEIGHTS + 4 :]
    plan = weight_plan(0, meta, refs, wp, w1, w2, sems)
    for kind in "pab":
        for slot in range(4):
            start_copies(0, meta, plan[kind][slot])
    for slot in range(4):
        wait_copies(plan["p"][slot])
    middle = h_ref[...].astype(jnp.float32) + project(meta, (p0, p1, p2, p3), wp) + shared[0, 4:5, :]
    middle_ref[...] = middle
    normed = layer_norm(middle, shared[0, 1:2, :], shared[0, 3:4, :]).astype(jnp.bfloat16)
    total[...] = middle + shared[0, 5:6, :]
    for slot in range(4):
        wait_copies(plan["a"][slot])
        active, slope = gelu_both(mm(normed, w1[slot]) + unit_bias(meta, varied, 0, slot))
        slope_ref[slot] = slope.astype(jnp.bfloat16)
        wait_copies(plan["b"][slot])
        total[...] += mm(active.astype(jnp.bfloat16), w2[slot])
    between = total[...].astype(jnp.bfloat16)
    between_ref[...] = between
    normed_ref[...] = layer_norm(
        between.astype(jnp.float32), shared[1, 0:1, :], shared[1, 2:3, :]
    ).astype(jnp.bfloat16)


def rows_turn_kernel(meta, p0, p1, p2, p3, h_ref, g_ref, shared, varied, *rest):
    refs = rest[:N_WEIGHTS]
    middle_ref, active_ref, grad_ref, o0, o1, o2, o3 = rest[N_WEIGHTS : N_WEIGHTS + 7]
    wp, w1, w2, total, sems = rest[N_WEIGHTS + 7 :]
    plan = weight_plan(1, meta, refs, wp, w1, w2, sems)
    for kind in "pab":
        for slot in range(4):
            start_copies(1, meta, plan[kind][slot])
    for slot in range(4):
        wait_copies(plan["p"][slot])
    middle = h_ref[...].astype(jnp.float32) + project(meta, (p0, p1, p2, p3), wp) + shared[1, 4:5, :]
    middle_ref[...] = middle
    normed = layer_norm(middle, shared[1, 1:2, :], shared[1, 3:4, :]).astype(jnp.bfloat16)
    grad = g_ref[...]
    for slot in range(4):
        wait_copies(plan["a"][slot])
        active, slope = gelu_both(mm(normed, w1[slot]) + unit_bias(meta, varied, 1, slot))
        active_ref[slot] = active.astype(jnp.bfloat16)
        wait_copies(plan["b"][slot])
        grad_hidden = (mm_nt(grad, w2[slot]) * slope).astype(jnp.bfloat16)
        part = mm_nt(grad_hidden, w1[slot])
        if slot == 0:
            total[...] = part
        else:
            total[...] += part
    grad_middle = grad.astype(jnp.float32) + norm_back(middle, shared[1, 1:2, :], total[...])
    grad_ref[...] = grad_middle
    back_to_heads(meta, grad_middle.astype(jnp.bfloat16), wp, (o0, o1, o2, o3))


def rows_backward_kernel(meta, gm_ref, keep, take, far, between_ref, middle_ref, slope_ref, shared, *rest):
    refs = rest[:N_WEIGHTS]
    grad_ref, o0, o1, o2, o3 = rest[N_WEIGHTS : N_WEIGHTS + 5]
    wp, w1, w2, total, sems = rest[N_WEIGHTS + 5 :]
    plan = weight_plan(0, meta, refs, wp, w1, w2, sems)
    for kind in "bap":
        for slot in range(4):
            start_copies(0, meta, plan[kind][slot])
    grad_normed = (
        keep[0].astype(jnp.float32) + take[0].astype(jnp.float32) + far[...].astype(jnp.float32)
    )
    grad_rows = gm_ref[...] + norm_back(
        between_ref[...].astype(jnp.float32), shared[1, 0:1, :], grad_normed
    )
    grad = grad_rows.astype(jnp.bfloat16)
    for slot in range(4):
        wait_copies(plan["b"][slot])
        grad_active = mm_nt(grad, w2[slot])
        grad_hidden = (grad_active * slope_ref[slot].astype(jnp.float32)).astype(jnp.bfloat16)
        wait_copies(plan["a"][slot])
        part = mm_nt(grad_hidden, w1[slot])
        if slot == 0:
            total[...] = part
        else:
            total[...] += part
    grad_middle = grad.astype(jnp.float32) + norm_back(middle_ref[...], shared[0, 1:2, :], total[...])
    grad_ref[...] = grad_middle
    for slot in range(4):
        wait_copies(plan["p"][slot])
    back_to_heads(meta, grad_middle.astype(jnp.bfloat16), wp, (o0, o1, o2, o3))


def rows_output_kernel(meta, active_ref, middle_ref, shared, *rest):
    refs = rest[:N_WEIGHTS]
    wide_ref, narrow_ref = rest[N_WEIGHTS : N_WEIGHTS + 2]
    wp, w1, w2, sems = rest[N_WEIGHTS + 2 :]
    plan = weight_plan(1, meta, refs, wp, w1, w2, sems)
    for slot in range(4):
        start_copies(1, meta, plan["b"][slot])
    total = middle_ref[...] + shared[1, 5:6, :]
    for slot in range(4):
        wait_copies(plan["b"][slot])
        total = total + mm(active_ref[slot], w2[slot])
    wide_ref[...] = total
    narrow_ref[...] = total.astype(jnp.bfloat16)


def rows_final_kernel(gm_ref, keep, take, far, h_ref, shared, wide_ref, narrow_ref):
    grad_normed = (
        keep[0].astype(jnp.float32) + take[0].astype(jnp.float32) + far[...].astype(jnp.float32)
    )
    grad_in = gm_ref[...] + norm_back(
        h_ref[...].astype(jnp.float32), shared[0, 0:1, :], grad_normed
    )
    wide_ref[...] = grad_in
    narrow_ref[...] = grad_in.astype(jnp.bfloat16)


def rows_call(kernel, small, weights, outs, scratch, flops, name):
    return pl.pallas_call(
        kernel,
        in_specs=[SMEM_SPACE] + [VMEM_SPACE] * (len(small) - 1) + [HBM_SPACE] * len(weights),
        out_specs=[VMEM_SPACE] * len(outs),
        out_shape=outs,
        scratch_shapes=scratch,
        compiler_params=kernel_params(52),
        cost_estimate=cost(flops, 2e7),
        name=name,
    )(*small, *weights)


def weight_scratch(total):
    bf = jnp.bfloat16
    found = [
        pltpu.VMEM((4, 256, 1024), bf),
        pltpu.VMEM((4, 1024, 1024), bf),
        pltpu.VMEM((4, 1024, 1024), bf),
    ]
    if total:
        found.append(pltpu.VMEM((BLOCK, 1024), jnp.float32))
    found.append(pltpu.SemaphoreType.DMA((21,)))
    return found


def spread_weights(layer, section, wp, w1, w2):
    own = (wp, w1, w2)
    dup = tuple(
        send(w, lambda s, t: (1 - layer, t) if s == layer else None) for w in own
    )

    def halves(group, half):
        return (
            jnp.concatenate(
                [group[0][half * 128 : half * 128 + 128], group[1][half * 512 : half * 512 + 512]]
            ),
            group[2][half * 512 : half * 512 + 512],
        )

    mine = section == layer
    first, second = jax.tree.map(
        lambda a, b: jnp.where(mine, a, b), halves(own, layer), halves(dup, 1 - layer)
    )
    x1, x2 = x_swap(first), x_swap(second)
    y1, y2 = y_swap(first), y_swap(second)
    d1, d2 = y_swap(x1), x_swap(y2)
    parts = (
        x1, x2, other_core(x1), other_core(x2),
        y1, y2, other_core(y1), other_core(y2),
        d1, d2, other_core(d1), other_core(d2),
    )
    return own + dup + parts


def gather_rows(own):
    near = other_core(own)
    far = x_swap(own)
    return (own, near, far, other_core(far))


def exchange_heads(o0, o1, o2, o3):
    return (
        o0,
        other_core(o1),
        x_swap(o2),
        send(o3, lambda s, t: (1 - s, t ^ 1)),
    )


def reduce_rows(keep, give):
    take = other_core(give)
    far = x_swap((keep[1].astype(jnp.float32) + take[1].astype(jnp.float32)).astype(jnp.bfloat16))
    return keep, take, far


def total_adapters(layer, part_down, part_up):
    part_down = part_down + other_core(part_down)
    part_down = part_down + x_swap(part_down)
    both = jnp.concatenate([part_down, part_up], axis=1)
    both = both + y_swap(both)
    size = lax.axis_size("dp")
    step = 1
    while step < size:
        both = both + lax.ppermute(both, "dp", [(i, i ^ step) for i in range(size)])
        step *= 2
    up = send(both[:, 1024:], lambda s, t: (layer, t) if s == t >> 1 else None)
    return both[:, :1024], up


def relay_body(
    activations, starts, attention_weights, projection_weight, feedforward_weight, output_weight,
    norm_gains, norm_biases, output_biases, query_value_bias, feedforward_bias,
    adapter_down_weight, adapter_up_weight,
):
    bf, f32 = jnp.bfloat16, jnp.float32
    section = lax.axis_index("section")
    place = lax.axis_index("tensor")
    y, x = place // 2, place % 2
    first = section == 0
    home = section == y

    meta = jnp.concatenate(
        [
            jnp.stack([section, x, y, place]).astype(jnp.int32),
            lax.dynamic_index_in_dim(starts, y, 0, keepdims=False).reshape(4),
        ]
    )
    slots = activations[0]
    same = lax.dynamic_index_in_dim(slots, y, 0, keepdims=False)
    cross = lax.dynamic_index_in_dim(slots, 1 - y, 0, keepdims=False)
    rows = jnp.where(home, *deal(0, same, cross))

    down_rows = adapter_down_weight[0].astype(f32).transpose(0, 2, 1).reshape(LOW, 1024)
    up0 = adapter_up_weight[0, 0].astype(f32)
    up1 = adapter_up_weight[0, 1].astype(f32)
    zero = jnp.zeros((ADAPTER_RANK, 256), f32)
    packed = jnp.concatenate(
        [
            norm_gains[0], norm_biases[0], output_biases[0], jnp.zeros((2, 1024), f32), down_rows,
            feedforward_bias,
            jnp.pad(query_value_bias[0].reshape(1, 512), ((0, 0), (0, 512))),
            jnp.zeros((6, 1024), f32),
            jnp.concatenate([up0, zero, jnp.zeros((ADAPTER_RANK, 512), f32)], axis=1),
            jnp.concatenate([zero, up1, jnp.zeros((ADAPTER_RANK, 512), f32)], axis=1),
        ]
    )
    partner = other_core(packed)
    both = jnp.where(first, jnp.stack([packed, partner]), jnp.stack([partner, packed]))
    shared = both[:, :16]
    varied = lax.all_gather(both[:, 16:], "tensor", axis=0)

    qkv = [deal(layer, attention_weights[0], attention_weights[0]) for layer in range(2)]
    weights = [
        spread_weights(layer, section, projection_weight[0], feedforward_weight[0], output_weight[0])
        for layer in range(2)
    ]
    grad_out = jnp.where(home, *deal(1, same, cross))

    sheet = jax.ShapeDtypeStruct((BLOCK, 1024), f32)
    thin = jax.ShapeDtypeStruct((BLOCK, 1024), bf)
    stack4 = jax.ShapeDtypeStruct((4, BLOCK, 1024), bf)
    piece = jax.ShapeDtypeStruct((BLOCK, 256), bf)

    normed = layer_norm(rows.astype(f32), shared[0, 0], shared[0, 2]).astype(bf)
    blocks0 = gather_rows(normed)
    *saved0, o0, o1, o2, o3 = attend_call(0, meta, blocks0, shared, varied, *qkv[0])
    heads = exchange_heads(o0, o1, o2, o3)
    middle0, slope0, between, normed = rows_call(
        rows_forward_kernel, (meta, *heads, rows, shared, varied), weights[0],
        [sheet, stack4, thin, thin], weight_scratch(True), 5e9, "rows_forward",
    )
    blocks1 = gather_rows(normed)
    *saved1, o0, o1, o2, o3 = attend_call(1, meta, blocks1, shared, varied, *qkv[1])
    heads = exchange_heads(o0, o1, o2, o3)
    middle1, active1, grad_middle1, o0, o1, o2, o3 = rows_call(
        rows_turn_kernel, (meta, *heads, between, grad_out, shared, varied), weights[1],
        [sheet, stack4, sheet, piece, piece, piece, piece], weight_scratch(True), 8e9, "rows_turn",
    )
    grads = exchange_heads(o0, o1, o2, o3)
    wide, narrow = rows_call(
        rows_output_kernel, (meta, active1, middle1, shared), weights[1],
        [sheet, thin], weight_scratch(False), 2.1e9, "rows_output",
    )
    out_same, out_cross = collect(1, wide, narrow)
    keep, give, down1, up1 = attend_back_call(
        1, meta, blocks1, grads, saved1, shared, varied, *qkv[1]
    )
    keep, take, far = reduce_rows(keep, give)
    grad_middle0, o0, o1, o2, o3 = rows_call(
        rows_backward_kernel,
        (meta, grad_middle1, keep, take, far, between, middle0, slope0, shared), weights[0],
        [sheet, piece, piece, piece, piece], weight_scratch(True), 5e9, "rows_backward",
    )
    total1 = total_adapters(1, down1, up1)
    grads = exchange_heads(o0, o1, o2, o3)
    keep, give, down0, up0 = attend_back_call(
        0, meta, blocks0, grads, saved0, shared, varied, *qkv[0]
    )
    keep, take, far = reduce_rows(keep, give)
    wide, narrow = pl.pallas_call(
        rows_final_kernel,
        in_specs=[VMEM_SPACE] * 6,
        out_specs=[VMEM_SPACE] * 2,
        out_shape=[sheet, thin],
        compiler_params=kernel_params(32),
        cost_estimate=cost(1e7, 6e6),
        name="rows_final",
    )(grad_middle0, keep, take, far, rows, shared)
    total0 = total_adapters(0, down0, up0)
    in_same, in_cross = collect(0, wide, narrow)
    same = jnp.where(first, in_same, out_same)
    cross = jnp.where(first, in_cross, out_cross).astype(f32)
    combined = jnp.where(y == 0, jnp.stack([same, cross]), jnp.stack([cross, same]))
    grad_down = jnp.where(first, total0[0], total1[0])
    grad_up = jnp.where(first, total0[1], total1[1])
    return (
        combined[None],
        grad_down.reshape(1, 2, ADAPTER_RANK, 1024).transpose(0, 1, 3, 2),
        jnp.stack([grad_up[:ADAPTER_RANK, :256], grad_up[ADAPTER_RANK:, 256:]])[None],
    )


def body(*arrays):
    dp = lax.axis_size("dp")
    known = (
        arrays[0].shape == (1, 2, BLOCK, 1024)
        and lax.axis_size("tensor") == 4
        and lax.axis_size("section") == 2
        and arrays[3].shape == (1, 256, 1024)
        and arrays[5].shape == (1, 1024, 1024)
        and dp & (dp - 1) == 0
    )
    return relay_body(*arrays) if known else plain_body(*arrays)


def solution(mesh):
    placed = (
        P("section", None, ("dp", "tensor"), None),
        P(None, "dp", None),
        P("section", None, None, "tensor"),
        P("section", "tensor", None),
        P("section", None, "tensor"),
        P("section", "tensor", None),
        P("section", None, None),
        P("section", None, None),
        P("section", None, None),
        P("section", None, "tensor"),
        P("section", "tensor"),
        P("section", None, None, None),
        P("section", None, None, "tensor"),
    )
    return jax.shard_map(
        body,
        mesh=mesh,
        in_specs=placed,
        out_specs=(
            P("section", None, ("dp", "tensor"), None),
            P("section", None, None, None),
            P("section", None, None, "tensor"),
        ),
        check_vma=False,
    )
```

```python
import functools

import jax
import jax.numpy as jnp
from jax import lax
from jax.experimental import pallas as pl
from jax.experimental.pallas import tpu as pltpu
from jax.sharding import PartitionSpec as P

HEAD = 64
ADAPTER_RANK = 4
SEQ_LEN = 1024


adapter_scale = 8.0


def from_behind(block, axis, distance):
    devices = range(lax.axis_size(axis))
    route = [(i - distance, i) for i in devices if i - distance in devices]
    return lax.ppermute(block, axis, route)


def contract_axes(left, right, left_dim, right_dim):
    return lax.dot_general(
        left, right, (((left_dim,), (right_dim,)), ((), ())), preferred_element_type=jnp.float32
    )


def layer_norm(rows, gain, shift):
    mean = jnp.mean(rows, axis=-1, keepdims=True)
    centered = rows - mean
    spread = jnp.mean(centered * centered, axis=-1, keepdims=True)
    return centered * lax.rsqrt(spread + 1e-05) * gain + shift


def gelu_tanh(value):
    return (
        0.5
        * value
        * (1.0 + jnp.tanh(0.7978845608028654 * (value + 0.044715 * value * value * value)))
    )


def doc_mask(doc_starts):
    positions = jnp.arange(SEQ_LEN, dtype=jnp.int32)
    labels = jnp.sum((doc_starts[None, :] <= positions[:, None]).astype(jnp.int32), axis=1)
    return (positions[None, :] <= positions[:, None]) & (labels[:, None] == labels[None, :])


def masked_scores(query_rows, keys, doc_starts):
    scores = jnp.einsum(
        "qhd,khd->hqk", query_rows, keys, preferred_element_type=jnp.float32
    ) * HEAD ** (-0.5)
    return jnp.where(doc_mask(doc_starts)[None], scores, -1e30)


def attend(items):
    query_rows, keys, value_rows, doc_starts = items
    scores = masked_scores(query_rows, keys, doc_starts)
    top = jnp.max(scores, axis=-1, keepdims=True)
    weights = jnp.exp(scores - top)
    total = jnp.sum(weights, axis=-1, keepdims=True)
    mixed = jnp.einsum(
        "hqk,khd->qhd",
        (weights / total).astype(jnp.bfloat16),
        value_rows,
        preferred_element_type=jnp.float32,
    )
    return (mixed.astype(jnp.bfloat16), (top + jnp.log(total))[:, :, 0])


def attend_back(items):
    query_rows, keys, value_rows, doc_starts, log_totals, grad_mixed = items
    scores = masked_scores(query_rows, keys, doc_starts)
    probs = jnp.exp(scores - log_totals[:, :, None])
    grad_probs = jnp.einsum(
        "qhd,khd->hqk", grad_mixed, value_rows, preferred_element_type=jnp.float32
    )
    inner = jnp.sum(probs * grad_probs, axis=-1, keepdims=True)
    grad_scores = (probs * (grad_probs - inner)).astype(jnp.bfloat16)
    query_gradient = jnp.einsum(
        "hqk,khd->qhd", grad_scores, keys, preferred_element_type=jnp.float32
    ) * HEAD ** (-0.5)
    grad_k = jnp.einsum(
        "hqk,qhd->khd", grad_scores, query_rows, preferred_element_type=jnp.float32
    ) * HEAD ** (-0.5)
    value_gradient = jnp.einsum(
        "hqk,qhd->khd", probs.astype(jnp.bfloat16), grad_mixed, preferred_element_type=jnp.float32
    )
    return (
        query_gradient.astype(jnp.bfloat16),
        grad_k.astype(jnp.bfloat16),
        value_gradient.astype(jnp.bfloat16),
    )


def reduce_adapters(part_a, second_portion):
    return (lax.psum(part_a, ("dp", "tensor")), lax.psum(second_portion, "dp"))


def plain_body(
    activations,
    starts,
    attention_weights,
    projection_weight,
    feedforward_weight,
    output_weight,
    norm_gains,
    norm_biases,
    output_biases,
    query_value_bias,
    feedforward_bias,
    adapter_down_weight,
    adapter_up_weight,
):
    section = lax.axis_index("section")
    first = section == 0
    batches = activations.shape[1]
    own_rows = activations.shape[2]
    width = activations.shape[3]
    head_cols = projection_weight.shape[1]
    local_heads = head_cols // HEAD
    shaped = (-1, SEQ_LEN, local_heads, HEAD)
    w_cat = jnp.concatenate(
        [attention_weights[0, 0], attention_weights[0, 1], attention_weights[0, 2]], axis=1
    )
    stacked_down_maps = jnp.concatenate(
        [adapter_down_weight[0, 0], adapter_down_weight[0, 1]], axis=1
    )

    def forward_relay(rows, group_starts):
        normalized_rows = layer_norm(rows, norm_gains[0, 0], norm_biases[0, 0]).astype(jnp.bfloat16)
        gathered = lax.all_gather(normalized_rows, "tensor", axis=0, tiled=True)
        joined = jnp.dot(gathered, w_cat, preferred_element_type=jnp.float32)
        apply_adapter = jnp.dot(
            gathered, stacked_down_maps, preferred_element_type=jnp.float32
        ).astype(jnp.bfloat16)
        query_rows = (
            joined[:, :head_cols]
            + query_value_bias[0, 0]
            + adapter_scale
            * jnp.dot(
                apply_adapter[:, :ADAPTER_RANK],
                adapter_up_weight[0, 0],
                preferred_element_type=jnp.float32,
            )
        ).astype(jnp.bfloat16)
        keys = joined[:, head_cols : 2 * head_cols].astype(jnp.bfloat16)
        value_rows = (
            joined[:, 2 * head_cols :]
            + query_value_bias[0, 1]
            + adapter_scale
            * jnp.dot(
                apply_adapter[:, ADAPTER_RANK:],
                adapter_up_weight[0, 1],
                preferred_element_type=jnp.float32,
            )
        ).astype(jnp.bfloat16)
        mixed, log_totals = lax.map(
            attend,
            (
                query_rows.reshape(shaped),
                keys.reshape(shaped),
                value_rows.reshape(shaped),
                group_starts,
            ),
        )
        mixed = mixed.reshape(-1, head_cols)
        middle = (
            rows
            + lax.psum_scatter(
                jnp.dot(mixed, projection_weight[0], preferred_element_type=jnp.float32),
                "tensor",
                scatter_dimension=0,
                tiled=True,
            )
            + output_biases[0, 0]
        )
        normed_two = layer_norm(middle, norm_gains[0, 1], norm_biases[0, 1]).astype(jnp.bfloat16)
        hidden = (
            jnp.dot(
                lax.all_gather(normed_two, "tensor", axis=0, tiled=True),
                feedforward_weight[0],
                preferred_element_type=jnp.float32,
            )
            + feedforward_bias[0]
        )
        active = gelu_tanh(hidden).astype(jnp.bfloat16)
        output = (
            middle
            + lax.psum_scatter(
                jnp.dot(active, output_weight[0], preferred_element_type=jnp.float32).astype(
                    jnp.bfloat16
                ),
                "tensor",
                scatter_dimension=0,
                tiled=True,
            ).astype(jnp.float32)
            + output_biases[0, 1]
        )
        return (
            output,
            (
                rows,
                middle,
                gathered,
                apply_adapter,
                query_rows,
                keys,
                value_rows,
                log_totals,
                hidden,
            ),
        )

    def backward_relay(grad_rows, cache, group_starts):
        rows, middle, gathered, apply_adapter, query_rows, keys, value_rows, log_totals, hidden = (
            cache
        )
        grad_active = contract_axes(
            lax.all_gather(grad_rows.astype(jnp.bfloat16), "tensor", axis=0, tiled=True),
            output_weight[0],
            1,
            1,
        )
        _, gelu_back = jax.vjp(gelu_tanh, hidden)
        grad_hidden = gelu_back(grad_active)[0].astype(jnp.bfloat16)
        grad_normed_two = lax.psum_scatter(
            contract_axes(grad_hidden, feedforward_weight[0], 1, 1).astype(jnp.bfloat16),
            "tensor",
            scatter_dimension=0,
            tiled=True,
        ).astype(jnp.float32)
        _, norm_two_back = jax.vjp(
            lambda inner_rows: layer_norm(inner_rows, norm_gains[0, 1], norm_biases[0, 1]), middle
        )
        grad_middle = grad_rows + norm_two_back(grad_normed_two)[0]
        grad_mixed = contract_axes(
            lax.all_gather(grad_middle.astype(jnp.bfloat16), "tensor", axis=0, tiled=True),
            projection_weight[0],
            1,
            1,
        ).astype(jnp.bfloat16)
        query_gradient, grad_k, value_gradient = lax.map(
            attend_back,
            (
                query_rows.reshape(shaped),
                keys.reshape(shaped),
                value_rows.reshape(shaped),
                group_starts,
                log_totals,
                grad_mixed.reshape(shaped),
            ),
        )
        query_gradient = query_gradient.reshape(-1, head_cols)
        grad_k = grad_k.reshape(-1, head_cols)
        value_gradient = value_gradient.reshape(-1, head_cols)
        grad_low = jnp.concatenate(
            [
                adapter_scale * contract_axes(query_gradient, adapter_up_weight[0, 0], 1, 1),
                adapter_scale * contract_axes(value_gradient, adapter_up_weight[0, 1], 1, 1),
            ],
            axis=1,
        ).astype(jnp.bfloat16)
        grad_joined = jnp.concatenate([query_gradient, grad_k, value_gradient], axis=1)
        grad_normed = lax.psum_scatter(
            (
                contract_axes(grad_joined, w_cat, 1, 1)
                + contract_axes(grad_low, stacked_down_maps, 1, 1)
            ).astype(jnp.bfloat16),
            "tensor",
            scatter_dimension=0,
            tiled=True,
        ).astype(jnp.float32)
        _, norm_back = jax.vjp(
            lambda inner_rows: layer_norm(inner_rows, norm_gains[0, 0], norm_biases[0, 0]), rows
        )
        grad_in = grad_middle + norm_back(grad_normed)[0]
        grad_down = contract_axes(gathered, grad_low, 0, 0)
        part_a = jnp.stack([grad_down[:, :ADAPTER_RANK], grad_down[:, ADAPTER_RANK:]])
        second_portion = adapter_scale * jnp.stack(
            [
                contract_axes(apply_adapter[:, :ADAPTER_RANK], query_gradient, 0, 0),
                contract_axes(apply_adapter[:, ADAPTER_RANK:], value_gradient, 0, 0),
            ]
        )
        return (grad_in, part_a, second_portion)

    received = jnp.zeros((own_rows, width), jnp.bfloat16)
    finals = []
    stored = []
    for tick in range(batches + 1):
        batch_index = jnp.clip(tick - section, 0, batches - 1)
        own = lax.dynamic_index_in_dim(activations[0], batch_index, 0, keepdims=False)
        rows = jnp.where(first, own, received).astype(jnp.float32)
        group_starts = lax.dynamic_index_in_dim(starts, batch_index, 0, keepdims=False)
        output, cache = forward_relay(rows, group_starts)
        finals.append(output)
        stored.append(rows)
        if tick < batches:
            received = from_behind(output.astype(jnp.bfloat16), "section", 1)
    stacked = jax.tree.map(lambda *items: jnp.stack(items), *stored)
    returned = jnp.zeros((own_rows, width), jnp.bfloat16)
    totals_a = jnp.zeros((2, width, ADAPTER_RANK), jnp.float32)
    totals_b = jnp.zeros((2, ADAPTER_RANK, head_cols), jnp.float32)
    grads_in = []
    for tick in range(batches + 1):
        position = tick - 1 + section
        batch_index = jnp.clip(position, 0, batches - 1)
        valid = ((position >= 0) & (position < batches)).astype(jnp.float32)
        own = lax.dynamic_index_in_dim(activations[0], batch_index, 0, keepdims=False)
        grad_rows = jnp.where(first, returned, own).astype(jnp.float32) * valid
        group_starts = lax.dynamic_index_in_dim(starts, batch_index, 0, keepdims=False)
        slot_index = jnp.clip(tick - 1 + 2 * section, 0, batches)
        picked = lax.dynamic_index_in_dim(stacked, slot_index, 0, keepdims=False)
        _, cache = forward_relay(picked, group_starts)
        grad_in, part_a, second_portion = backward_relay(grad_rows, cache, group_starts)
        grads_in.append(grad_in)
        if tick < batches:
            returned = from_behind(grad_in.astype(jnp.bfloat16), "section", -1)
        part_a, second_portion = reduce_adapters(part_a, second_portion)
        totals_a = totals_a + part_a
        totals_b = totals_b + second_portion
    combined = jnp.stack(
        [jnp.where(first, grads_in[index + 1], finals[index + 1]) for index in range(batches)]
    )
    return (combined[None], totals_a[None], totals_b[None])


LOW = 2 * ADAPTER_RANK
VMEM_SPACE = pl.BlockSpec(memory_space=pltpu.VMEM)
SMEM_SPACE = pl.BlockSpec(memory_space=pltpu.SMEM)
HBM_SPACE = pl.BlockSpec(memory_space=pltpu.HBM)
BLOCK = 256


def send(block, route):
    pairs = []
    for s in range(2):
        for t in range(4):
            to = route(s, t)
            if to is not None:
                pairs.append((s * 4 + t, to[0] * 4 + to[1]))
    return lax.ppermute(block, ("section", "tensor"), pairs)


def other_core(block):
    return send(block, lambda s, t: (1 - s, t))


def x_swap(block):
    return send(block, lambda s, t: (s, t ^ 1))


def y_swap(block):
    return send(block, lambda s, t: (s, t ^ 2))


def after(value, *others):
    return lax.optimization_barrier((value, others))[0]


def cross_send(block, source=0):
    return send(block, lambda s, t: (t >> 1, t ^ 2) if s == source else None)


def collect(target, same_chip, cross_chip):
    return (
        send(same_chip, lambda s, t: (target, t) if s == t >> 1 and s != target else None),
        send(cross_chip, lambda s, t: (target, t ^ 2) if s != t >> 1 else None),
    )


def mm(left, right):
    return jnp.dot(left, right, preferred_element_type=jnp.float32)


def mm_nt(left, right):
    return contract_axes(left, right, 1, 1)


def norm_back(rows, gain, grad):
    mean = jnp.mean(rows, axis=-1, keepdims=True)
    centered = rows - mean
    scale = lax.rsqrt(jnp.mean(centered * centered, axis=-1, keepdims=True) + 1e-05)
    unit = centered * scale
    scaled = grad * gain
    return scale * (
        scaled
        - jnp.mean(scaled, axis=-1, keepdims=True)
        - unit * jnp.mean(scaled * unit, axis=-1, keepdims=True)
    )


def gelu_both(value):
    square = value * value
    bent = jnp.tanh(0.7978845608028654 * value * (1.0 + 0.044715 * square))
    half = 0.5 * (1.0 + bent)
    slope = half + 0.5 * value * (1.0 - bent * bent) * (
        0.7978845608028654 * (1.0 + 3.0 * 0.044715 * square)
    )
    return value * half, slope


def cost(flops, read):
    return pl.CostEstimate(flops=1000, bytes_accessed=1000, transcendentals=0)


def kernel_params(mib):
    return pltpu.CompilerParams(vmem_limit_bytes=mib * 1024 * 1024)


def position_mask(meta, query_block, key_block):
    shape = (BLOCK, BLOCK)
    key_pos = key_block * BLOCK + lax.broadcasted_iota(jnp.int32, shape, 0)
    query_pos = query_block * BLOCK + lax.broadcasted_iota(jnp.int32, (1, BLOCK), 1)
    low = jnp.zeros((1, BLOCK), jnp.int32)
    for c in range(4):
        first = meta[4 + c]
        low = jnp.where(first <= query_pos, jnp.maximum(low, first), low)
    valid = key_pos >= low
    if query_block == key_block:
        valid = valid & (key_pos <= query_pos)
    return valid


def head_lanes(half):
    return (lax.broadcasted_iota(jnp.int32, (1, 2 * HEAD), 1) // HEAD) == half


def start_pick(choices, target, sem):
    for condition, source in choices:

        @pl.when(condition)
        def _(source=source):
            pltpu.make_async_copy(source, target, sem).start()


def load_qkv_weight(layer, meta, w_own, w_other, w_cross, w_buf, sem):
    s, y = meta[0], meta[2]
    start_pick(
        (
            ((s == y) & (s == layer), w_own),
            ((s == y) & (s != layer), w_other),
            (s != y, w_cross),
        ),
        w_buf,
        sem,
    )


def block_places(meta):
    s, x = meta[0], meta[1]
    return (x + 2 * s, x + 2 * (1 - s), (1 - x) + 2 * s, (1 - x) + 2 * (1 - s))


def attend_kernel(
    layer, meta, n0, n1, n2, n3, shared, varied, w_own, w_other, w_cross,
    q_out, k_out, v_out, lse_out, mixed_out, o0, o1, o2, o3,
    w_buf, score_buf, vt_buf, q_ref, k_ref, v_ref, lse_ref, mixed_ref, sem, out_sems,
):
    load_qkv_weight(layer, meta, w_own, w_other, w_cross, w_buf, sem)
    down = shared[layer, 8:16, :].astype(jnp.bfloat16)
    bias = varied[layer, 1:2, :]
    up = varied[layer, 8:16, 0:512].astype(jnp.bfloat16)
    places = block_places(meta)
    pltpu.make_async_copy(w_own, w_buf, sem).wait()
    for place, block in zip(places, (n0, n1, n2, n3)):
        rows = pl.ds(pl.multiple_of(place * BLOCK, BLOCK), BLOCK)
        normed = block[...]
        low = mm_nt(normed, down).astype(jnp.bfloat16)
        lifted = adapter_scale * mm(low, up)
        q_ref[rows, :] = (mm(normed, w_buf[0]) + bias[:, 0:256] + lifted[:, 0:256]).astype(
            jnp.bfloat16
        )
        k_ref[rows, :] = mm(normed, w_buf[1]).astype(jnp.bfloat16)
        v_ref[rows, :] = (mm(normed, w_buf[2]) + bias[:, 256:512] + lifted[:, 256:512]).astype(
            jnp.bfloat16
        )
    saved = [
        pltpu.make_async_copy(source, target, out_sems.at[i])
        for i, (source, target) in enumerate(
            (
                (q_ref, q_out), (k_ref, k_out), (v_ref, v_out), (lse_ref, lse_out),
                (mixed_ref, mixed_out),
            )
        )
    ]
    for copy in saved[:3]:
        copy.start()
    for b in range(4):
        vt_buf[:, b * BLOCK : (b + 1) * BLOCK] = v_ref[b * BLOCK : (b + 1) * BLOCK, :].T

    def one_head(head, carry):
        lanes = pl.ds(pl.multiple_of((head // 2) * 128, 128), 128)
        chosen = head_lanes(head % 2)
        deep = pl.ds(pl.multiple_of(head * HEAD, HEAD), HEAD)
        for i in range(4):
            part = q_ref[i * BLOCK : (i + 1) * BLOCK, lanes]
            query = jnp.where(chosen, part * HEAD ** (-0.5), 0.0).astype(jnp.bfloat16)
            top = jnp.full((1, BLOCK), -1e30, jnp.float32)
            for j in range(i + 1):
                scores = mm_nt(k_ref[j * BLOCK : (j + 1) * BLOCK, lanes], query)
                scores = jnp.where(position_mask(meta, i, j), scores, -1e30)
                score_buf[j] = scores
                top = jnp.maximum(top, jnp.max(scores, axis=0, keepdims=True))
            total = jnp.zeros((1, BLOCK), jnp.float32)
            mixed = jnp.zeros((HEAD, BLOCK), jnp.float32)
            for j in range(i + 1):
                weights = jnp.exp(score_buf[j] - top)
                total = total + jnp.sum(weights, axis=0, keepdims=True)
                mixed = mixed + mm(
                    vt_buf[deep, j * BLOCK : (j + 1) * BLOCK], weights.astype(jnp.bfloat16)
                )
            mixed_ref[deep, i * BLOCK : (i + 1) * BLOCK] = mixed / total
            lse_ref[pl.ds(head, 1), i * BLOCK : (i + 1) * BLOCK] = top + jnp.log(total)
        return carry

    lax.fori_loop(0, 4, one_head, 0)
    for copy in saved[3:]:
        copy.start()
    for place, out in zip(places, (o0, o1, o2, o3)):
        columns = pl.ds(pl.multiple_of(place * BLOCK, BLOCK), BLOCK)
        heads_out = mixed_ref[:, columns].T.astype(jnp.bfloat16)
        out[...] = mm_nt(heads_out, w_buf[3]).astype(jnp.bfloat16)
    for copy in saved:
        copy.wait()


def attend_call(layer, meta, blocks, shared, varied, *weight):
    bf, f32 = jnp.bfloat16, jnp.float32
    wide = jax.ShapeDtypeStruct((SEQ_LEN, 256), bf)
    piece = jax.ShapeDtypeStruct((BLOCK, 1024), bf)
    return pl.pallas_call(
        functools.partial(attend_kernel, layer),
        in_specs=[SMEM_SPACE] + [VMEM_SPACE] * 6 + [HBM_SPACE] * 3,
        out_specs=[HBM_SPACE] * 5 + [VMEM_SPACE] * 4,
        out_shape=[wide, wide, wide, jax.ShapeDtypeStruct((8, SEQ_LEN), f32),
                   jax.ShapeDtypeStruct((256, SEQ_LEN), f32)] + [piece] * 4,
        scratch_shapes=[
            pltpu.VMEM((4, 1024, 256), bf),
            pltpu.VMEM((4, BLOCK, BLOCK), f32),
            pltpu.VMEM((256, SEQ_LEN), bf),
            pltpu.VMEM((SEQ_LEN, 256), bf),
            pltpu.VMEM((SEQ_LEN, 256), bf),
            pltpu.VMEM((SEQ_LEN, 256), bf),
            pltpu.VMEM((8, SEQ_LEN), f32),
            pltpu.VMEM((256, SEQ_LEN), f32),
            pltpu.SemaphoreType.DMA,
            pltpu.SemaphoreType.DMA((5,)),
        ],
        compiler_params=kernel_params(40),
        cost_estimate=cost(3.5e9, 8e6),
        name="attention_forward",
    )(meta, *blocks, shared, varied, *weight)


def attend_back_kernel(
    layer, meta, n0, n1, n2, n3, g0, g1, g2, g3, q_ref, k_ref, v_ref, lse_ref, mixed_ref,
    shared, varied, w_own, w_other, w_cross,
    keep0, give0, keep1, give1, down_ref, up_ref,
    w_buf, kt_buf, do_buf, delta_buf, dqt_buf, dk_buf, dv_buf, dq_buf, sem,
):
    load_qkv_weight(layer, meta, w_own, w_other, w_cross, w_buf, sem)
    places = block_places(meta)
    pltpu.make_async_copy(w_own, w_buf, sem).wait()
    for place, block in zip(places, (g0, g1, g2, g3)):
        rows = pl.ds(pl.multiple_of(place * BLOCK, BLOCK), BLOCK)
        do_buf[rows, :] = mm(block[...], w_buf[3]).astype(jnp.bfloat16)
    for b in range(4):
        span = slice(b * BLOCK, (b + 1) * BLOCK)
        kt_buf[:, span] = k_ref[span, :].T
        product = do_buf[span, :].astype(jnp.float32).T * mixed_ref[:, span]
        for head in range(4):
            delta_buf[head : head + 1, span] = jnp.sum(
                product[head * HEAD : (head + 1) * HEAD], axis=0, keepdims=True
            )
    dk_buf[...] = jnp.zeros_like(dk_buf)
    dv_buf[...] = jnp.zeros_like(dv_buf)

    def one_head(head, carry):
        lanes = pl.ds(pl.multiple_of((head // 2) * 128, 128), 128)
        chosen = head_lanes(head % 2)
        deep = pl.ds(pl.multiple_of(head * HEAD, HEAD), HEAD)
        for i in range(4):
            span = slice(i * BLOCK, (i + 1) * BLOCK)
            query = jnp.where(chosen, q_ref[span, lanes] * HEAD ** (-0.5), 0.0).astype(jnp.bfloat16)
            grad_mixed = jnp.where(chosen, do_buf[span, lanes], 0.0).astype(jnp.bfloat16)
            lse = lse_ref[pl.ds(head, 1), span]
            delta = delta_buf[pl.ds(head, 1), span]
            grad_query = jnp.zeros((HEAD, BLOCK), jnp.float32)
            for j in range(i + 1):
                keys = slice(j * BLOCK, (j + 1) * BLOCK)
                scores = mm_nt(k_ref[keys, lanes], query)
                probs = jnp.where(position_mask(meta, i, j), jnp.exp(scores - lse), 0.0)
                grad_probs = mm_nt(v_ref[keys, lanes], grad_mixed)
                grad_scores = (probs * (grad_probs - delta)).astype(jnp.bfloat16)
                dv_buf[keys, lanes] += mm(probs.astype(jnp.bfloat16), grad_mixed)
                dk_buf[keys, lanes] += mm(grad_scores, query)
                grad_query = grad_query + mm(kt_buf[deep, keys], grad_scores)
            dqt_buf[deep, span] = grad_query * HEAD ** (-0.5)
        return carry

    lax.fori_loop(0, 4, one_head, 0)
    down = shared[layer, 8:16, :].astype(jnp.bfloat16)
    up = varied[layer, 8:16, 0:512].astype(jnp.bfloat16)
    for b in range(4):
        span = slice(b * BLOCK, (b + 1) * BLOCK)
        dq_buf[span, :] = dqt_buf[:, span].T.astype(jnp.bfloat16)
    total_down = jnp.zeros((LOW, 1024), jnp.float32)
    total_up = jnp.zeros((LOW, 512), jnp.float32)
    targets = (keep0, give0, keep1, give1)
    for place, block, target in zip(places, (n0, n1, n2, n3), targets):
        rows = pl.ds(pl.multiple_of(place * BLOCK, BLOCK), BLOCK)
        normed = block[...]
        grad_q = dq_buf[rows, :]
        grad_k = dk_buf[rows, :].astype(jnp.bfloat16)
        grad_v = dv_buf[rows, :].astype(jnp.bfloat16)
        both = jnp.concatenate([grad_q, grad_v], axis=1)
        low_grad = (adapter_scale * mm_nt(both, up)).astype(jnp.bfloat16)
        low_grad_t = (adapter_scale * mm_nt(up, both)).astype(jnp.bfloat16)
        low_t = mm_nt(down, normed).astype(jnp.bfloat16)
        grad_normed = (
            mm_nt(grad_q, w_buf[0]) + mm_nt(grad_k, w_buf[1]) + mm_nt(grad_v, w_buf[2])
            + mm(low_grad, down)
        )
        target[...] = grad_normed.astype(jnp.bfloat16)
        total_down = total_down + mm(low_grad_t, normed)
        total_up = total_up + adapter_scale * mm(low_t, both)
    down_ref[...] = total_down
    up_ref[...] = total_up


def attend_back_call(layer, meta, blocks, grads, saved, shared, varied, *weight):
    bf, f32 = jnp.bfloat16, jnp.float32
    part = jax.ShapeDtypeStruct((BLOCK, 1024), bf)
    return pl.pallas_call(
        functools.partial(attend_back_kernel, layer),
        in_specs=[SMEM_SPACE] + [VMEM_SPACE] * 15 + [HBM_SPACE] * 3,
        out_specs=[VMEM_SPACE] * 6,
        out_shape=[part, part, part, part, jax.ShapeDtypeStruct((LOW, 1024), f32),
                   jax.ShapeDtypeStruct((LOW, 512), f32)],
        scratch_shapes=[
            pltpu.VMEM((4, 1024, 256), bf),
            pltpu.VMEM((256, SEQ_LEN), bf),
            pltpu.VMEM((SEQ_LEN, 256), bf),
            pltpu.VMEM((8, SEQ_LEN), f32),
            pltpu.VMEM((256, SEQ_LEN), f32),
            pltpu.VMEM((SEQ_LEN, 256), f32),
            pltpu.VMEM((SEQ_LEN, 256), f32),
            pltpu.VMEM((SEQ_LEN, 256), bf),
            pltpu.SemaphoreType.DMA,
        ],
        compiler_params=kernel_params(48),
        cost_estimate=cost(6e9, 12e6),
        name="attention_backward",
    )(meta, *blocks, *grads, *saved, shared, varied, *weight)


def summed(keep, take, far):
    return keep[...].astype(jnp.float32) + take[...].astype(jnp.float32) + far[...].astype(jnp.float32)


def rows_middle_kernel(layer, h_ref, keep, take, far, shared, middle_ref, normed_ref):
    middle = h_ref[...].astype(jnp.float32) + summed(keep, take, far) + shared[layer, 4:5, :]
    middle_ref[...] = middle
    normed_ref[...] = layer_norm(middle, shared[layer, 1:2, :], shared[layer, 3:4, :]).astype(
        jnp.bfloat16
    )


def load_units(layer, meta, pieces, w1, w2, sems):
    s, y = meta[0], meta[2]
    own, other, cross = pieces
    copies = []
    for m, matrix in enumerate((w1, w2)):
        rows = slice(1024 * m, 1024 * (m + 1))
        start_pick(
            (
                ((s == y) & (s == layer), own.at[rows]),
                ((s == y) & (s != layer), other.at[rows]),
                (s != y, cross.at[rows]),
            ),
            matrix,
            sems.at[m],
        )
        copies.append(pltpu.make_async_copy(own.at[rows], matrix, sems.at[m]))
    return copies


def units_kernel(layer, meta, n0, n1, bias, *rest):
    out0, out1, slope0, slope1, w1, w2, sems = rest[3:]
    waits = load_units(layer, meta, rest[:3], w1, w2, sems)
    waits[0].wait()
    actives = []
    for block, slope_ref in ((n0, slope0), (n1, slope1)):
        active, slope = gelu_both(mm(block[...], w1[...]) + bias[layer, 0:1, :])
        actives.append(active.astype(jnp.bfloat16))
        slope_ref[...] = slope.astype(jnp.bfloat16)
    waits[1].wait()
    for active, out in zip(actives, (out0, out1)):
        out[...] = mm(active, w2[...]).astype(jnp.bfloat16)


def units_turn_kernel(layer, meta, n0, n1, g0, g1, bias, *rest):
    back0, back1, out0, out1, w1, w2, sems = rest[3:]
    for copy in load_units(layer, meta, rest[:3], w1, w2, sems):
        copy.wait()
    for block, grad, back, out in ((n0, g0, back0, out0), (n1, g1, back1, out1)):
        active, slope = gelu_both(mm(block[...], w1[...]) + bias[layer, 0:1, :])
        grad_hidden = (mm_nt(grad[...], w2[...]) * slope).astype(jnp.bfloat16)
        back[...] = mm_nt(grad_hidden, w1[...]).astype(jnp.bfloat16)
        out[...] = mm(active.astype(jnp.bfloat16), w2[...]).astype(jnp.bfloat16)


def units_back_kernel(layer, meta, g0, g1, slope0, slope1, *rest):
    back0, back1, w1, w2, sems = rest[3:]
    waits = load_units(layer, meta, rest[:3], w1, w2, sems)
    waits[1].wait()
    grads = [
        (mm_nt(grad[...], w2[...]) * slope[...].astype(jnp.float32)).astype(jnp.bfloat16)
        for grad, slope in ((g0, slope0), (g1, slope1))
    ]
    waits[0].wait()
    for grad, back in zip(grads, (back0, back1)):
        back[...] = mm_nt(grad, w1[...]).astype(jnp.bfloat16)


def rows_first_kernel(rows, shared, normed_ref):
    normed_ref[...] = layer_norm(
        rows[...].astype(jnp.float32), shared[0, 0:1, :], shared[0, 2:3, :]
    ).astype(jnp.bfloat16)


def rows_next_kernel(middle, keep, take, far, shared, between_ref, normed_ref):
    between = (middle[...] + summed(keep, take, far) + shared[0, 5:6, :]).astype(jnp.bfloat16)
    between_ref[...] = between
    normed_ref[...] = layer_norm(
        between.astype(jnp.float32), shared[1, 0:1, :], shared[1, 2:3, :]
    ).astype(jnp.bfloat16)


def rows_turn_kernel(layer, middle, g_ref, keep, take, far, shared, grad_ref, sent_ref):
    grad_middle = g_ref[...].astype(jnp.float32) + norm_back(
        middle[...], shared[layer, 1:2, :], summed(keep, take, far)
    )
    grad_ref[...] = grad_middle
    sent_ref[...] = grad_middle.astype(jnp.bfloat16)


def rows_before_kernel(gm_ref, keep, take, far, between_ref, shared, grad_ref):
    grad_rows = gm_ref[...] + norm_back(
        between_ref[...].astype(jnp.float32), shared[1, 0:1, :], summed(keep, take, far)
    )
    grad_ref[...] = grad_rows.astype(jnp.bfloat16)


def rows_output_kernel(middle, keep, take, far, shared, wide_ref, narrow_ref):
    total = middle[...] + summed(keep, take, far) + shared[1, 5:6, :]
    wide_ref[...] = total
    narrow_ref[...] = total.astype(jnp.bfloat16)


def rows_final_kernel(gm_ref, keep, take, far, h_ref, shared, wide_ref, narrow_ref):
    grad_in = gm_ref[...] + norm_back(
        h_ref[...].astype(jnp.float32), shared[0, 0:1, :], summed(keep, take, far)
    )
    wide_ref[...] = grad_in
    narrow_ref[...] = grad_in.astype(jnp.bfloat16)


def plain_call(kernel, scalar, small, large, outs, scratch, flops, name, mib=40):
    specs = [VMEM_SPACE] * len(small) + [HBM_SPACE] * len(large)
    operands = (*small, *large)
    if scalar is not None:
        specs, operands = [SMEM_SPACE] + specs, (scalar, *operands)
    return pl.pallas_call(
        kernel,
        in_specs=specs,
        out_specs=[VMEM_SPACE] * len(outs),
        out_shape=outs,
        scratch_shapes=scratch,
        compiler_params=kernel_params(mib),
        cost_estimate=cost(flops, 8e6),
        name=name,
    )(*operands)


def deal_rows(source, slots, section, y):
    moved = [
        send(
            slots[m],
            lambda s, t, m=m: (t >> 1, 2 * m + (t & 1))
            if s == source and (t >> 1, 2 * m + (t & 1)) != (s, t)
            else None,
        )
        for m in range(2)
    ]
    stays = (section == source) & (y == source)
    return jnp.where(stays, slots[source], jnp.where(y == 0, moved[0], moved[1]))


def z_swap(block):
    return lax.ppermute(block, "dp", [(i, i ^ 1) for i in range(lax.axis_size("dp"))])


def gather_rows(own):
    near = other_core(own)
    far = x_swap(own)
    return (own, near, far, other_core(far))


def reduce_rows(keep0, give0, keep1, give1):
    passed = (keep1.astype(jnp.float32) + other_core(give1).astype(jnp.float32)).astype(jnp.bfloat16)
    return keep0, other_core(give0), x_swap(passed)


def total_over_z(part_down, part_up):
    both = jnp.concatenate([part_down, part_up], axis=1)
    size = lax.axis_size("dp")
    step = 1
    while step < size:
        both = both + lax.ppermute(both, "dp", [(i, i ^ step) for i in range(size)])
        step *= 2
    return both


def total_over_cores(both):
    both = both + y_swap(both)
    down = both[:, :1024]
    return down + other_core(down), both[:, 1024:]


def total_over_x(layer, total):
    down, up = total
    moved = send(up, lambda s, t: (layer, t) if s == t >> 1 and s != layer else None)
    stays = lax.axis_index("tensor") // 2 == layer
    return down + x_swap(down), jnp.where(stays, up, moved)


def relay_body(
    activations, starts, attention_weights, projection_weight, feedforward_weight, output_weight,
    norm_gains, norm_biases, output_biases, query_value_bias, feedforward_bias,
    adapter_down_weight, adapter_up_weight,
):
    bf, f32 = jnp.bfloat16, jnp.float32
    section = lax.axis_index("section")
    place = lax.axis_index("tensor")
    y, x = place // 2, place % 2
    first = section == 0

    rows = deal_rows(0, activations[0], section, y)
    down_rows = adapter_down_weight[0].astype(f32).transpose(0, 2, 1).reshape(LOW, 1024)
    up0 = adapter_up_weight[0, 0].astype(f32)
    up1 = adapter_up_weight[0, 1].astype(f32)
    zero = jnp.zeros((ADAPTER_RANK, 256), f32)
    common = jnp.concatenate(
        [norm_gains[0], norm_biases[0], output_biases[0], jnp.zeros((2, 1024), f32), down_rows]
    )
    own_part = jnp.concatenate(
        [
            feedforward_bias,
            jnp.pad(query_value_bias[0].reshape(1, 512), ((0, 0), (0, 512))),
            jnp.zeros((6, 1024), f32),
            jnp.concatenate([up0, zero, jnp.zeros((ADAPTER_RANK, 512), f32)], axis=1),
            jnp.concatenate([zero, up1, jnp.zeros((ADAPTER_RANK, 512), f32)], axis=1),
        ]
    )
    partner = other_core(common)
    partner_part = other_core(own_part)
    parts = jnp.where(
        first, jnp.stack([own_part, partner_part]), jnp.stack([partner_part, own_part])
    )
    near_varied = jnp.where(section == y, parts, y_swap(parts))
    shared = jnp.where(first, jnp.stack([common, partner]), jnp.stack([partner, common]))
    meta = jnp.concatenate(
        [
            jnp.stack([section, x, y, place]).astype(jnp.int32),
            lax.dynamic_index_in_dim(starts, y, 0, keepdims=False).reshape(4),
        ]
    )
    own_a = jnp.concatenate([attention_weights[0], projection_weight[0].T[None]])
    other_a = other_core(own_a)
    weights_a0 = (own_a, other_a, cross_send(other_a, 1))

    sheet = jax.ShapeDtypeStruct((BLOCK, 1024), f32)
    thin = jax.ShapeDtypeStruct((BLOCK, 1024), bf)
    quarter_scratch = [
        pltpu.VMEM((1024, 1024), bf), pltpu.VMEM((1024, 1024), bf), pltpu.SemaphoreType.DMA((2,))
    ]

    normed = plain_call(rows_first_kernel, None, (rows, shared), (), [thin], [], 1e7, "rows_first")[0]
    own_b = jnp.concatenate(after((feedforward_weight[0], output_weight[0]), normed))
    near, far = other_core(normed), x_swap(normed)
    far, near_varied, own_b, *weights_a0 = lax.optimization_barrier(
        (far, near_varied, own_b, *weights_a0)
    )
    other_b = other_core(own_b)
    blocks0 = (normed, near, far, other_core(far))
    weights_b0 = (own_b, other_b, cross_send(after(own_b, far)))
    *saved0, keep0, give0, keep1, give1 = attend_call(
        0, meta, blocks0, shared, near_varied, *weights_a0
    )
    weights_a1 = (own_a, other_a, cross_send(after(other_a, give1)))
    sums = reduce_rows(keep0, give0, keep1, give1)
    middle0, normed0 = plain_call(
        functools.partial(rows_middle_kernel, 0), None, (rows, *sums, shared), (), [sheet, thin],
        [], 1e7, "rows_middle",
    )
    grad_out = deal_rows(1, after(activations[0], middle0), section, y)
    n0, n1, n2 = normed0, other_core(normed0), x_swap(normed0)
    units = functools.partial(units_kernel, 0)
    keep0, give0, *slopes_near = plain_call(
        units, meta, (n0, n1, near_varied), weights_b0, [thin] * 4, quarter_scratch,
        2.2e9, "units_near",
    )
    n3 = other_core(after(n2, keep0))
    keep1, give1, *slopes_far = plain_call(
        units, meta, (n2, n3, near_varied), weights_b0, [thin] * 4, quarter_scratch,
        2.2e9, "units_far",
    )
    sums = reduce_rows(keep0, give0, keep1, give1)
    between, normed = plain_call(
        rows_next_kernel, None, (middle0, *sums, shared), (), [thin, thin], [], 1e7, "rows_next",
    )
    normed, grad_out, *weights_a1 = lax.optimization_barrier((normed, grad_out, *weights_a1))
    weights_b1 = (own_b, other_b, cross_send(after(other_b, normed)))
    blocks1 = gather_rows(normed)
    g0, g1, g2, g3 = gather_rows(after(grad_out, blocks1[2]))
    *saved1, keep0, give0, keep1, give1 = attend_call(
        1, meta, blocks1, shared, near_varied, *weights_a1
    )
    keep0, give0, keep1, give1 = after((keep0, give0, keep1, give1), g2)
    sums = reduce_rows(keep0, give0, keep1, give1)
    middle1, normed1 = plain_call(
        functools.partial(rows_middle_kernel, 1), None, (between, *sums, shared), (),
        [sheet, thin], [], 1e7, "rows_middle",
    )
    n0, n1, n2 = normed1, other_core(normed1), x_swap(normed1)
    units = functools.partial(units_turn_kernel, 1)
    keep0, give0, out_keep0, out_give0 = plain_call(
        units, meta, (n0, n1, g0, g1, near_varied), weights_b1, [thin] * 4, quarter_scratch,
        4.4e9, "units_turn_near",
    )
    n3 = other_core(after(n2, keep0))
    keep1, give1, out_keep1, out_give1 = plain_call(
        units, meta, (n2, n3, g2, g3, near_varied), weights_b1, [thin] * 4, quarter_scratch,
        4.4e9, "units_turn_far",
    )
    sums = reduce_rows(keep0, give0, keep1, give1)
    grad_middle1, sent = plain_call(
        functools.partial(rows_turn_kernel, 1), None, (middle1, grad_out, *sums, shared), (),
        [sheet, thin], [], 1e7, "rows_turn",
    )
    grads = gather_rows(sent)
    out_parts = after((out_keep0, out_give0, out_keep1, out_give1), grads[2])
    out_sums = reduce_rows(*out_parts)
    keep0, give0, keep1, give1, down1, up1 = attend_back_call(
        1, meta, blocks1, grads, saved1, shared, near_varied, *weights_a1
    )
    keep0, give0, keep1, give1 = after((keep0, give0, keep1, give1), out_sums)
    sums = reduce_rows(keep0, give0, keep1, give1)
    total1 = total_over_z(*after((down1, up1), sums[1]))
    sums, total1 = lax.optimization_barrier((sums, total1))
    grad_between = plain_call(
        rows_before_kernel, None, (grad_middle1, *sums, between, shared), (), [thin], [], 1e7,
        "rows_before",
    )[0]
    g0, g1, g2 = grad_between, other_core(grad_between), x_swap(grad_between)
    out_wide, narrow = plain_call(
        rows_output_kernel, None, (middle1, *after(out_sums, g1), shared), (),
        [sheet, thin], [], 1e7, "rows_output",
    )
    out_same, out_cross = collect(1, out_wide, narrow)
    units = functools.partial(units_back_kernel, 0)
    keep0, give0 = plain_call(
        units, meta, (g0, g1, *slopes_near), weights_b0, [thin] * 2, quarter_scratch,
        2.2e9, "units_back_near",
    )
    g3 = other_core(after(g2, keep0))
    keep1, give1 = plain_call(
        units, meta, (g2, g3, *slopes_far), weights_b0, [thin] * 2, quarter_scratch,
        2.2e9, "units_back_far",
    )
    sums = reduce_rows(keep0, give0, keep1, give1)
    total1 = total_over_cores(after(total1, sums[1]))
    sums, total1 = lax.optimization_barrier((sums, total1))
    grad_middle0, sent = plain_call(
        functools.partial(rows_turn_kernel, 0), None, (middle0, grad_between, *sums, shared), (),
        [sheet, thin], [], 1e7, "rows_turn",
    )
    grads = after(gather_rows(sent), out_same, out_cross)
    total1 = total_over_x(1, after(total1, grads))
    keep0, give0, keep1, give1, down0, up0 = attend_back_call(
        0, meta, blocks0, grads, saved0, shared, near_varied, *weights_a0
    )
    keep0, give0, keep1, give1 = after((keep0, give0, keep1, give1), total1)
    sums = reduce_rows(keep0, give0, keep1, give1)
    wide, narrow = plain_call(
        rows_final_kernel, None, (grad_middle0, *sums, rows, shared), (), [sheet, thin], [], 1e7,
        "rows_final",
    )
    in_same, in_cross = collect(0, wide, narrow)
    total0 = total_over_z(*after((down0, up0), sums[1]))
    total0 = total_over_x(0, total_over_cores(total0))
    same = jnp.where(
        first, jnp.where(y == 0, wide, in_same), jnp.where(y == 1, out_wide, out_same)
    )
    cross = jnp.where(first, in_cross, out_cross).astype(f32)
    combined = jnp.where(y == 0, jnp.stack([same, cross]), jnp.stack([cross, same]))
    grad_down = jnp.where(first, total0[0], total1[0])
    grad_up = jnp.where(first, total0[1], total1[1])
    return (
        combined[None],
        grad_down.reshape(1, 2, ADAPTER_RANK, 1024).transpose(0, 1, 3, 2),
        jnp.stack([grad_up[:ADAPTER_RANK, :256], grad_up[ADAPTER_RANK:, 256:]])[None],
    )


def body(*arrays):
    dp = lax.axis_size("dp")
    known = (
        arrays[0].shape == (1, 2, BLOCK, 1024)
        and lax.axis_size("tensor") == 4
        and lax.axis_size("section") == 2
        and arrays[3].shape == (1, 256, 1024)
        and arrays[5].shape == (1, 1024, 1024)
        and dp & (dp - 1) == 0
    )
    return relay_body(*arrays) if known else plain_body(*arrays)


def solution(mesh):
    placed = (
        P("section", None, ("dp", "tensor"), None),
        P(None, "dp", None),
        P("section", None, None, "tensor"),
        P("section", "tensor", None),
        P("section", None, "tensor"),
        P("section", "tensor", None),
        P("section", None, None),
        P("section", None, None),
        P("section", None, None),
        P("section", None, "tensor"),
        P("section", "tensor"),
        P("section", None, None, None),
        P("section", None, None, "tensor"),
    )
    return jax.shard_map(
        body,
        mesh=mesh,
        in_specs=placed,
        out_specs=(
            P("section", None, ("dp", "tensor"), None),
            P("section", None, None, None),
            P("section", None, None, "tensor"),
        ),
        check_vma=False,
    )
```

```python
import functools

import jax
import jax.numpy as jnp
from jax import lax
from jax.experimental import pallas as pl
from jax.experimental.pallas import tpu as pltpu
from jax.sharding import PartitionSpec as P

HEAD = 64
ADAPTER_RANK = 4
SEQ_LEN = 1024


adapter_scale = 8.0


def from_behind(block, axis, distance):
    devices = range(lax.axis_size(axis))
    route = [(i - distance, i) for i in devices if i - distance in devices]
    return lax.ppermute(block, axis, route)


def contract_axes(left, right, left_dim, right_dim):
    return lax.dot_general(
        left, right, (((left_dim,), (right_dim,)), ((), ())), preferred_element_type=jnp.float32
    )


def layer_norm(rows, gain, shift):
    mean = jnp.mean(rows, axis=-1, keepdims=True)
    centered = rows - mean
    spread = jnp.mean(centered * centered, axis=-1, keepdims=True)
    return centered * lax.rsqrt(spread + 1e-05) * gain + shift


def gelu_tanh(value):
    return (
        0.5
        * value
        * (1.0 + jnp.tanh(0.7978845608028654 * (value + 0.044715 * value * value * value)))
    )


def doc_mask(doc_starts):
    positions = jnp.arange(SEQ_LEN, dtype=jnp.int32)
    labels = jnp.sum((doc_starts[None, :] <= positions[:, None]).astype(jnp.int32), axis=1)
    return (positions[None, :] <= positions[:, None]) & (labels[:, None] == labels[None, :])


def masked_scores(query_rows, keys, doc_starts):
    scores = jnp.einsum(
        "qhd,khd->hqk", query_rows, keys, preferred_element_type=jnp.float32
    ) * HEAD ** (-0.5)
    return jnp.where(doc_mask(doc_starts)[None], scores, -1e30)


def attend(items):
    query_rows, keys, value_rows, doc_starts = items
    scores = masked_scores(query_rows, keys, doc_starts)
    top = jnp.max(scores, axis=-1, keepdims=True)
    weights = jnp.exp(scores - top)
    total = jnp.sum(weights, axis=-1, keepdims=True)
    mixed = jnp.einsum(
        "hqk,khd->qhd",
        (weights / total).astype(jnp.bfloat16),
        value_rows,
        preferred_element_type=jnp.float32,
    )
    return (mixed.astype(jnp.bfloat16), (top + jnp.log(total))[:, :, 0])


def attend_back(items):
    query_rows, keys, value_rows, doc_starts, log_totals, grad_mixed = items
    scores = masked_scores(query_rows, keys, doc_starts)
    probs = jnp.exp(scores - log_totals[:, :, None])
    grad_probs = jnp.einsum(
        "qhd,khd->hqk", grad_mixed, value_rows, preferred_element_type=jnp.float32
    )
    inner = jnp.sum(probs * grad_probs, axis=-1, keepdims=True)
    grad_scores = (probs * (grad_probs - inner)).astype(jnp.bfloat16)
    query_gradient = jnp.einsum(
        "hqk,khd->qhd", grad_scores, keys, preferred_element_type=jnp.float32
    ) * HEAD ** (-0.5)
    grad_k = jnp.einsum(
        "hqk,qhd->khd", grad_scores, query_rows, preferred_element_type=jnp.float32
    ) * HEAD ** (-0.5)
    value_gradient = jnp.einsum(
        "hqk,qhd->khd", probs.astype(jnp.bfloat16), grad_mixed, preferred_element_type=jnp.float32
    )
    return (
        query_gradient.astype(jnp.bfloat16),
        grad_k.astype(jnp.bfloat16),
        value_gradient.astype(jnp.bfloat16),
    )


def reduce_adapters(part_a, second_portion):
    return (lax.psum(part_a, ("dp", "tensor")), lax.psum(second_portion, "dp"))


def plain_body(
    activations,
    starts,
    attention_weights,
    projection_weight,
    feedforward_weight,
    output_weight,
    norm_gains,
    norm_biases,
    output_biases,
    query_value_bias,
    feedforward_bias,
    adapter_down_weight,
    adapter_up_weight,
):
    section = lax.axis_index("section")
    first = section == 0
    batches = activations.shape[1]
    own_rows = activations.shape[2]
    width = activations.shape[3]
    head_cols = projection_weight.shape[1]
    local_heads = head_cols // HEAD
    shaped = (-1, SEQ_LEN, local_heads, HEAD)
    w_cat = jnp.concatenate(
        [attention_weights[0, 0], attention_weights[0, 1], attention_weights[0, 2]], axis=1
    )
    stacked_down_maps = jnp.concatenate(
        [adapter_down_weight[0, 0], adapter_down_weight[0, 1]], axis=1
    )

    def forward_relay(rows, group_starts):
        normalized_rows = layer_norm(rows, norm_gains[0, 0], norm_biases[0, 0]).astype(jnp.bfloat16)
        gathered = lax.all_gather(normalized_rows, "tensor", axis=0, tiled=True)
        joined = jnp.dot(gathered, w_cat, preferred_element_type=jnp.float32)
        apply_adapter = jnp.dot(
            gathered, stacked_down_maps, preferred_element_type=jnp.float32
        ).astype(jnp.bfloat16)
        query_rows = (
            joined[:, :head_cols]
            + query_value_bias[0, 0]
            + adapter_scale
            * jnp.dot(
                apply_adapter[:, :ADAPTER_RANK],
                adapter_up_weight[0, 0],
                preferred_element_type=jnp.float32,
            )
        ).astype(jnp.bfloat16)
        keys = joined[:, head_cols : 2 * head_cols].astype(jnp.bfloat16)
        value_rows = (
            joined[:, 2 * head_cols :]
            + query_value_bias[0, 1]
            + adapter_scale
            * jnp.dot(
                apply_adapter[:, ADAPTER_RANK:],
                adapter_up_weight[0, 1],
                preferred_element_type=jnp.float32,
            )
        ).astype(jnp.bfloat16)
        mixed, log_totals = lax.map(
            attend,
            (
                query_rows.reshape(shaped),
                keys.reshape(shaped),
                value_rows.reshape(shaped),
                group_starts,
            ),
        )
        mixed = mixed.reshape(-1, head_cols)
        middle = (
            rows
            + lax.psum_scatter(
                jnp.dot(mixed, projection_weight[0], preferred_element_type=jnp.float32),
                "tensor",
                scatter_dimension=0,
                tiled=True,
            )
            + output_biases[0, 0]
        )
        normed_two = layer_norm(middle, norm_gains[0, 1], norm_biases[0, 1]).astype(jnp.bfloat16)
        hidden = (
            jnp.dot(
                lax.all_gather(normed_two, "tensor", axis=0, tiled=True),
                feedforward_weight[0],
                preferred_element_type=jnp.float32,
            )
            + feedforward_bias[0]
        )
        active = gelu_tanh(hidden).astype(jnp.bfloat16)
        output = (
            middle
            + lax.psum_scatter(
                jnp.dot(active, output_weight[0], preferred_element_type=jnp.float32).astype(
                    jnp.bfloat16
                ),
                "tensor",
                scatter_dimension=0,
                tiled=True,
            ).astype(jnp.float32)
            + output_biases[0, 1]
        )
        return (
            output,
            (
                rows,
                middle,
                gathered,
                apply_adapter,
                query_rows,
                keys,
                value_rows,
                log_totals,
                hidden,
            ),
        )

    def backward_relay(grad_rows, cache, group_starts):
        rows, middle, gathered, apply_adapter, query_rows, keys, value_rows, log_totals, hidden = (
            cache
        )
        grad_active = contract_axes(
            lax.all_gather(grad_rows.astype(jnp.bfloat16), "tensor", axis=0, tiled=True),
            output_weight[0],
            1,
            1,
        )
        _, gelu_back = jax.vjp(gelu_tanh, hidden)
        grad_hidden = gelu_back(grad_active)[0].astype(jnp.bfloat16)
        grad_normed_two = lax.psum_scatter(
            contract_axes(grad_hidden, feedforward_weight[0], 1, 1).astype(jnp.bfloat16),
            "tensor",
            scatter_dimension=0,
            tiled=True,
        ).astype(jnp.float32)
        _, norm_two_back = jax.vjp(
            lambda inner_rows: layer_norm(inner_rows, norm_gains[0, 1], norm_biases[0, 1]), middle
        )
        grad_middle = grad_rows + norm_two_back(grad_normed_two)[0]
        grad_mixed = contract_axes(
            lax.all_gather(grad_middle.astype(jnp.bfloat16), "tensor", axis=0, tiled=True),
            projection_weight[0],
            1,
            1,
        ).astype(jnp.bfloat16)
        query_gradient, grad_k, value_gradient = lax.map(
            attend_back,
            (
                query_rows.reshape(shaped),
                keys.reshape(shaped),
                value_rows.reshape(shaped),
                group_starts,
                log_totals,
                grad_mixed.reshape(shaped),
            ),
        )
        query_gradient = query_gradient.reshape(-1, head_cols)
        grad_k = grad_k.reshape(-1, head_cols)
        value_gradient = value_gradient.reshape(-1, head_cols)
        grad_low = jnp.concatenate(
            [
                adapter_scale * contract_axes(query_gradient, adapter_up_weight[0, 0], 1, 1),
                adapter_scale * contract_axes(value_gradient, adapter_up_weight[0, 1], 1, 1),
            ],
            axis=1,
        ).astype(jnp.bfloat16)
        grad_joined = jnp.concatenate([query_gradient, grad_k, value_gradient], axis=1)
        grad_normed = lax.psum_scatter(
            (
                contract_axes(grad_joined, w_cat, 1, 1)
                + contract_axes(grad_low, stacked_down_maps, 1, 1)
            ).astype(jnp.bfloat16),
            "tensor",
            scatter_dimension=0,
            tiled=True,
        ).astype(jnp.float32)
        _, norm_back = jax.vjp(
            lambda inner_rows: layer_norm(inner_rows, norm_gains[0, 0], norm_biases[0, 0]), rows
        )
        grad_in = grad_middle + norm_back(grad_normed)[0]
        grad_down = contract_axes(gathered, grad_low, 0, 0)
        part_a = jnp.stack([grad_down[:, :ADAPTER_RANK], grad_down[:, ADAPTER_RANK:]])
        second_portion = adapter_scale * jnp.stack(
            [
                contract_axes(apply_adapter[:, :ADAPTER_RANK], query_gradient, 0, 0),
                contract_axes(apply_adapter[:, ADAPTER_RANK:], value_gradient, 0, 0),
            ]
        )
        return (grad_in, part_a, second_portion)

    received = jnp.zeros((own_rows, width), jnp.bfloat16)
    finals = []
    stored = []
    for tick in range(batches + 1):
        batch_index = jnp.clip(tick - section, 0, batches - 1)
        own = lax.dynamic_index_in_dim(activations[0], batch_index, 0, keepdims=False)
        rows = jnp.where(first, own, received).astype(jnp.float32)
        group_starts = lax.dynamic_index_in_dim(starts, batch_index, 0, keepdims=False)
        output, cache = forward_relay(rows, group_starts)
        finals.append(output)
        stored.append(rows)
        if tick < batches:
            received = from_behind(output.astype(jnp.bfloat16), "section", 1)
    stacked = jax.tree.map(lambda *items: jnp.stack(items), *stored)
    returned = jnp.zeros((own_rows, width), jnp.bfloat16)
    totals_a = jnp.zeros((2, width, ADAPTER_RANK), jnp.float32)
    totals_b = jnp.zeros((2, ADAPTER_RANK, head_cols), jnp.float32)
    grads_in = []
    for tick in range(batches + 1):
        position = tick - 1 + section
        batch_index = jnp.clip(position, 0, batches - 1)
        valid = ((position >= 0) & (position < batches)).astype(jnp.float32)
        own = lax.dynamic_index_in_dim(activations[0], batch_index, 0, keepdims=False)
        grad_rows = jnp.where(first, returned, own).astype(jnp.float32) * valid
        group_starts = lax.dynamic_index_in_dim(starts, batch_index, 0, keepdims=False)
        slot_index = jnp.clip(tick - 1 + 2 * section, 0, batches)
        picked = lax.dynamic_index_in_dim(stacked, slot_index, 0, keepdims=False)
        _, cache = forward_relay(picked, group_starts)
        grad_in, part_a, second_portion = backward_relay(grad_rows, cache, group_starts)
        grads_in.append(grad_in)
        if tick < batches:
            returned = from_behind(grad_in.astype(jnp.bfloat16), "section", -1)
        part_a, second_portion = reduce_adapters(part_a, second_portion)
        totals_a = totals_a + part_a
        totals_b = totals_b + second_portion
    combined = jnp.stack(
        [jnp.where(first, grads_in[index + 1], finals[index + 1]) for index in range(batches)]
    )
    return (combined[None], totals_a[None], totals_b[None])


LOW = 2 * ADAPTER_RANK
VMEM_SPACE = pl.BlockSpec(memory_space=pltpu.VMEM)
SMEM_SPACE = pl.BlockSpec(memory_space=pltpu.SMEM)
HBM_SPACE = pl.BlockSpec(memory_space=pltpu.HBM)
BLOCK = 256
CHUNK = 2 * BLOCK


def send(block, route):
    pairs = []
    for s in range(2):
        for t in range(4):
            to = route(s, t)
            if to is not None:
                pairs.append((s * 4 + t, to[0] * 4 + to[1]))
    return lax.ppermute(block, ("section", "tensor"), pairs)


def other_core(block):
    return send(block, lambda s, t: (1 - s, t))


def x_swap(block):
    return send(block, lambda s, t: (s, t ^ 1))


def y_swap(block):
    return send(block, lambda s, t: (s, t ^ 2))


def after(value, *others):
    return lax.optimization_barrier((value, others))[0]


def cross_send(block, source=0):
    return send(block, lambda s, t: (t >> 1, t ^ 2) if s == source else None)


def collect(target, same_chip, cross_chip):
    return (
        send(same_chip, lambda s, t: (target, t) if s == t & 1 and s != target else None),
        send(cross_chip, lambda s, t: (target, t ^ 2) if s == t & 1 else None),
    )


def mm(left, right):
    return jnp.dot(left, right, preferred_element_type=jnp.float32)


def mm_nt(left, right):
    return contract_axes(left, right, 1, 1)


def norm_back(rows, gain, grad):
    mean = jnp.mean(rows, axis=-1, keepdims=True)
    centered = rows - mean
    scale = lax.rsqrt(jnp.mean(centered * centered, axis=-1, keepdims=True) + 1e-05)
    unit = centered * scale
    scaled = grad * gain
    return scale * (
        scaled
        - jnp.mean(scaled, axis=-1, keepdims=True)
        - unit * jnp.mean(scaled * unit, axis=-1, keepdims=True)
    )


def gelu_both(value):
    square = value * value
    bent = jnp.tanh(0.7978845608028654 * value * (1.0 + 0.044715 * square))
    half = 0.5 * (1.0 + bent)
    slope = half + 0.5 * value * (1.0 - bent * bent) * (
        0.7978845608028654 * (1.0 + 3.0 * 0.044715 * square)
    )
    return value * half, slope


def cost(flops, read):
    return pl.CostEstimate(flops=1000, bytes_accessed=1000, transcendentals=0)


def kernel_params(mib):
    return pltpu.CompilerParams(vmem_limit_bytes=mib * 1024 * 1024)


def position_mask(meta, query_block, key_block):
    shape = (BLOCK, BLOCK)
    key_pos = key_block * BLOCK + lax.broadcasted_iota(jnp.int32, shape, 0)
    query_pos = query_block * BLOCK + lax.broadcasted_iota(jnp.int32, (1, BLOCK), 1)
    low = jnp.zeros((1, BLOCK), jnp.int32)
    for c in range(4):
        first = meta[4 + c]
        low = jnp.where(first <= query_pos, jnp.maximum(low, first), low)
    valid = key_pos >= low
    if query_block == key_block:
        valid = valid & (key_pos <= query_pos)
    return valid


def head_lanes(half):
    return (lax.broadcasted_iota(jnp.int32, (1, 2 * HEAD), 1) // HEAD) == half


def start_pick(choices, target, sem):
    for condition, source in choices:

        @pl.when(condition)
        def _(source=source):
            pltpu.make_async_copy(source, target, sem).start()


def load_qkv_weight(layer, meta, pieces, w_buf, sem):
    own, other, lead, trail = pieces
    s, y, w = meta[0], meta[2], meta[8]
    start_pick(
        (((s == y) & (s == layer), own), ((s == y) & (s != layer), other)), w_buf, sem
    )

    @pl.when(s != y)
    def _():
        for part, side in ((lead, w), (trail, 1 - w)):
            pltpu.make_async_copy(part, w_buf.at[pl.ds(2 * side, 2)], sem).start()

    return pltpu.make_async_copy(own, w_buf, sem)


def half_rows(core):
    return pl.ds(pl.multiple_of(core * BLOCK, BLOCK), BLOCK)


def lay_out(meta, own, near, target):
    s = meta[0]
    target[half_rows(s), :] = own[...]
    target[half_rows(1 - s), :] = near[...]


def share_out(meta, source, keep, give):
    s = meta[0]
    keep[...] = source[half_rows(s), :]
    give[...] = source[half_rows(1 - s), :]


def attend_kernel(layer, chunk, meta, shared, varied, own, near, *rest):
    before, rest = rest[: 2 * chunk], rest[2 * chunk :]
    q_out, k_out, v_out, lse_out, mixed_out, keep, give = rest[4:11]
    (
        n_buf, w_buf, score_buf, vt_buf, q_ref, k_ref, v_ref, lse_ref, mixed_ref, sem, out_sems
    ) = rest[11:]
    loaded = load_qkv_weight(layer, meta, rest[:4], w_buf, sem)
    down = shared[layer, 8:16, :].astype(jnp.bfloat16)
    bias = varied[layer, 1:2, :]
    up = varied[layer, 8:16, 0:512].astype(jnp.bfloat16)
    lay_out(meta, own, near, n_buf)
    keys = [k_ref] if chunk == 0 else [before[0], k_ref]
    if chunk == 1:
        for b in range(2):
            span = slice(b * BLOCK, (b + 1) * BLOCK)
            vt_buf[:, span] = before[1][span, :].T
    loaded.wait()
    normed = n_buf[...]
    low = mm_nt(normed, down).astype(jnp.bfloat16)
    lifted = adapter_scale * mm(low, up)
    q_ref[...] = (mm(normed, w_buf[0]) + bias[:, 0:256] + lifted[:, 0:256]).astype(jnp.bfloat16)
    k_ref[...] = mm(normed, w_buf[1]).astype(jnp.bfloat16)
    v_ref[...] = (mm(normed, w_buf[2]) + bias[:, 256:512] + lifted[:, 256:512]).astype(jnp.bfloat16)
    saved = [
        pltpu.make_async_copy(source, target, out_sems.at[i])
        for i, (source, target) in enumerate(
            (
                (q_ref, q_out), (k_ref, k_out), (v_ref, v_out), (lse_ref, lse_out),
                (mixed_ref, mixed_out),
            )
        )
    ]
    for copy in saved[:3]:
        copy.start()
    for b in range(2):
        span = slice(b * BLOCK, (b + 1) * BLOCK)
        vt_buf[:, chunk * CHUNK + b * BLOCK : chunk * CHUNK + (b + 1) * BLOCK] = v_ref[span, :].T

    def one_head(head, carry):
        lanes = pl.ds(pl.multiple_of((head // 2) * 128, 128), 128)
        chosen = head_lanes(head % 2)
        deep = pl.ds(pl.multiple_of(head * HEAD, HEAD), HEAD)
        for i in range(2):
            span = slice(i * BLOCK, (i + 1) * BLOCK)
            place = 2 * chunk + i
            query = jnp.where(chosen, q_ref[span, lanes] * HEAD ** (-0.5), 0.0).astype(jnp.bfloat16)
            top = jnp.full((1, BLOCK), -1e30, jnp.float32)
            for j in range(place + 1):
                rows = slice((j % 2) * BLOCK, (j % 2 + 1) * BLOCK)
                scores = mm_nt(keys[j // 2][rows, lanes], query)
                scores = jnp.where(position_mask(meta, place, j), scores, -1e30)
                score_buf[j] = scores
                top = jnp.maximum(top, jnp.max(scores, axis=0, keepdims=True))
            total = jnp.zeros((1, BLOCK), jnp.float32)
            mixed = jnp.zeros((HEAD, BLOCK), jnp.float32)
            for j in range(place + 1):
                weights = jnp.exp(score_buf[j] - top)
                total = total + jnp.sum(weights, axis=0, keepdims=True)
                mixed = mixed + mm(
                    vt_buf[deep, j * BLOCK : (j + 1) * BLOCK], weights.astype(jnp.bfloat16)
                )
            mixed_ref[deep, span] = mixed / total
            lse_ref[pl.ds(head, 1), span] = top + jnp.log(total)
        return carry

    lax.fori_loop(0, 4, one_head, 0)
    for copy in saved[3:]:
        copy.start()
    for b in range(2):
        span = slice(b * BLOCK, (b + 1) * BLOCK)
        n_buf[span, :] = mm_nt(
            mixed_ref[:, span].T.astype(jnp.bfloat16), w_buf[3]
        ).astype(jnp.bfloat16)
    share_out(meta, n_buf, keep, give)
    for copy in saved:
        copy.wait()


def attend_call(layer, chunk, meta, blocks, before, shared, varied, weight):
    bf, f32 = jnp.bfloat16, jnp.float32
    wide = jax.ShapeDtypeStruct((CHUNK, 256), bf)
    piece = jax.ShapeDtypeStruct((BLOCK, 1024), bf)
    *saved, keep, give = pl.pallas_call(
        functools.partial(attend_kernel, layer, chunk),
        in_specs=[SMEM_SPACE] + [VMEM_SPACE] * (4 + 2 * chunk) + [HBM_SPACE] * 4,
        out_specs=[HBM_SPACE] * 5 + [VMEM_SPACE] * 2,
        out_shape=[wide, wide, wide, jax.ShapeDtypeStruct((8, CHUNK), f32),
                   jax.ShapeDtypeStruct((256, CHUNK), f32), piece, piece],
        scratch_shapes=[
            pltpu.VMEM((CHUNK, 1024), bf),
            pltpu.VMEM((4, 1024, 256), bf),
            pltpu.VMEM((2 + 2 * chunk, BLOCK, BLOCK), f32),
            pltpu.VMEM((256, CHUNK * (1 + chunk)), bf),
            pltpu.VMEM((CHUNK, 256), bf),
            pltpu.VMEM((CHUNK, 256), bf),
            pltpu.VMEM((CHUNK, 256), bf),
            pltpu.VMEM((8, CHUNK), f32),
            pltpu.VMEM((256, CHUNK), f32),
            pltpu.SemaphoreType.DMA,
            pltpu.SemaphoreType.DMA((5,)),
        ],
        compiler_params=kernel_params(24),
        cost_estimate=cost(3.5e9, 8e6),
        name="attention_forward_%d" % chunk,
    )(meta, shared, varied, *blocks, *(before if chunk else ()), *weight)
    return saved, keep, give


def attend_back_kernel(layer, chunk, meta, shared, varied, n_own, n_near, g_own, g_near, *rest):
    q_ref, lse_ref, mixed_ref = rest[:3]
    keys, values = rest[3 : 4 + chunk], rest[4 + chunk : 5 + 2 * chunk]
    rest = rest[5 + 2 * chunk :]
    if chunk == 0:
        dk_in, dv_in, down_in, up_in = rest[:4]
        keep, give, down_ref, up_ref = rest[8:12]
        weight, scratch = rest[4:8], rest[12:]
    else:
        keep, give, down_ref, up_ref, dk_out, dv_out = rest[4:10]
        weight, scratch = rest[:4], rest[10:]
    (
        n_buf, g_buf, w_buf, kt_buf, do_buf, delta_buf, dqt_buf, dk_buf, dv_buf, dq_buf, sem
    ) = scratch
    loaded = load_qkv_weight(layer, meta, weight, w_buf, sem)
    lay_out(meta, g_own, g_near, g_buf)
    lay_out(meta, n_own, n_near, n_buf)
    for j in range(2 + 2 * chunk):
        rows = slice((j % 2) * BLOCK, (j % 2 + 1) * BLOCK)
        kt_buf[:, j * BLOCK : (j + 1) * BLOCK] = keys[j // 2][rows, :].T
    if chunk == 0:
        dk_buf[...] = dk_in[...]
        dv_buf[...] = dv_in[...]
    else:
        dk_buf[...] = jnp.zeros_like(dk_buf)
        dv_buf[...] = jnp.zeros_like(dv_buf)
    loaded.wait()
    do_buf[...] = mm(g_buf[...], w_buf[3]).astype(jnp.bfloat16)
    for b in range(2):
        span = slice(b * BLOCK, (b + 1) * BLOCK)
        product = do_buf[span, :].astype(jnp.float32).T * mixed_ref[:, span]
        for head in range(4):
            delta_buf[head : head + 1, span] = jnp.sum(
                product[head * HEAD : (head + 1) * HEAD], axis=0, keepdims=True
            )

    def one_head(head, carry):
        lanes = pl.ds(pl.multiple_of((head // 2) * 128, 128), 128)
        chosen = head_lanes(head % 2)
        deep = pl.ds(pl.multiple_of(head * HEAD, HEAD), HEAD)
        for i in range(2):
            span = slice(i * BLOCK, (i + 1) * BLOCK)
            place = 2 * chunk + i
            query = jnp.where(chosen, q_ref[span, lanes] * HEAD ** (-0.5), 0.0).astype(jnp.bfloat16)
            grad_mixed = jnp.where(chosen, do_buf[span, lanes], 0.0).astype(jnp.bfloat16)
            lse = lse_ref[pl.ds(head, 1), span]
            delta = delta_buf[pl.ds(head, 1), span]
            grad_query = jnp.zeros((HEAD, BLOCK), jnp.float32)
            for j in range(place + 1):
                rows = slice((j % 2) * BLOCK, (j % 2 + 1) * BLOCK)
                all_rows = slice(j * BLOCK, (j + 1) * BLOCK)
                scores = mm_nt(keys[j // 2][rows, lanes], query)
                probs = jnp.where(position_mask(meta, place, j), jnp.exp(scores - lse), 0.0)
                grad_probs = mm_nt(values[j // 2][rows, lanes], grad_mixed)
                grad_scores = (probs * (grad_probs - delta)).astype(jnp.bfloat16)
                dv_buf[all_rows, lanes] += mm(probs.astype(jnp.bfloat16), grad_mixed)
                dk_buf[all_rows, lanes] += mm(grad_scores, query)
                grad_query = grad_query + mm(kt_buf[deep, all_rows], grad_scores)
            dqt_buf[deep, span] = grad_query * HEAD ** (-0.5)
        return carry

    lax.fori_loop(0, 4, one_head, 0)
    down = shared[layer, 8:16, :].astype(jnp.bfloat16)
    up = varied[layer, 8:16, 0:512].astype(jnp.bfloat16)
    for b in range(2):
        span = slice(b * BLOCK, (b + 1) * BLOCK)
        dq_buf[span, :] = dqt_buf[:, span].T.astype(jnp.bfloat16)
    done = slice(chunk * CHUNK, (chunk + 1) * CHUNK)
    normed = n_buf[...]
    grad_q = dq_buf[...]
    grad_k = dk_buf[done, :].astype(jnp.bfloat16)
    grad_v = dv_buf[done, :].astype(jnp.bfloat16)
    both = jnp.concatenate([grad_q, grad_v], axis=1)
    low_grad = (adapter_scale * mm_nt(both, up)).astype(jnp.bfloat16)
    low_grad_t = (adapter_scale * mm_nt(up, both)).astype(jnp.bfloat16)
    low_t = mm_nt(down, normed).astype(jnp.bfloat16)
    g_buf[...] = (
        mm_nt(grad_q, w_buf[0]) + mm_nt(grad_k, w_buf[1]) + mm_nt(grad_v, w_buf[2])
        + mm(low_grad, down)
    ).astype(jnp.bfloat16)
    share_out(meta, g_buf, keep, give)
    total_down = mm(low_grad_t, normed)
    total_up = adapter_scale * mm(low_t, both)
    if chunk == 0:
        total_down = total_down + down_in[...]
        total_up = total_up + up_in[...]
    else:
        dk_out[...] = dk_buf[0:CHUNK, :]
        dv_out[...] = dv_buf[0:CHUNK, :]
    down_ref[...] = total_down
    up_ref[...] = total_up


def attend_back_call(layer, chunk, meta, blocks, grads, saved, carried, shared, varied, weight):
    bf, f32 = jnp.bfloat16, jnp.float32
    piece = jax.ShapeDtypeStruct((BLOCK, 1024), bf)
    tall = jax.ShapeDtypeStruct((CHUNK, 256), f32)
    spans = CHUNK * (1 + chunk)
    q, _, _, lse, mixed = saved[chunk]
    keys = [one[1] for one in saved[: chunk + 1]]
    values = [one[2] for one in saved[: chunk + 1]]
    inputs = (shared, varied, *blocks, *grads, q, lse, mixed, *keys, *values, *carried)
    return pl.pallas_call(
        functools.partial(attend_back_kernel, layer, chunk),
        in_specs=[SMEM_SPACE] + [VMEM_SPACE] * len(inputs) + [HBM_SPACE] * 4,
        out_specs=[VMEM_SPACE] * (4 + 2 * chunk),
        out_shape=[piece, piece, jax.ShapeDtypeStruct((LOW, 1024), f32),
                   jax.ShapeDtypeStruct((LOW, 512), f32)] + [tall] * (2 * chunk),
        scratch_shapes=[
            pltpu.VMEM((CHUNK, 1024), bf),
            pltpu.VMEM((CHUNK, 1024), bf),
            pltpu.VMEM((4, 1024, 256), bf),
            pltpu.VMEM((256, spans), bf),
            pltpu.VMEM((CHUNK, 256), bf),
            pltpu.VMEM((8, CHUNK), f32),
            pltpu.VMEM((256, CHUNK), f32),
            pltpu.VMEM((spans, 256), f32),
            pltpu.VMEM((spans, 256), f32),
            pltpu.VMEM((CHUNK, 256), bf),
            pltpu.SemaphoreType.DMA,
        ],
        compiler_params=kernel_params(24),
        cost_estimate=cost(6e9, 12e6),
        name="attention_backward_%d" % chunk,
    )(meta, *inputs, *weight)


def summed(passed, far):
    return passed[...].astype(jnp.float32) + far[...].astype(jnp.float32)


def rows_middle_kernel(layer, h_ref, passed, far, shared, middle_ref, normed_ref):
    middle = h_ref[...].astype(jnp.float32) + summed(passed, far) + shared[layer, 4:5, :]
    middle_ref[...] = middle
    normed_ref[...] = layer_norm(middle, shared[layer, 1:2, :], shared[layer, 3:4, :]).astype(
        jnp.bfloat16
    )


def load_units(layer, meta, pieces, w1, w2, sems):
    own, other, (lead, trail) = pieces[0:2], pieces[2:4], pieces[4:6]
    s, y, w = meta[0], meta[2], meta[8]
    copies = []
    for m, matrix in enumerate((w1, w2)):
        start_pick(
            (
                ((s == y) & (s == layer), own[m]),
                ((s == y) & (s != layer), other[m]),
                ((s != y) & (w == m), lead),
                ((s != y) & (w != m), trail),
            ),
            matrix,
            sems.at[m],
        )
        copies.append(pltpu.make_async_copy(own[m], matrix, sems.at[m]))
    return copies


def stack_rows(blocks, target):
    for i, block in enumerate(blocks):
        target[i * BLOCK : (i + 1) * BLOCK, :] = block[...]


def halve(total, keep, give):
    keep[...] = total[:BLOCK].astype(jnp.bfloat16)
    give[...] = total[BLOCK:].astype(jnp.bfloat16)


def units_kernel(layer, meta, n0, n1, bias, *rest):
    keep, give, slope_out, w1, w2, sems, n_buf, slope_buf, out_sem = rest[6:]
    waits = load_units(layer, meta, rest[:6], w1, w2, sems)
    stack_rows((n0, n1), n_buf)
    waits[0].wait()
    active, slope = gelu_both(mm(n_buf[...], w1[...]) + bias[layer, 0:1, :])
    slope_buf[...] = slope.astype(jnp.bfloat16)
    saving = pltpu.make_async_copy(slope_buf, slope_out, out_sem)
    saving.start()
    waits[1].wait()
    halve(mm(active.astype(jnp.bfloat16), w2[...]), keep, give)
    saving.wait()


def units_turn_kernel(layer, meta, n0, n1, g0, g1, bias, *rest):
    keep, give, out_keep, out_give, w1, w2, sems, n_buf, g_buf = rest[6:]
    waits = load_units(layer, meta, rest[:6], w1, w2, sems)
    stack_rows((n0, n1), n_buf)
    stack_rows((g0, g1), g_buf)
    for copy in waits:
        copy.wait()
    active, slope = gelu_both(mm(n_buf[...], w1[...]) + bias[layer, 0:1, :])
    grad_hidden = (mm_nt(g_buf[...], w2[...]) * slope).astype(jnp.bfloat16)
    halve(mm_nt(grad_hidden, w1[...]), keep, give)
    halve(mm(active.astype(jnp.bfloat16), w2[...]), out_keep, out_give)


def units_back_kernel(layer, meta, g0, g1, slope_in, *rest):
    keep, give, w1, w2, sems, g_buf, slope_buf, in_sem = rest[6:]
    waits = load_units(layer, meta, rest[:6], w1, w2, sems)
    fetch = pltpu.make_async_copy(slope_in, slope_buf, in_sem)
    fetch.start()
    stack_rows((g0, g1), g_buf)
    waits[1].wait()
    fetch.wait()
    grad = (mm_nt(g_buf[...], w2[...]) * slope_buf[...].astype(jnp.float32)).astype(jnp.bfloat16)
    waits[0].wait()
    halve(mm_nt(grad, w1[...]), keep, give)


def rows_first_kernel(meta, mine, crossed, far_mine, far_crossed, shared, *outs):
    holder = meta[0] == meta[1]
    upper = meta[2] == 0
    first = jnp.where(holder, mine[...], far_mine[...])
    second = jnp.where(holder, crossed[...], far_crossed[...])
    for c, (one, other) in enumerate(((first, second), (second, first))):
        rows = jnp.where(upper, one, other)
        outs[c][...] = rows
        outs[2 + c][...] = layer_norm(
            rows.astype(jnp.float32), shared[0, 0:1, :], shared[0, 2:3, :]
        ).astype(jnp.bfloat16)


def rows_next_kernel(middle, passed, far, shared, between_ref, normed_ref):
    between = (middle[...] + summed(passed, far) + shared[0, 5:6, :]).astype(jnp.bfloat16)
    between_ref[...] = between
    normed_ref[...] = layer_norm(
        between.astype(jnp.float32), shared[1, 0:1, :], shared[1, 2:3, :]
    ).astype(jnp.bfloat16)


def rows_turn_kernel(layer, middle, g_ref, passed, far, shared, grad_ref, sent_ref):
    grad_middle = g_ref[...].astype(jnp.float32) + norm_back(
        middle[...], shared[layer, 1:2, :], summed(passed, far)
    )
    grad_ref[...] = grad_middle
    sent_ref[...] = grad_middle.astype(jnp.bfloat16)


def rows_before_kernel(gm_ref, passed, far, between_ref, shared, grad_ref):
    grad_rows = gm_ref[...] + norm_back(
        between_ref[...].astype(jnp.float32), shared[1, 0:1, :], summed(passed, far)
    )
    grad_ref[...] = grad_rows.astype(jnp.bfloat16)


def rows_output_kernel(middle, passed, far, shared, wide_ref, narrow_ref):
    total = middle[...] + summed(passed, far) + shared[1, 5:6, :]
    wide_ref[...] = total
    narrow_ref[...] = total.astype(jnp.bfloat16)


def rows_final_kernel(gm_ref, passed, far, h_ref, shared, wide_ref, narrow_ref):
    grad_in = gm_ref[...] + norm_back(
        h_ref[...].astype(jnp.float32), shared[0, 0:1, :], summed(passed, far)
    )
    wide_ref[...] = grad_in
    narrow_ref[...] = grad_in.astype(jnp.bfloat16)


def units_call(kernel, meta, small, saved, weights, outs, saving, scratch, name):
    return pl.pallas_call(
        kernel,
        in_specs=[SMEM_SPACE] + [VMEM_SPACE] * len(small) + [HBM_SPACE] * (len(saved) + len(weights)),
        out_specs=[VMEM_SPACE] * len(outs) + [HBM_SPACE] * len(saving),
        out_shape=[*outs, *saving],
        scratch_shapes=scratch,
        compiler_params=kernel_params(24),
        cost_estimate=cost(2e9, 8e6),
        name=name,
    )(meta, *small, *saved, *weights)


def plain_call(kernel, scalar, small, large, outs, scratch, flops, name):
    specs = [VMEM_SPACE] * len(small) + [HBM_SPACE] * len(large)
    operands = (*small, *large)
    if scalar is not None:
        specs, operands = [SMEM_SPACE] + specs, (scalar, *operands)
    return pl.pallas_call(
        kernel,
        in_specs=specs,
        out_specs=[VMEM_SPACE] * len(outs),
        out_shape=outs,
        scratch_shapes=scratch,
        compiler_params=kernel_params(24),
        cost_estimate=cost(flops, 8e6),
        name=name,
    )(*operands)


def deal_rows(source, slots, section, y):
    same = lax.dynamic_index_in_dim(slots, y, 0, keepdims=False)
    cross = lax.dynamic_index_in_dim(slots, 1 - y, 0, keepdims=False)
    moved = send(same, lambda s, t: (t & 1, t) if s == source and s != t & 1 else None)
    crossed = send(cross, lambda s, t: (t & 1, t ^ 2) if s == source else None)
    mine = jnp.where(section == source, same, moved)
    return mine, crossed


def to_x(block):
    return send(block, lambda s, t: (s, t ^ 1) if s == t & 1 else None)


def from_x(block):
    return send(block, lambda s, t: (s, t ^ 1) if s != t & 1 else None)


def z_swap(block):
    size = lax.axis_size("dp")
    pairs = [
        ((s * size + z) * 4 + t, (s * size + (z ^ 1)) * 4 + t)
        for s in range(2) for z in range(size) for t in range(4) if s != t >> 1
    ]
    return lax.ppermute(block, ("section", "dp", "tensor"), pairs)


def chip_sum(keep, give, last, swap=x_swap):
    take = other_core(after(give, last))
    passed = (keep.astype(jnp.float32) + take.astype(jnp.float32)).astype(jnp.bfloat16)
    return passed, swap(passed)


def total_over_z(downs, ups):
    both = jnp.concatenate([jnp.concatenate(downs), jnp.concatenate(ups)], axis=1)
    size = lax.axis_size("dp")
    step = 1
    while step < size:
        both = both + lax.ppermute(both, "dp", [(i, i ^ step) for i in range(size)])
        step *= 2
    return both


def total_over_cores(both, section, y):
    both = both + y_swap(both)
    moved = other_core(both)
    down = both[:, :1024] + moved[:, :1024]
    down = jnp.where(section == 0, down[:LOW], down[LOW:])
    up = jnp.where(section == y, both[:, 1024:], moved[:, 1024:])
    return down + x_swap(down), jnp.where(section == 0, up[:LOW], up[LOW:])


def relay_body(
    activations, starts, attention_weights, projection_weight, feedforward_weight, output_weight,
    norm_gains, norm_biases, output_biases, query_value_bias, feedforward_bias,
    adapter_down_weight, adapter_up_weight,
):
    bf, f32 = jnp.bfloat16, jnp.float32
    section = lax.axis_index("section")
    place = lax.axis_index("tensor")
    y, x = place // 2, place % 2
    first = section == 0

    mine, crossed = deal_rows(0, activations[0], section, y)
    down_rows = adapter_down_weight[0].astype(f32).transpose(0, 2, 1).reshape(LOW, 1024)
    up0 = adapter_up_weight[0, 0].astype(f32)
    up1 = adapter_up_weight[0, 1].astype(f32)
    zero = jnp.zeros((ADAPTER_RANK, 256), f32)
    common = jnp.concatenate(
        [norm_gains[0], norm_biases[0], output_biases[0], jnp.zeros((2, 1024), f32), down_rows]
    )
    own_part = jnp.concatenate(
        [
            feedforward_bias,
            jnp.pad(query_value_bias[0].reshape(1, 512), ((0, 0), (0, 512))),
            jnp.zeros((6, 1024), f32),
            jnp.concatenate([up0, zero, jnp.zeros((ADAPTER_RANK, 512), f32)], axis=1),
            jnp.concatenate([zero, up1, jnp.zeros((ADAPTER_RANK, 512), f32)], axis=1),
        ]
    )
    partner = other_core(common)
    partner_part = other_core(own_part)
    parts = jnp.where(
        first, jnp.stack([own_part, partner_part]), jnp.stack([partner_part, own_part])
    )
    near_varied = jnp.where(section == y, parts, y_swap(parts))
    shared = jnp.where(first, jnp.stack([common, partner]), jnp.stack([partner, common]))
    meta = jnp.concatenate(
        [
            jnp.stack([section, x, y, place]).astype(jnp.int32),
            lax.dynamic_index_in_dim(starts, y, 0, keepdims=False).reshape(4),
            (lax.axis_index("dp") % 2).astype(jnp.int32)[None],
        ]
    )
    even = lax.axis_index("dp") % 2 == 0
    own_a = jnp.concatenate([attention_weights[0], projection_weight[0].T[None]])
    w1_own, w2_own = feedforward_weight[0], output_weight[0]
    other_a = other_core(own_a)
    mine, crossed, shared = lax.optimization_barrier((mine, crossed, shared))
    lead_a0 = cross_send(after(jnp.where(even, own_a[:2], own_a[2:]), crossed, near_varied))
    far_mine, far_crossed = to_x(mine), to_x(crossed)
    g_mine, g_crossed = deal_rows(1, after(activations[0], crossed), section, y)
    far_crossed, g_mine, g_crossed = lax.optimization_barrier((far_crossed, g_mine, g_crossed))
    trail_a0 = z_swap(after(lead_a0, far_mine, far_crossed))

    sheet = jax.ShapeDtypeStruct((BLOCK, 1024), f32)
    thin = jax.ShapeDtypeStruct((BLOCK, 1024), bf)
    slope_shape = jax.ShapeDtypeStruct((CHUNK, 1024), bf)
    matrices = [
        pltpu.VMEM((1024, 1024), bf), pltpu.VMEM((1024, 1024), bf), pltpu.SemaphoreType.DMA((2,))
    ]
    group = pltpu.VMEM((CHUNK, 1024), bf)

    def small(kernel, *operands, outs, name):
        return plain_call(kernel, None, operands, (), outs, [], 1e7, name)

    def attend(layer, chunk, normed, before, weight, near=None):
        near = other_core(normed) if near is None else near
        return attend_call(
            layer, chunk, meta, (normed, near), before, shared, near_varied, weight
        )

    def units(layer, normed, weight):
        return units_call(
            functools.partial(units_kernel, layer), meta, (normed, other_core(normed), near_varied),
            (), weight, [thin, thin], [slope_shape],
            [*matrices, group, group, pltpu.SemaphoreType.DMA], "units",
        )

    def units_turn(layer, normed, grad, near_grad, weight):
        return units_call(
            functools.partial(units_turn_kernel, layer), meta,
            (normed, other_core(normed), grad, near_grad, near_varied), (), weight,
            [thin] * 4, [], [*matrices, group, group], "units_turn",
        )

    def units_back(layer, grad, slope, weight):
        return units_call(
            functools.partial(units_back_kernel, layer), meta, (grad, other_core(grad)), (slope,),
            weight, [thin, thin], [], [*matrices, group, group, pltpu.SemaphoreType.DMA],
            "units_back",
        )

    def middle(layer, rows, sums):
        return small(
            functools.partial(rows_middle_kernel, layer), rows, *sums, shared, outs=[sheet, thin],
            name="rows_middle",
        )

    def turn(layer, middle_rows, grad, sums):
        return small(
            functools.partial(rows_turn_kernel, layer), middle_rows, grad, *sums, shared,
            outs=[sheet, thin], name="rows_turn",
        )

    row0, row1, n0, n1 = plain_call(
        rows_first_kernel, meta, (mine, crossed, far_mine, far_crossed, shared), (), [thin] * 4,
        [], 1e7, "rows_first",
    )
    g_far = [to_x(one) for one in (g_mine, g_crossed)]
    weights_a0 = (own_a, other_a, lead_a0, trail_a0)
    near_n0 = other_core(n0)
    lead_b0 = cross_send(jnp.where(even, *after((w1_own, w2_own), near_n0)))
    n00, n01 = n0, n1
    saved00, keep, give = attend(0, 0, n0, (), weights_a0, near_n0)
    keep, give, g_far = lax.optimization_barrier((keep, give, g_far))
    sum0 = chip_sum(keep, give, lead_a0)
    other_w1, other_w2 = (other_core(after(one, sum0[0])) for one in (w1_own, w2_own))
    trail_b0 = z_swap(after(lead_b0, sum0[0]))
    weights_b0 = (w1_own, w2_own, other_w1, other_w2, lead_b0, trail_b0)
    saved01, keep, give = attend(0, 1, n1, saved00[1:3], weights_a0)
    sum1 = chip_sum(keep, give, sum0[1])
    lead_a1 = cross_send(jnp.where(even, *after((other_a[:2], other_a[2:]), sum0[0])))
    middle00, n0 = middle(0, row0, sum0)
    keep, give, slope0 = units(0, n0, weights_b0)
    sum2 = chip_sum(keep, give, sum1[1])
    sum1, lead_a1 = lax.optimization_barrier((sum1, lead_a1))
    trail_a1 = z_swap(lead_a1)
    lead_b1 = cross_send(jnp.where(even, *after((other_w1, other_w2), lead_a1)))
    middle01, n1 = middle(0, row1, sum1)
    keep, give, slope1 = units(0, n1, weights_b0)
    sum3 = chip_sum(keep, give, sum2[1])
    weights_a1 = (own_a, other_a, lead_a1, trail_a1)
    between0, n10 = small(rows_next_kernel, middle00, *sum2, shared, outs=[thin, thin], name="rows_next")
    saved10, keep, give = attend(1, 0, n10, (), weights_a1)
    sum4 = chip_sum(keep, give, sum3[1])
    sum3, lead_b1 = lax.optimization_barrier((sum3, lead_b1))
    trail_b1 = z_swap(lead_b1)
    weights_b1 = (w1_own, w2_own, other_w1, other_w2, lead_b1, trail_b1)
    between1, n11 = small(rows_next_kernel, middle01, *sum3, shared, outs=[thin, thin], name="rows_next")
    saved11, keep, give = attend(1, 1, n11, saved10[1:3], weights_a1)
    sum5 = chip_sum(keep, give, sum4[1])
    holder, upper = section == x, y == 0
    mine, crossed = (
        jnp.where(holder, one, two) for one, two in zip((g_mine, g_crossed), after(g_far, sum4[0]))
    )
    grad_outs = (jnp.where(upper, mine, crossed), jnp.where(upper, crossed, mine))
    near_outs = [other_core(one) for one in grad_outs]
    middle10, m0 = middle(1, between0, sum4)
    keep, give, out_keep0, out_give0 = units_turn(1, m0, grad_outs[0], near_outs[0], weights_b1)
    sum6 = chip_sum(keep, give, sum5[1])
    middle11, m1 = middle(1, between1, sum5)
    keep, give, out_keep1, out_give1 = units_turn(1, m1, grad_outs[1], near_outs[1], weights_b1)
    sum7 = chip_sum(keep, give, sum6[1])
    grad_middle10, g0 = turn(1, middle10, grad_outs[0], sum6)
    grad_middle11, g1 = turn(1, middle11, grad_outs[1], sum7)
    keep, give, down1, up1, dk, dv = attend_back_call(
        1, 1, meta, (n11, other_core(n11)), (g1, other_core(g1)), (saved10, saved11), (), shared,
        near_varied, weights_a1,
    )
    out_sums = [
        chip_sum(*after(one, g1), sum7[1], from_x)
        for one in ((out_keep0, out_give0), (out_keep1, out_give1))
    ]
    keep, give, out_sums = lax.optimization_barrier((keep, give, out_sums))
    sum8 = chip_sum(keep, give, sum7[1])
    keep, give, down1, up1 = attend_back_call(
        1, 0, meta, (n10, other_core(n10)), (g0, other_core(g0)), (saved10, saved11),
        (dk, dv, down1, up1), shared, near_varied, weights_a1,
    )
    sum9 = chip_sum(keep, give, sum8[1])
    before1 = small(
        rows_before_kernel, grad_middle11, *sum8, between1, shared, outs=[thin], name="rows_before"
    )[0]
    keep, give = units_back(0, before1, slope1, weights_b0)
    sum10 = chip_sum(keep, give, sum9[1])
    outs = [
        small(rows_output_kernel, one, *after(two, keep), shared, outs=[sheet, thin],
              name="rows_output")
        for one, two in zip((middle10, middle11), out_sums)
    ]
    out_wide = jnp.where(upper, outs[0][0], outs[1][0])
    out_same, out_cross = collect(1, out_wide, jnp.where(upper, outs[1][1], outs[0][1]))
    sum9, out_same, out_cross = lax.optimization_barrier((sum9, out_same, out_cross))
    before0 = small(
        rows_before_kernel, grad_middle10, *sum9, between0, shared, outs=[thin], name="rows_before"
    )[0]
    keep, give = units_back(0, before0, slope0, weights_b0)
    sum11 = chip_sum(keep, give, sum10[1])
    grad_middle01, h1 = turn(0, middle01, before1, sum10)
    keep, give, down0, up0, dk, dv = attend_back_call(
        0, 1, meta, (n01, other_core(n01)), (h1, other_core(h1)), (saved00, saved01), (), shared,
        near_varied, weights_a0,
    )
    sum12 = chip_sum(keep, give, sum11[1], from_x)
    grad_middle00, h0 = turn(0, middle00, before0, sum11)
    keep, give, down0, up0 = attend_back_call(
        0, 0, meta, (n00, other_core(n00)), (h0, other_core(h0)), (saved00, saved01),
        (dk, dv, down0, up0), shared, near_varied, weights_a0,
    )
    sum13 = chip_sum(keep, give, sum12[1], from_x)
    totals = total_over_z((down0, down1), after((up0, up1), sum13[0]))
    sum13, totals = lax.optimization_barrier((sum13, totals))
    ends = [
        small(rows_final_kernel, one, *two, three, shared, outs=[sheet, thin], name="rows_final")
        for one, two, three in ((grad_middle00, sum13, row0), (grad_middle01, sum12, row1))
    ]
    wide = jnp.where(upper, ends[0][0], ends[1][0])
    in_same, in_cross = collect(0, wide, jnp.where(upper, ends[1][1], ends[0][1]))
    grad_down, grad_up = total_over_cores(totals, section, y)
    same = jnp.where(
        first, jnp.where(x == 0, wide, in_same), jnp.where(x == 1, out_wide, out_same)
    )
    cross = jnp.where(first, in_cross, out_cross).astype(f32)
    combined = jnp.where(y == 0, jnp.stack([same, cross]), jnp.stack([cross, same]))
    return (
        combined[None],
        grad_down.reshape(1, 2, ADAPTER_RANK, 1024).transpose(0, 1, 3, 2),
        jnp.stack([grad_up[:ADAPTER_RANK, :256], grad_up[ADAPTER_RANK:, 256:]])[None],
    )


def body(*arrays):
    dp = lax.axis_size("dp")
    known = (
        arrays[0].shape == (1, 2, BLOCK, 1024)
        and lax.axis_size("tensor") == 4
        and lax.axis_size("section") == 2
        and arrays[3].shape == (1, 256, 1024)
        and arrays[5].shape == (1, 1024, 1024)
        and dp & (dp - 1) == 0
    )
    return relay_body(*arrays) if known else plain_body(*arrays)


def solution(mesh):
    placed = (
        P("section", None, ("dp", "tensor"), None),
        P(None, "dp", None),
        P("section", None, None, "tensor"),
        P("section", "tensor", None),
        P("section", None, "tensor"),
        P("section", "tensor", None),
        P("section", None, None),
        P("section", None, None),
        P("section", None, None),
        P("section", None, "tensor"),
        P("section", "tensor"),
        P("section", None, None, None),
        P("section", None, None, "tensor"),
    )
    return jax.shard_map(
        body,
        mesh=mesh,
        in_specs=placed,
        out_specs=(
            P("section", None, ("dp", "tensor"), None),
            P("section", None, None, None),
            P("section", None, None, "tensor"),
        ),
        check_vma=False,
    )
```

```python
import functools

import jax
import jax.numpy as jnp
from jax import lax
from jax.experimental import pallas as pl
from jax.experimental.pallas import tpu as pltpu
from jax.sharding import PartitionSpec as P

HEAD = 64
ADAPTER_RANK = 4
SEQ_LEN = 1024


adapter_scale = 8.0


def from_behind(block, axis, distance):
    devices = range(lax.axis_size(axis))
    route = [(i - distance, i) for i in devices if i - distance in devices]
    return lax.ppermute(block, axis, route)


def contract_axes(left, right, left_dim, right_dim):
    return lax.dot_general(
        left, right, (((left_dim,), (right_dim,)), ((), ())), preferred_element_type=jnp.float32
    )


def layer_norm(rows, gain, shift):
    mean = jnp.mean(rows, axis=-1, keepdims=True)
    centered = rows - mean
    spread = jnp.mean(centered * centered, axis=-1, keepdims=True)
    return centered * lax.rsqrt(spread + 1e-05) * gain + shift


def gelu_tanh(value):
    return (
        0.5
        * value
        * (1.0 + jnp.tanh(0.7978845608028654 * (value + 0.044715 * value * value * value)))
    )


def doc_mask(doc_starts):
    positions = jnp.arange(SEQ_LEN, dtype=jnp.int32)
    labels = jnp.sum((doc_starts[None, :] <= positions[:, None]).astype(jnp.int32), axis=1)
    return (positions[None, :] <= positions[:, None]) & (labels[:, None] == labels[None, :])


def masked_scores(query_rows, keys, doc_starts):
    scores = jnp.einsum(
        "qhd,khd->hqk", query_rows, keys, preferred_element_type=jnp.float32
    ) * HEAD ** (-0.5)
    return jnp.where(doc_mask(doc_starts)[None], scores, -1e30)


def attend(items):
    query_rows, keys, value_rows, doc_starts = items
    scores = masked_scores(query_rows, keys, doc_starts)
    top = jnp.max(scores, axis=-1, keepdims=True)
    weights = jnp.exp(scores - top)
    total = jnp.sum(weights, axis=-1, keepdims=True)
    mixed = jnp.einsum(
        "hqk,khd->qhd",
        (weights / total).astype(jnp.bfloat16),
        value_rows,
        preferred_element_type=jnp.float32,
    )
    return (mixed.astype(jnp.bfloat16), (top + jnp.log(total))[:, :, 0])


def attend_back(items):
    query_rows, keys, value_rows, doc_starts, log_totals, grad_mixed = items
    scores = masked_scores(query_rows, keys, doc_starts)
    probs = jnp.exp(scores - log_totals[:, :, None])
    grad_probs = jnp.einsum(
        "qhd,khd->hqk", grad_mixed, value_rows, preferred_element_type=jnp.float32
    )
    inner = jnp.sum(probs * grad_probs, axis=-1, keepdims=True)
    grad_scores = (probs * (grad_probs - inner)).astype(jnp.bfloat16)
    query_gradient = jnp.einsum(
        "hqk,khd->qhd", grad_scores, keys, preferred_element_type=jnp.float32
    ) * HEAD ** (-0.5)
    grad_k = jnp.einsum(
        "hqk,qhd->khd", grad_scores, query_rows, preferred_element_type=jnp.float32
    ) * HEAD ** (-0.5)
    value_gradient = jnp.einsum(
        "hqk,qhd->khd", probs.astype(jnp.bfloat16), grad_mixed, preferred_element_type=jnp.float32
    )
    return (
        query_gradient.astype(jnp.bfloat16),
        grad_k.astype(jnp.bfloat16),
        value_gradient.astype(jnp.bfloat16),
    )


def reduce_adapters(part_a, second_portion):
    return (lax.psum(part_a, ("dp", "tensor")), lax.psum(second_portion, "dp"))


def plain_body(
    activations,
    starts,
    attention_weights,
    projection_weight,
    feedforward_weight,
    output_weight,
    norm_gains,
    norm_biases,
    output_biases,
    query_value_bias,
    feedforward_bias,
    adapter_down_weight,
    adapter_up_weight,
):
    section = lax.axis_index("section")
    first = section == 0
    batches = activations.shape[1]
    own_rows = activations.shape[2]
    width = activations.shape[3]
    head_cols = projection_weight.shape[1]
    local_heads = head_cols // HEAD
    shaped = (-1, SEQ_LEN, local_heads, HEAD)
    w_cat = jnp.concatenate(
        [attention_weights[0, 0], attention_weights[0, 1], attention_weights[0, 2]], axis=1
    )
    stacked_down_maps = jnp.concatenate(
        [adapter_down_weight[0, 0], adapter_down_weight[0, 1]], axis=1
    )

    def forward_relay(rows, group_starts):
        normalized_rows = layer_norm(rows, norm_gains[0, 0], norm_biases[0, 0]).astype(jnp.bfloat16)
        gathered = lax.all_gather(normalized_rows, "tensor", axis=0, tiled=True)
        joined = jnp.dot(gathered, w_cat, preferred_element_type=jnp.float32)
        apply_adapter = jnp.dot(
            gathered, stacked_down_maps, preferred_element_type=jnp.float32
        ).astype(jnp.bfloat16)
        query_rows = (
            joined[:, :head_cols]
            + query_value_bias[0, 0]
            + adapter_scale
            * jnp.dot(
                apply_adapter[:, :ADAPTER_RANK],
                adapter_up_weight[0, 0],
                preferred_element_type=jnp.float32,
            )
        ).astype(jnp.bfloat16)
        keys = joined[:, head_cols : 2 * head_cols].astype(jnp.bfloat16)
        value_rows = (
            joined[:, 2 * head_cols :]
            + query_value_bias[0, 1]
            + adapter_scale
            * jnp.dot(
                apply_adapter[:, ADAPTER_RANK:],
                adapter_up_weight[0, 1],
                preferred_element_type=jnp.float32,
            )
        ).astype(jnp.bfloat16)
        mixed, log_totals = lax.map(
            attend,
            (
                query_rows.reshape(shaped),
                keys.reshape(shaped),
                value_rows.reshape(shaped),
                group_starts,
            ),
        )
        mixed = mixed.reshape(-1, head_cols)
        middle = (
            rows
            + lax.psum_scatter(
                jnp.dot(mixed, projection_weight[0], preferred_element_type=jnp.float32),
                "tensor",
                scatter_dimension=0,
                tiled=True,
            )
            + output_biases[0, 0]
        )
        normed_two = layer_norm(middle, norm_gains[0, 1], norm_biases[0, 1]).astype(jnp.bfloat16)
        hidden = (
            jnp.dot(
                lax.all_gather(normed_two, "tensor", axis=0, tiled=True),
                feedforward_weight[0],
                preferred_element_type=jnp.float32,
            )
            + feedforward_bias[0]
        )
        active = gelu_tanh(hidden).astype(jnp.bfloat16)
        output = (
            middle
            + lax.psum_scatter(
                jnp.dot(active, output_weight[0], preferred_element_type=jnp.float32).astype(
                    jnp.bfloat16
                ),
                "tensor",
                scatter_dimension=0,
                tiled=True,
            ).astype(jnp.float32)
            + output_biases[0, 1]
        )
        return (
            output,
            (
                rows,
                middle,
                gathered,
                apply_adapter,
                query_rows,
                keys,
                value_rows,
                log_totals,
                hidden,
            ),
        )

    def backward_relay(grad_rows, cache, group_starts):
        rows, middle, gathered, apply_adapter, query_rows, keys, value_rows, log_totals, hidden = (
            cache
        )
        grad_active = contract_axes(
            lax.all_gather(grad_rows.astype(jnp.bfloat16), "tensor", axis=0, tiled=True),
            output_weight[0],
            1,
            1,
        )
        _, gelu_back = jax.vjp(gelu_tanh, hidden)
        grad_hidden = gelu_back(grad_active)[0].astype(jnp.bfloat16)
        grad_normed_two = lax.psum_scatter(
            contract_axes(grad_hidden, feedforward_weight[0], 1, 1).astype(jnp.bfloat16),
            "tensor",
            scatter_dimension=0,
            tiled=True,
        ).astype(jnp.float32)
        _, norm_two_back = jax.vjp(
            lambda inner_rows: layer_norm(inner_rows, norm_gains[0, 1], norm_biases[0, 1]), middle
        )
        grad_middle = grad_rows + norm_two_back(grad_normed_two)[0]
        grad_mixed = contract_axes(
            lax.all_gather(grad_middle.astype(jnp.bfloat16), "tensor", axis=0, tiled=True),
            projection_weight[0],
            1,
            1,
        ).astype(jnp.bfloat16)
        query_gradient, grad_k, value_gradient = lax.map(
            attend_back,
            (
                query_rows.reshape(shaped),
                keys.reshape(shaped),
                value_rows.reshape(shaped),
                group_starts,
                log_totals,
                grad_mixed.reshape(shaped),
            ),
        )
        query_gradient = query_gradient.reshape(-1, head_cols)
        grad_k = grad_k.reshape(-1, head_cols)
        value_gradient = value_gradient.reshape(-1, head_cols)
        grad_low = jnp.concatenate(
            [
                adapter_scale * contract_axes(query_gradient, adapter_up_weight[0, 0], 1, 1),
                adapter_scale * contract_axes(value_gradient, adapter_up_weight[0, 1], 1, 1),
            ],
            axis=1,
        ).astype(jnp.bfloat16)
        grad_joined = jnp.concatenate([query_gradient, grad_k, value_gradient], axis=1)
        grad_normed = lax.psum_scatter(
            (
                contract_axes(grad_joined, w_cat, 1, 1)
                + contract_axes(grad_low, stacked_down_maps, 1, 1)
            ).astype(jnp.bfloat16),
            "tensor",
            scatter_dimension=0,
            tiled=True,
        ).astype(jnp.float32)
        _, norm_back = jax.vjp(
            lambda inner_rows: layer_norm(inner_rows, norm_gains[0, 0], norm_biases[0, 0]), rows
        )
        grad_in = grad_middle + norm_back(grad_normed)[0]
        grad_down = contract_axes(gathered, grad_low, 0, 0)
        part_a = jnp.stack([grad_down[:, :ADAPTER_RANK], grad_down[:, ADAPTER_RANK:]])
        second_portion = adapter_scale * jnp.stack(
            [
                contract_axes(apply_adapter[:, :ADAPTER_RANK], query_gradient, 0, 0),
                contract_axes(apply_adapter[:, ADAPTER_RANK:], value_gradient, 0, 0),
            ]
        )
        return (grad_in, part_a, second_portion)

    received = jnp.zeros((own_rows, width), jnp.bfloat16)
    finals = []
    stored = []
    for tick in range(batches + 1):
        batch_index = jnp.clip(tick - section, 0, batches - 1)
        own = lax.dynamic_index_in_dim(activations[0], batch_index, 0, keepdims=False)
        rows = jnp.where(first, own, received).astype(jnp.float32)
        group_starts = lax.dynamic_index_in_dim(starts, batch_index, 0, keepdims=False)
        output, cache = forward_relay(rows, group_starts)
        finals.append(output)
        stored.append(rows)
        if tick < batches:
            received = from_behind(output.astype(jnp.bfloat16), "section", 1)
    stacked = jax.tree.map(lambda *items: jnp.stack(items), *stored)
    returned = jnp.zeros((own_rows, width), jnp.bfloat16)
    totals_a = jnp.zeros((2, width, ADAPTER_RANK), jnp.float32)
    totals_b = jnp.zeros((2, ADAPTER_RANK, head_cols), jnp.float32)
    grads_in = []
    for tick in range(batches + 1):
        position = tick - 1 + section
        batch_index = jnp.clip(position, 0, batches - 1)
        valid = ((position >= 0) & (position < batches)).astype(jnp.float32)
        own = lax.dynamic_index_in_dim(activations[0], batch_index, 0, keepdims=False)
        grad_rows = jnp.where(first, returned, own).astype(jnp.float32) * valid
        group_starts = lax.dynamic_index_in_dim(starts, batch_index, 0, keepdims=False)
        slot_index = jnp.clip(tick - 1 + 2 * section, 0, batches)
        picked = lax.dynamic_index_in_dim(stacked, slot_index, 0, keepdims=False)
        _, cache = forward_relay(picked, group_starts)
        grad_in, part_a, second_portion = backward_relay(grad_rows, cache, group_starts)
        grads_in.append(grad_in)
        if tick < batches:
            returned = from_behind(grad_in.astype(jnp.bfloat16), "section", -1)
        part_a, second_portion = reduce_adapters(part_a, second_portion)
        totals_a = totals_a + part_a
        totals_b = totals_b + second_portion
    combined = jnp.stack(
        [jnp.where(first, grads_in[index + 1], finals[index + 1]) for index in range(batches)]
    )
    return (combined[None], totals_a[None], totals_b[None])


LOW = 2 * ADAPTER_RANK
VMEM_SPACE = pl.BlockSpec(memory_space=pltpu.VMEM)
SMEM_SPACE = pl.BlockSpec(memory_space=pltpu.SMEM)
HBM_SPACE = pl.BlockSpec(memory_space=pltpu.HBM)
BLOCK = 256
CHUNK = 2 * BLOCK


def send(block, route):
    pairs = []
    for s in range(2):
        for t in range(4):
            to = route(s, t)
            if to is not None:
                pairs.append((s * 4 + t, to[0] * 4 + to[1]))
    return lax.ppermute(block, ("section", "tensor"), pairs)


def other_core(block):
    return send(block, lambda s, t: (1 - s, t))


def x_swap(block):
    return send(block, lambda s, t: (s, t ^ 1))


def y_swap(block):
    return send(block, lambda s, t: (s, t ^ 2))


def after(value, *others):
    return lax.optimization_barrier((value, others))[0]


def cross_send(block, source=0):
    return send(block, lambda s, t: (t >> 1, t ^ 2) if s == source else None)


def collect(target, same_chip, cross_chip):
    return (
        send(same_chip, lambda s, t: (target, t) if s == t & 1 and s != target else None),
        send(cross_chip, lambda s, t: (target, t ^ 2) if s == t & 1 else None),
    )


def mm(left, right):
    return jnp.dot(left, right, preferred_element_type=jnp.float32)


def mm_nt(left, right):
    return contract_axes(left, right, 1, 1)


def norm_back(rows, gain, grad):
    mean = jnp.mean(rows, axis=-1, keepdims=True)
    centered = rows - mean
    scale = lax.rsqrt(jnp.mean(centered * centered, axis=-1, keepdims=True) + 1e-05)
    unit = centered * scale
    scaled = grad * gain
    return scale * (
        scaled
        - jnp.mean(scaled, axis=-1, keepdims=True)
        - unit * jnp.mean(scaled * unit, axis=-1, keepdims=True)
    )


def gelu_both(value):
    square = value * value
    bent = jnp.tanh(0.7978845608028654 * value * (1.0 + 0.044715 * square))
    half = 0.5 * (1.0 + bent)
    slope = half + 0.5 * value * (1.0 - bent * bent) * (
        0.7978845608028654 * (1.0 + 3.0 * 0.044715 * square)
    )
    return value * half, slope


def cost(flops, read):
    return pl.CostEstimate(flops=1000, bytes_accessed=1000, transcendentals=0)


def kernel_params(mib):
    return pltpu.CompilerParams(vmem_limit_bytes=mib * 1024 * 1024)


def position_mask(meta, query_block, key_block):
    shape = (BLOCK, BLOCK)
    key_pos = key_block * BLOCK + lax.broadcasted_iota(jnp.int32, shape, 0)
    query_pos = query_block * BLOCK + lax.broadcasted_iota(jnp.int32, (1, BLOCK), 1)
    low = jnp.zeros((1, BLOCK), jnp.int32)
    for c in range(4):
        first = meta[4 + c]
        low = jnp.where(first <= query_pos, jnp.maximum(low, first), low)
    valid = key_pos >= low
    if query_block == key_block:
        valid = valid & (key_pos <= query_pos)
    return valid


def head_lanes(half):
    return (lax.broadcasted_iota(jnp.int32, (1, 2 * HEAD), 1) // HEAD) == half


def start_pick(choices, target, sem):
    for condition, source in choices:

        @pl.when(condition)
        def _(source=source):
            pltpu.make_async_copy(source, target, sem).start()


def load_qkv_weight(layer, meta, pieces, w_buf, sem):
    own, other, lead, trail = pieces
    s, y, w = meta[0], meta[2], meta[8]
    start_pick(
        (((s == y) & (s == layer), own), ((s == y) & (s != layer), other)), w_buf, sem
    )

    @pl.when(s != y)
    def _():
        for part, side in ((lead, w), (trail, 1 - w)):
            pltpu.make_async_copy(part, w_buf.at[pl.ds(2 * side, 2)], sem).start()

    return pltpu.make_async_copy(own, w_buf, sem)


def half_rows(core):
    return pl.ds(pl.multiple_of(core * BLOCK, BLOCK), BLOCK)


def lay_out(meta, own, near, target):
    s = meta[0]
    target[half_rows(s), :] = own[...]
    target[half_rows(1 - s), :] = near[...]


def share_out(meta, source, keep, give):
    s = meta[0]
    keep[...] = source[half_rows(s), :]
    give[...] = source[half_rows(1 - s), :]


def attend_kernel(layer, chunk, meta, shared, varied, own, near, *rest):
    before, rest = rest[: 2 * chunk], rest[2 * chunk :]
    q_out, k_out, v_out, lse_out, mixed_out, keep, give = rest[4:11]
    (
        n_buf, w_buf, score_buf, vt_buf, q_ref, k_ref, v_ref, lse_ref, mixed_ref, sem, out_sems
    ) = rest[11:]
    loaded = load_qkv_weight(layer, meta, rest[:4], w_buf, sem)
    down = shared[layer, 8:16, :].astype(jnp.bfloat16)
    bias = varied[layer, 1:2, :]
    up = varied[layer, 8:16, 0:512].astype(jnp.bfloat16)
    lay_out(meta, own, near, n_buf)
    keys = [k_ref] if chunk == 0 else [before[0], k_ref]
    if chunk == 1:
        for b in range(2):
            span = slice(b * BLOCK, (b + 1) * BLOCK)
            vt_buf[:, span] = before[1][span, :].T
    loaded.wait()
    normed = n_buf[...]
    low = mm_nt(normed, down).astype(jnp.bfloat16)
    lifted = adapter_scale * mm(low, up)
    q_ref[...] = (mm(normed, w_buf[0]) + bias[:, 0:256] + lifted[:, 0:256]).astype(jnp.bfloat16)
    k_ref[...] = mm(normed, w_buf[1]).astype(jnp.bfloat16)
    v_ref[...] = (mm(normed, w_buf[2]) + bias[:, 256:512] + lifted[:, 256:512]).astype(jnp.bfloat16)
    saved = [
        pltpu.make_async_copy(source, target, out_sems.at[i])
        for i, (source, target) in enumerate(
            (
                (q_ref, q_out), (k_ref, k_out), (v_ref, v_out), (lse_ref, lse_out),
                (mixed_ref, mixed_out),
            )
        )
    ]
    for copy in saved[:3]:
        copy.start()
    for b in range(2):
        span = slice(b * BLOCK, (b + 1) * BLOCK)
        vt_buf[:, chunk * CHUNK + b * BLOCK : chunk * CHUNK + (b + 1) * BLOCK] = v_ref[span, :].T

    def one_head(head, carry):
        lanes = pl.ds(pl.multiple_of((head // 2) * 128, 128), 128)
        chosen = head_lanes(head % 2)
        deep = pl.ds(pl.multiple_of(head * HEAD, HEAD), HEAD)
        for i in range(2):
            span = slice(i * BLOCK, (i + 1) * BLOCK)
            place = 2 * chunk + i
            query = jnp.where(chosen, q_ref[span, lanes] * HEAD ** (-0.5), 0.0).astype(jnp.bfloat16)
            top = jnp.full((1, BLOCK), -1e30, jnp.float32)
            for j in range(place + 1):
                rows = slice((j % 2) * BLOCK, (j % 2 + 1) * BLOCK)
                scores = mm_nt(keys[j // 2][rows, lanes], query)
                scores = jnp.where(position_mask(meta, place, j), scores, -1e30)
                score_buf[j] = scores
                top = jnp.maximum(top, jnp.max(scores, axis=0, keepdims=True))
            total = jnp.zeros((1, BLOCK), jnp.float32)
            mixed = jnp.zeros((HEAD, BLOCK), jnp.float32)
            for j in range(place + 1):
                weights = jnp.exp(score_buf[j] - top)
                total = total + jnp.sum(weights, axis=0, keepdims=True)
                mixed = mixed + mm(
                    vt_buf[deep, j * BLOCK : (j + 1) * BLOCK], weights.astype(jnp.bfloat16)
                )
            mixed_ref[deep, span] = mixed / total
            lse_ref[pl.ds(head, 1), span] = top + jnp.log(total)
        return carry

    lax.fori_loop(0, 4, one_head, 0)
    for copy in saved[3:]:
        copy.start()
    for b in range(2):
        span = slice(b * BLOCK, (b + 1) * BLOCK)
        n_buf[span, :] = mm_nt(
            mixed_ref[:, span].T.astype(jnp.bfloat16), w_buf[3]
        ).astype(jnp.bfloat16)
    share_out(meta, n_buf, keep, give)
    for copy in saved:
        copy.wait()


def attend_call(layer, chunk, meta, blocks, before, shared, varied, weight):
    bf, f32 = jnp.bfloat16, jnp.float32
    wide = jax.ShapeDtypeStruct((CHUNK, 256), bf)
    piece = jax.ShapeDtypeStruct((BLOCK, 1024), bf)
    *saved, keep, give = pl.pallas_call(
        functools.partial(attend_kernel, layer, chunk),
        in_specs=[SMEM_SPACE] + [VMEM_SPACE] * (4 + 2 * chunk) + [HBM_SPACE] * 4,
        out_specs=[HBM_SPACE] * 5 + [VMEM_SPACE] * 2,
        out_shape=[wide, wide, wide, jax.ShapeDtypeStruct((8, CHUNK), f32),
                   jax.ShapeDtypeStruct((256, CHUNK), f32), piece, piece],
        scratch_shapes=[
            pltpu.VMEM((CHUNK, 1024), bf),
            pltpu.VMEM((4, 1024, 256), bf),
            pltpu.VMEM((2 + 2 * chunk, BLOCK, BLOCK), f32),
            pltpu.VMEM((256, CHUNK * (1 + chunk)), bf),
            pltpu.VMEM((CHUNK, 256), bf),
            pltpu.VMEM((CHUNK, 256), bf),
            pltpu.VMEM((CHUNK, 256), bf),
            pltpu.VMEM((8, CHUNK), f32),
            pltpu.VMEM((256, CHUNK), f32),
            pltpu.SemaphoreType.DMA,
            pltpu.SemaphoreType.DMA((5,)),
        ],
        compiler_params=kernel_params(24),
        cost_estimate=cost(3.5e9, 8e6),
        name="attention_forward_%d" % chunk,
    )(meta, shared, varied, *blocks, *(before if chunk else ()), *weight)
    return saved, keep, give


def attend_back_kernel(layer, chunk, meta, shared, varied, n_own, n_near, g_own, g_near, *rest):
    n_saved = 5 + 2 * chunk
    saved, rest = rest[:n_saved], rest[n_saved:]
    saved_sems, rest = rest[-1], rest[:-1]
    bufs, rest = rest[-n_saved:], rest[:-n_saved]
    fetches = [
        pltpu.make_async_copy(source, target, saved_sems.at[i])
        for i, (source, target) in enumerate(zip(saved, bufs))
    ]
    for fetch in fetches:
        fetch.start()
    q_ref, lse_ref, mixed_ref = bufs[:3]
    keys, values = bufs[3 : 4 + chunk], bufs[4 + chunk :]
    if chunk == 0:
        dk_in, dv_in, down_in, up_in = rest[:4]
        keep, give, down_ref, up_ref = rest[8:12]
        weight, scratch = rest[4:8], rest[12:]
    else:
        keep, give, down_ref, up_ref, dk_out, dv_out = rest[4:10]
        weight, scratch = rest[:4], rest[10:]
    (
        n_buf, g_buf, w_buf, kt_buf, do_buf, delta_buf, dqt_buf, dk_buf, dv_buf, dq_buf, sem
    ) = scratch
    loaded = load_qkv_weight(layer, meta, weight, w_buf, sem)
    lay_out(meta, g_own, g_near, g_buf)
    lay_out(meta, n_own, n_near, n_buf)
    for fetch in fetches:
        fetch.wait()
    for j in range(2 + 2 * chunk):
        rows = slice((j % 2) * BLOCK, (j % 2 + 1) * BLOCK)
        kt_buf[:, j * BLOCK : (j + 1) * BLOCK] = keys[j // 2][rows, :].T
    if chunk == 0:
        dk_buf[...] = dk_in[...]
        dv_buf[...] = dv_in[...]
    else:
        dk_buf[...] = jnp.zeros_like(dk_buf)
        dv_buf[...] = jnp.zeros_like(dv_buf)
    loaded.wait()
    do_buf[...] = mm(g_buf[...], w_buf[3]).astype(jnp.bfloat16)
    for b in range(2):
        span = slice(b * BLOCK, (b + 1) * BLOCK)
        product = do_buf[span, :].astype(jnp.float32).T * mixed_ref[:, span]
        for head in range(4):
            delta_buf[head : head + 1, span] = jnp.sum(
                product[head * HEAD : (head + 1) * HEAD], axis=0, keepdims=True
            )

    def one_head(head, carry):
        lanes = pl.ds(pl.multiple_of((head // 2) * 128, 128), 128)
        chosen = head_lanes(head % 2)
        deep = pl.ds(pl.multiple_of(head * HEAD, HEAD), HEAD)
        for i in range(2):
            span = slice(i * BLOCK, (i + 1) * BLOCK)
            place = 2 * chunk + i
            query = jnp.where(chosen, q_ref[span, lanes] * HEAD ** (-0.5), 0.0).astype(jnp.bfloat16)
            grad_mixed = jnp.where(chosen, do_buf[span, lanes], 0.0).astype(jnp.bfloat16)
            lse = lse_ref[pl.ds(head, 1), span]
            delta = delta_buf[pl.ds(head, 1), span]
            grad_query = jnp.zeros((HEAD, BLOCK), jnp.float32)
            for j in range(place + 1):
                rows = slice((j % 2) * BLOCK, (j % 2 + 1) * BLOCK)
                all_rows = slice(j * BLOCK, (j + 1) * BLOCK)
                scores = mm_nt(keys[j // 2][rows, lanes], query)
                probs = jnp.where(position_mask(meta, place, j), jnp.exp(scores - lse), 0.0)
                grad_probs = mm_nt(values[j // 2][rows, lanes], grad_mixed)
                grad_scores = (probs * (grad_probs - delta)).astype(jnp.bfloat16)
                dv_buf[all_rows, lanes] += mm(probs.astype(jnp.bfloat16), grad_mixed)
                dk_buf[all_rows, lanes] += mm(grad_scores, query)
                grad_query = grad_query + mm(kt_buf[deep, all_rows], grad_scores)
            dqt_buf[deep, span] = grad_query * HEAD ** (-0.5)
        return carry

    lax.fori_loop(0, 4, one_head, 0)
    down = shared[layer, 8:16, :].astype(jnp.bfloat16)
    up = varied[layer, 8:16, 0:512].astype(jnp.bfloat16)
    for b in range(2):
        span = slice(b * BLOCK, (b + 1) * BLOCK)
        dq_buf[span, :] = dqt_buf[:, span].T.astype(jnp.bfloat16)
    done = slice(chunk * CHUNK, (chunk + 1) * CHUNK)
    normed = n_buf[...]
    grad_q = dq_buf[...]
    grad_k = dk_buf[done, :].astype(jnp.bfloat16)
    grad_v = dv_buf[done, :].astype(jnp.bfloat16)
    both = jnp.concatenate([grad_q, grad_v], axis=1)
    low_grad = (adapter_scale * mm_nt(both, up)).astype(jnp.bfloat16)
    low_grad_t = (adapter_scale * mm_nt(up, both)).astype(jnp.bfloat16)
    low_t = mm_nt(down, normed).astype(jnp.bfloat16)
    g_buf[...] = (
        mm_nt(grad_q, w_buf[0]) + mm_nt(grad_k, w_buf[1]) + mm_nt(grad_v, w_buf[2])
        + mm(low_grad, down)
    ).astype(jnp.bfloat16)
    share_out(meta, g_buf, keep, give)
    total_down = mm(low_grad_t, normed)
    total_up = adapter_scale * mm(low_t, both)
    if chunk == 0:
        total_down = total_down + down_in[...]
        total_up = total_up + up_in[...]
    else:
        dk_out[...] = dk_buf[0:CHUNK, :]
        dv_out[...] = dv_buf[0:CHUNK, :]
    down_ref[...] = total_down
    up_ref[...] = total_up


def attend_back_call(layer, chunk, meta, blocks, grads, saved, carried, shared, varied, weight):
    bf, f32 = jnp.bfloat16, jnp.float32
    piece = jax.ShapeDtypeStruct((BLOCK, 1024), bf)
    tall = jax.ShapeDtypeStruct((CHUNK, 256), f32)
    spans = CHUNK * (1 + chunk)
    q, _, _, lse, mixed = saved[chunk]
    keys = [one[1] for one in saved[: chunk + 1]]
    values = [one[2] for one in saved[: chunk + 1]]
    held = (q, lse, mixed, *keys, *values)
    inputs = (shared, varied, *blocks, *grads, *held, *carried)
    return pl.pallas_call(
        functools.partial(attend_back_kernel, layer, chunk),
        in_specs=[SMEM_SPACE] + [VMEM_SPACE] * 6 + [HBM_SPACE] * len(held)
        + [VMEM_SPACE] * len(carried) + [HBM_SPACE] * 4,
        out_specs=[VMEM_SPACE] * (4 + 2 * chunk),
        out_shape=[piece, piece, jax.ShapeDtypeStruct((LOW, 1024), f32),
                   jax.ShapeDtypeStruct((LOW, 512), f32)] + [tall] * (2 * chunk),
        scratch_shapes=[
            pltpu.VMEM((CHUNK, 1024), bf),
            pltpu.VMEM((CHUNK, 1024), bf),
            pltpu.VMEM((4, 1024, 256), bf),
            pltpu.VMEM((256, spans), bf),
            pltpu.VMEM((CHUNK, 256), bf),
            pltpu.VMEM((8, CHUNK), f32),
            pltpu.VMEM((256, CHUNK), f32),
            pltpu.VMEM((spans, 256), f32),
            pltpu.VMEM((spans, 256), f32),
            pltpu.VMEM((CHUNK, 256), bf),
            pltpu.SemaphoreType.DMA,
            *[pltpu.VMEM(one.shape, one.dtype) for one in held],
            pltpu.SemaphoreType.DMA((len(held),)),
        ],
        compiler_params=kernel_params(24),
        cost_estimate=cost(6e9, 12e6),
        name="attention_backward_%d" % chunk,
    )(meta, *inputs, *weight)


def summed(passed, far):
    return passed[...].astype(jnp.float32) + far[...].astype(jnp.float32)


def rows_middle_kernel(layer, h_ref, passed, far, shared, middle_ref, normed_ref):
    middle = h_ref[...].astype(jnp.float32) + summed(passed, far) + shared[layer, 4:5, :]
    middle_ref[...] = middle
    normed_ref[...] = layer_norm(middle, shared[layer, 1:2, :], shared[layer, 3:4, :]).astype(
        jnp.bfloat16
    )


def load_units(layer, meta, pieces, w1, w2, sems):
    own, other, (lead, trail) = pieces[0:2], pieces[2:4], pieces[4:6]
    s, y, w = meta[0], meta[2], meta[8]
    copies = []
    for m, matrix in enumerate((w1, w2)):
        start_pick(
            (
                ((s == y) & (s == layer), own[m]),
                ((s == y) & (s != layer), other[m]),
                ((s != y) & (w == m), lead),
                ((s != y) & (w != m), trail),
            ),
            matrix,
            sems.at[m],
        )
        copies.append(pltpu.make_async_copy(own[m], matrix, sems.at[m]))
    return copies


def stack_rows(blocks, target):
    for i, block in enumerate(blocks):
        target[i * BLOCK : (i + 1) * BLOCK, :] = block[...]


def halve(total, keep, give):
    keep[...] = total[:BLOCK].astype(jnp.bfloat16)
    give[...] = total[BLOCK:].astype(jnp.bfloat16)


def units_kernel(layer, meta, n0, n1, bias, *rest):
    keep, give, slope_out, w1, w2, sems, n_buf, slope_buf, out_sem = rest[6:]
    waits = load_units(layer, meta, rest[:6], w1, w2, sems)
    stack_rows((n0, n1), n_buf)
    waits[0].wait()
    active, slope = gelu_both(mm(n_buf[...], w1[...]) + bias[layer, 0:1, :])
    slope_buf[...] = slope.astype(jnp.bfloat16)
    saving = pltpu.make_async_copy(slope_buf, slope_out, out_sem)
    saving.start()
    waits[1].wait()
    halve(mm(active.astype(jnp.bfloat16), w2[...]), keep, give)
    saving.wait()


def units_turn_kernel(layer, meta, n0, n1, g0, g1, bias, *rest):
    keep, give, out_keep, out_give, w1, w2, sems, n_buf, g_buf = rest[6:]
    waits = load_units(layer, meta, rest[:6], w1, w2, sems)
    stack_rows((n0, n1), n_buf)
    stack_rows((g0, g1), g_buf)
    for copy in waits:
        copy.wait()
    active, slope = gelu_both(mm(n_buf[...], w1[...]) + bias[layer, 0:1, :])
    grad_hidden = (mm_nt(g_buf[...], w2[...]) * slope).astype(jnp.bfloat16)
    halve(mm_nt(grad_hidden, w1[...]), keep, give)
    halve(mm(active.astype(jnp.bfloat16), w2[...]), out_keep, out_give)


def units_back_kernel(layer, meta, g0, g1, slope_in, *rest):
    keep, give, w1, w2, sems, g_buf, slope_buf, in_sem = rest[6:]
    waits = load_units(layer, meta, rest[:6], w1, w2, sems)
    fetch = pltpu.make_async_copy(slope_in, slope_buf, in_sem)
    fetch.start()
    stack_rows((g0, g1), g_buf)
    waits[1].wait()
    fetch.wait()
    grad = (mm_nt(g_buf[...], w2[...]) * slope_buf[...].astype(jnp.float32)).astype(jnp.bfloat16)
    waits[0].wait()
    halve(mm_nt(grad, w1[...]), keep, give)


def rows_first_kernel(meta, mine, crossed, far_mine, far_crossed, shared, *outs):
    holder = meta[0] == meta[1]
    upper = meta[2] == 0
    first = jnp.where(holder, mine[...], far_mine[...])
    second = jnp.where(holder, crossed[...], far_crossed[...])
    for c, (one, other) in enumerate(((first, second), (second, first))):
        rows = jnp.where(upper, one, other)
        outs[c][...] = rows
        outs[2 + c][...] = layer_norm(
            rows.astype(jnp.float32), shared[0, 0:1, :], shared[0, 2:3, :]
        ).astype(jnp.bfloat16)


def rows_next_kernel(middle, passed, far, shared, between_ref, normed_ref):
    between = (middle[...] + summed(passed, far) + shared[0, 5:6, :]).astype(jnp.bfloat16)
    between_ref[...] = between
    normed_ref[...] = layer_norm(
        between.astype(jnp.float32), shared[1, 0:1, :], shared[1, 2:3, :]
    ).astype(jnp.bfloat16)


def rows_turn_kernel(layer, middle, g_ref, passed, far, shared, grad_ref, sent_ref):
    grad_middle = g_ref[...].astype(jnp.float32) + norm_back(
        middle[...], shared[layer, 1:2, :], summed(passed, far)
    )
    grad_ref[...] = grad_middle
    sent_ref[...] = grad_middle.astype(jnp.bfloat16)


def rows_before_kernel(gm_ref, passed, far, between_ref, shared, grad_ref):
    grad_rows = gm_ref[...] + norm_back(
        between_ref[...].astype(jnp.float32), shared[1, 0:1, :], summed(passed, far)
    )
    grad_ref[...] = grad_rows.astype(jnp.bfloat16)


def rows_output_kernel(middle, passed, far, shared, wide_ref, narrow_ref):
    total = middle[...] + summed(passed, far) + shared[1, 5:6, :]
    wide_ref[...] = total
    narrow_ref[...] = total.astype(jnp.bfloat16)


def rows_final_kernel(gm_ref, passed, far, h_ref, shared, wide_ref, narrow_ref):
    grad_in = gm_ref[...] + norm_back(
        h_ref[...].astype(jnp.float32), shared[0, 0:1, :], summed(passed, far)
    )
    wide_ref[...] = grad_in
    narrow_ref[...] = grad_in.astype(jnp.bfloat16)


def units_call(kernel, meta, small, saved, weights, outs, saving, scratch, name):
    return pl.pallas_call(
        kernel,
        in_specs=[SMEM_SPACE] + [VMEM_SPACE] * len(small) + [HBM_SPACE] * (len(saved) + len(weights)),
        out_specs=[VMEM_SPACE] * len(outs) + [HBM_SPACE] * len(saving),
        out_shape=[*outs, *saving],
        scratch_shapes=scratch,
        compiler_params=kernel_params(24),
        cost_estimate=cost(2e9, 8e6),
        name=name,
    )(meta, *small, *saved, *weights)


def plain_call(kernel, scalar, small, large, outs, scratch, flops, name):
    specs = [VMEM_SPACE] * len(small) + [HBM_SPACE] * len(large)
    operands = (*small, *large)
    if scalar is not None:
        specs, operands = [SMEM_SPACE] + specs, (scalar, *operands)
    return pl.pallas_call(
        kernel,
        in_specs=specs,
        out_specs=[VMEM_SPACE] * len(outs),
        out_shape=outs,
        scratch_shapes=scratch,
        compiler_params=kernel_params(24),
        cost_estimate=cost(flops, 8e6),
        name=name,
    )(*operands)


def deal_rows(source, slots, section, y):
    same = lax.dynamic_index_in_dim(slots, y, 0, keepdims=False)
    cross = lax.dynamic_index_in_dim(slots, 1 - y, 0, keepdims=False)
    moved = send(same, lambda s, t: (t & 1, t) if s == source and s != t & 1 else None)
    crossed = send(cross, lambda s, t: (t & 1, t ^ 2) if s == source else None)
    mine = jnp.where(section == source, same, moved)
    return mine, crossed


def to_x(block):
    return send(block, lambda s, t: (s, t ^ 1) if s == t & 1 else None)


def from_x(block):
    return send(block, lambda s, t: (s, t ^ 1) if s != t & 1 else None)


def z_swap(block):
    size = lax.axis_size("dp")
    pairs = [
        ((s * size + z) * 4 + t, (s * size + (z ^ 1)) * 4 + t)
        for s in range(2) for z in range(size) for t in range(4) if s != t >> 1
    ]
    return lax.ppermute(block, ("section", "dp", "tensor"), pairs)


def chip_sum(keep, give, last, swap=x_swap):
    take = other_core(after(give, last))
    passed = (keep.astype(jnp.float32) + take.astype(jnp.float32)).astype(jnp.bfloat16)
    return passed, swap(passed)


def total_over_z(downs, ups):
    both = jnp.concatenate([jnp.concatenate(downs), jnp.concatenate(ups)], axis=1)
    size = lax.axis_size("dp")
    step = 1
    while step < size:
        both = both + lax.ppermute(both, "dp", [(i, i ^ step) for i in range(size)])
        step *= 2
    return both


def total_over_cores(both, section, y):
    both = both + y_swap(both)
    moved = other_core(both)
    down = both[:, :1024] + moved[:, :1024]
    down = jnp.where(section == 0, down[:LOW], down[LOW:])
    up = jnp.where(section == y, both[:, 1024:], moved[:, 1024:])
    return down + x_swap(down), jnp.where(section == 0, up[:LOW], up[LOW:])


def relay_body(
    activations, starts, attention_weights, projection_weight, feedforward_weight, output_weight,
    norm_gains, norm_biases, output_biases, query_value_bias, feedforward_bias,
    adapter_down_weight, adapter_up_weight,
):
    bf, f32 = jnp.bfloat16, jnp.float32
    section = lax.axis_index("section")
    place = lax.axis_index("tensor")
    y, x = place // 2, place % 2
    first = section == 0

    mine, crossed = deal_rows(0, activations[0], section, y)
    down_rows = adapter_down_weight[0].astype(f32).transpose(0, 2, 1).reshape(LOW, 1024)
    up0 = adapter_up_weight[0, 0].astype(f32)
    up1 = adapter_up_weight[0, 1].astype(f32)
    zero = jnp.zeros((ADAPTER_RANK, 256), f32)
    common = jnp.concatenate(
        [norm_gains[0], norm_biases[0], output_biases[0], jnp.zeros((2, 1024), f32), down_rows]
    )
    own_part = jnp.concatenate(
        [
            feedforward_bias,
            jnp.pad(query_value_bias[0].reshape(1, 512), ((0, 0), (0, 512))),
            jnp.zeros((6, 1024), f32),
            jnp.concatenate([up0, zero, jnp.zeros((ADAPTER_RANK, 512), f32)], axis=1),
            jnp.concatenate([zero, up1, jnp.zeros((ADAPTER_RANK, 512), f32)], axis=1),
        ]
    )
    partner = other_core(common)
    partner_part = other_core(own_part)
    parts = jnp.where(
        first, jnp.stack([own_part, partner_part]), jnp.stack([partner_part, own_part])
    )
    near_varied = jnp.where(section == y, parts, y_swap(parts))
    shared = jnp.where(first, jnp.stack([common, partner]), jnp.stack([partner, common]))
    meta = jnp.concatenate(
        [
            jnp.stack([section, x, y, place]).astype(jnp.int32),
            lax.dynamic_index_in_dim(starts, y, 0, keepdims=False).reshape(4),
            (lax.axis_index("dp") % 2).astype(jnp.int32)[None],
        ]
    )
    even = lax.axis_index("dp") % 2 == 0
    own_a = jnp.concatenate([attention_weights[0], projection_weight[0].T[None]])
    w1_own, w2_own = feedforward_weight[0], output_weight[0]
    other_a = other_core(own_a)
    mine, crossed, shared = lax.optimization_barrier((mine, crossed, shared))
    lead_a0 = cross_send(after(jnp.where(even, own_a[:2], own_a[2:]), crossed, near_varied))
    far_mine, far_crossed = to_x(mine), to_x(crossed)
    g_mine, g_crossed = deal_rows(1, after(activations[0], crossed), section, y)
    far_crossed, g_mine, g_crossed = lax.optimization_barrier((far_crossed, g_mine, g_crossed))
    trail_a0 = z_swap(after(lead_a0, far_mine, far_crossed))

    sheet = jax.ShapeDtypeStruct((BLOCK, 1024), f32)
    thin = jax.ShapeDtypeStruct((BLOCK, 1024), bf)
    slope_shape = jax.ShapeDtypeStruct((CHUNK, 1024), bf)
    matrices = [
        pltpu.VMEM((1024, 1024), bf), pltpu.VMEM((1024, 1024), bf), pltpu.SemaphoreType.DMA((2,))
    ]
    group = pltpu.VMEM((CHUNK, 1024), bf)

    def small(kernel, *operands, outs, name):
        return plain_call(kernel, None, operands, (), outs, [], 1e7, name)

    def attend(layer, chunk, normed, before, weight, near=None):
        near = other_core(normed) if near is None else near
        return attend_call(
            layer, chunk, meta, (normed, near), before, shared, near_varied, weight
        )

    def units(layer, normed, weight):
        return units_call(
            functools.partial(units_kernel, layer), meta, (normed, other_core(normed), near_varied),
            (), weight, [thin, thin], [slope_shape],
            [*matrices, group, group, pltpu.SemaphoreType.DMA], "units",
        )

    def units_turn(layer, normed, grad, near_grad, weight):
        return units_call(
            functools.partial(units_turn_kernel, layer), meta,
            (normed, other_core(normed), grad, near_grad, near_varied), (), weight,
            [thin] * 4, [], [*matrices, group, group], "units_turn",
        )

    def units_back(layer, grad, slope, weight):
        return units_call(
            functools.partial(units_back_kernel, layer), meta, (grad, other_core(grad)), (slope,),
            weight, [thin, thin], [], [*matrices, group, group, pltpu.SemaphoreType.DMA],
            "units_back",
        )

    def middle(layer, rows, sums):
        return small(
            functools.partial(rows_middle_kernel, layer), rows, *sums, shared, outs=[sheet, thin],
            name="rows_middle",
        )

    def turn(layer, middle_rows, grad, sums):
        return small(
            functools.partial(rows_turn_kernel, layer), middle_rows, grad, *sums, shared,
            outs=[sheet, thin], name="rows_turn",
        )

    row0, row1, n0, n1 = plain_call(
        rows_first_kernel, meta, (mine, crossed, far_mine, far_crossed, shared), (), [thin] * 4,
        [], 1e7, "rows_first",
    )
    g_far = [to_x(one) for one in (g_mine, g_crossed)]
    weights_a0 = (own_a, other_a, lead_a0, trail_a0)
    near_n0 = other_core(n0)
    lead_b0 = cross_send(jnp.where(even, *after((w1_own, w2_own), near_n0)))
    n00, n01 = n0, n1
    saved00, keep, give = attend(0, 0, n0, (), weights_a0, near_n0)
    keep, give, g_far = lax.optimization_barrier((keep, give, g_far))
    sum0 = chip_sum(keep, give, lead_a0)
    other_w1, other_w2 = (other_core(after(one, sum0[0])) for one in (w1_own, w2_own))
    trail_b0 = z_swap(after(lead_b0, sum0[0]))
    weights_b0 = (w1_own, w2_own, other_w1, other_w2, lead_b0, trail_b0)
    saved01, keep, give = attend(0, 1, n1, saved00[1:3], weights_a0)
    sum1 = chip_sum(keep, give, sum0[1])
    lead_a1 = cross_send(jnp.where(even, *after((other_a[:2], other_a[2:]), sum0[0])))
    middle00, n0 = middle(0, row0, sum0)
    keep, give, slope0 = units(0, n0, weights_b0)
    sum2 = chip_sum(keep, give, sum1[1])
    sum1, lead_a1 = lax.optimization_barrier((sum1, lead_a1))
    trail_a1 = z_swap(lead_a1)
    lead_b1 = cross_send(jnp.where(even, *after((other_w1, other_w2), lead_a1)))
    middle01, n1 = middle(0, row1, sum1)
    keep, give, slope1 = units(0, n1, weights_b0)
    sum3 = chip_sum(keep, give, sum2[1])
    sum2, trail_a1 = lax.optimization_barrier((sum2, trail_a1))
    weights_a1 = (own_a, other_a, lead_a1, trail_a1)
    between0, n10 = small(rows_next_kernel, middle00, *sum2, shared, outs=[thin, thin], name="rows_next")
    saved10, keep, give = attend(1, 0, n10, (), weights_a1)
    sum4 = chip_sum(keep, give, sum3[1])
    sum3, lead_b1 = lax.optimization_barrier((sum3, lead_b1))
    trail_b1 = z_swap(lead_b1)
    weights_b1 = (w1_own, w2_own, other_w1, other_w2, lead_b1, trail_b1)
    between1, n11 = small(rows_next_kernel, middle01, *sum3, shared, outs=[thin, thin], name="rows_next")
    saved11, keep, give = attend(1, 1, n11, saved10[1:3], weights_a1)
    sum5 = chip_sum(keep, give, sum4[1])
    holder, upper = section == x, y == 0
    mine, crossed = (
        jnp.where(holder, one, two) for one, two in zip((g_mine, g_crossed), after(g_far, sum4[0]))
    )
    grad_outs = (jnp.where(upper, mine, crossed), jnp.where(upper, crossed, mine))
    near_outs = [other_core(one) for one in grad_outs]
    middle10, m0 = middle(1, between0, sum4)
    keep, give, out_keep0, out_give0 = units_turn(1, m0, grad_outs[0], near_outs[0], weights_b1)
    sum6 = chip_sum(keep, give, sum5[1])
    middle11, m1 = middle(1, between1, sum5)
    keep, give, out_keep1, out_give1 = units_turn(1, m1, grad_outs[1], near_outs[1], weights_b1)
    sum7 = chip_sum(keep, give, sum6[1])
    grad_middle10, g0 = turn(1, middle10, grad_outs[0], sum6)
    grad_middle11, g1 = turn(1, middle11, grad_outs[1], sum7)
    keep, give, down1, up1, dk, dv = attend_back_call(
        1, 1, meta, (n11, other_core(n11)), (g1, other_core(g1)), (saved10, saved11), (), shared,
        near_varied, weights_a1,
    )
    out_sums = [
        chip_sum(*after(one, g1), sum7[1], from_x)
        for one in ((out_keep0, out_give0), (out_keep1, out_give1))
    ]
    keep, give, out_sums = lax.optimization_barrier((keep, give, out_sums))
    sum8 = chip_sum(keep, give, sum7[1])
    keep, give, down1, up1 = attend_back_call(
        1, 0, meta, (n10, other_core(n10)), (g0, other_core(g0)), (saved10, saved11),
        (dk, dv, down1, up1), shared, near_varied, weights_a1,
    )
    sum9 = chip_sum(keep, give, sum8[1])
    before1 = small(
        rows_before_kernel, grad_middle11, *after(sum8, keep), between1, shared, outs=[thin], name="rows_before"
    )[0]
    keep, give = units_back(0, before1, slope1, weights_b0)
    sum10 = chip_sum(keep, give, sum9[1])
    before0 = small(
        rows_before_kernel, grad_middle10, *sum9, between0, shared, outs=[thin], name="rows_before"
    )[0]
    keep, give = units_back(0, before0, slope0, weights_b0)
    sum11 = chip_sum(keep, give, sum10[1])
    grad_middle01, h1 = turn(0, middle01, before1, sum10)
    keep, give, down0, up0, dk, dv = attend_back_call(
        0, 1, meta, (n01, other_core(n01)), (h1, other_core(h1)), (saved00, saved01), (), shared,
        near_varied, weights_a0,
    )
    sum12 = chip_sum(keep, give, sum11[1], from_x)
    grad_middle00, h0 = turn(0, middle00, before0, sum11)
    keep, give, down0, up0 = attend_back_call(
        0, 0, meta, (n00, other_core(n00)), (h0, other_core(h0)), (saved00, saved01),
        (dk, dv, down0, up0), shared, near_varied, weights_a0,
    )
    sum13 = chip_sum(keep, give, sum12[1], from_x)
    outs = [
        small(rows_output_kernel, one, *after(two, sum13[0]), shared, outs=[sheet, thin],
              name="rows_output")
        for one, two in zip((middle10, middle11), out_sums)
    ]
    out_wide = jnp.where(upper, outs[0][0], outs[1][0])
    out_same, out_cross = collect(1, out_wide, jnp.where(upper, outs[1][1], outs[0][1]))
    totals = total_over_z((down0, down1), after((up0, up1), sum13[0]))
    sum13, totals = lax.optimization_barrier((sum13, totals))
    ends = [
        small(rows_final_kernel, one, *two, three, shared, outs=[sheet, thin], name="rows_final")
        for one, two, three in ((grad_middle00, sum13, row0), (grad_middle01, sum12, row1))
    ]
    wide = jnp.where(upper, ends[0][0], ends[1][0])
    in_same, in_cross = collect(0, wide, jnp.where(upper, ends[1][1], ends[0][1]))
    grad_down, grad_up = total_over_cores(totals, section, y)
    same = jnp.where(
        first, jnp.where(x == 0, wide, in_same), jnp.where(x == 1, out_wide, out_same)
    )
    cross = jnp.where(first, in_cross, out_cross).astype(f32)
    combined = jnp.where(y == 0, jnp.stack([same, cross]), jnp.stack([cross, same]))
    return (
        combined[None],
        grad_down.reshape(1, 2, ADAPTER_RANK, 1024).transpose(0, 1, 3, 2),
        jnp.stack([grad_up[:ADAPTER_RANK, :256], grad_up[ADAPTER_RANK:, 256:]])[None],
    )


def body(*arrays):
    dp = lax.axis_size("dp")
    known = (
        arrays[0].shape == (1, 2, BLOCK, 1024)
        and lax.axis_size("tensor") == 4
        and lax.axis_size("section") == 2
        and arrays[3].shape == (1, 256, 1024)
        and arrays[5].shape == (1, 1024, 1024)
        and dp & (dp - 1) == 0
    )
    return relay_body(*arrays) if known else plain_body(*arrays)


def solution(mesh):
    placed = (
        P("section", None, ("dp", "tensor"), None),
        P(None, "dp", None),
        P("section", None, None, "tensor"),
        P("section", "tensor", None),
        P("section", None, "tensor"),
        P("section", "tensor", None),
        P("section", None, None),
        P("section", None, None),
        P("section", None, None),
        P("section", None, "tensor"),
        P("section", "tensor"),
        P("section", None, None, None),
        P("section", None, None, "tensor"),
    )
    return jax.shard_map(
        body,
        mesh=mesh,
        in_specs=placed,
        out_specs=(
            P("section", None, ("dp", "tensor"), None),
            P("section", None, None, None),
            P("section", None, None, "tensor"),
        ),
        check_vma=False,
    )
```

```python
import functools

import jax
import jax.numpy as jnp
from jax import lax
from jax.experimental import pallas as pl
from jax.experimental.pallas import tpu as pltpu
from jax.sharding import PartitionSpec as P

HEAD = 64
ADAPTER_RANK = 4
SEQ_LEN = 1024


adapter_scale = 8.0


def from_behind(block, axis, distance):
    devices = range(lax.axis_size(axis))
    route = [(i - distance, i) for i in devices if i - distance in devices]
    return lax.ppermute(block, axis, route)


def contract_axes(left, right, left_dim, right_dim):
    return lax.dot_general(
        left, right, (((left_dim,), (right_dim,)), ((), ())), preferred_element_type=jnp.float32
    )


def layer_norm(rows, gain, shift):
    mean = jnp.mean(rows, axis=-1, keepdims=True)
    centered = rows - mean
    spread = jnp.mean(centered * centered, axis=-1, keepdims=True)
    return centered * lax.rsqrt(spread + 1e-05) * gain + shift


def gelu_tanh(value):
    return (
        0.5
        * value
        * (1.0 + jnp.tanh(0.7978845608028654 * (value + 0.044715 * value * value * value)))
    )


def doc_mask(doc_starts):
    positions = jnp.arange(SEQ_LEN, dtype=jnp.int32)
    labels = jnp.sum((doc_starts[None, :] <= positions[:, None]).astype(jnp.int32), axis=1)
    return (positions[None, :] <= positions[:, None]) & (labels[:, None] == labels[None, :])


def masked_scores(query_rows, keys, doc_starts):
    scores = jnp.einsum(
        "qhd,khd->hqk", query_rows, keys, preferred_element_type=jnp.float32
    ) * HEAD ** (-0.5)
    return jnp.where(doc_mask(doc_starts)[None], scores, -1e30)


def attend(items):
    query_rows, keys, value_rows, doc_starts = items
    scores = masked_scores(query_rows, keys, doc_starts)
    top = jnp.max(scores, axis=-1, keepdims=True)
    weights = jnp.exp(scores - top)
    total = jnp.sum(weights, axis=-1, keepdims=True)
    mixed = jnp.einsum(
        "hqk,khd->qhd",
        (weights / total).astype(jnp.bfloat16),
        value_rows,
        preferred_element_type=jnp.float32,
    )
    return (mixed.astype(jnp.bfloat16), (top + jnp.log(total))[:, :, 0])


def attend_back(items):
    query_rows, keys, value_rows, doc_starts, log_totals, grad_mixed = items
    scores = masked_scores(query_rows, keys, doc_starts)
    probs = jnp.exp(scores - log_totals[:, :, None])
    grad_probs = jnp.einsum(
        "qhd,khd->hqk", grad_mixed, value_rows, preferred_element_type=jnp.float32
    )
    inner = jnp.sum(probs * grad_probs, axis=-1, keepdims=True)
    grad_scores = (probs * (grad_probs - inner)).astype(jnp.bfloat16)
    query_gradient = jnp.einsum(
        "hqk,khd->qhd", grad_scores, keys, preferred_element_type=jnp.float32
    ) * HEAD ** (-0.5)
    grad_k = jnp.einsum(
        "hqk,qhd->khd", grad_scores, query_rows, preferred_element_type=jnp.float32
    ) * HEAD ** (-0.5)
    value_gradient = jnp.einsum(
        "hqk,qhd->khd", probs.astype(jnp.bfloat16), grad_mixed, preferred_element_type=jnp.float32
    )
    return (
        query_gradient.astype(jnp.bfloat16),
        grad_k.astype(jnp.bfloat16),
        value_gradient.astype(jnp.bfloat16),
    )


def reduce_adapters(part_a, second_portion):
    return (lax.psum(part_a, ("dp", "tensor")), lax.psum(second_portion, "dp"))


def plain_body(
    activations,
    starts,
    attention_weights,
    projection_weight,
    feedforward_weight,
    output_weight,
    norm_gains,
    norm_biases,
    output_biases,
    query_value_bias,
    feedforward_bias,
    adapter_down_weight,
    adapter_up_weight,
):
    section = lax.axis_index("section")
    first = section == 0
    batches = activations.shape[1]
    own_rows = activations.shape[2]
    width = activations.shape[3]
    head_cols = projection_weight.shape[1]
    local_heads = head_cols // HEAD
    shaped = (-1, SEQ_LEN, local_heads, HEAD)
    w_cat = jnp.concatenate(
        [attention_weights[0, 0], attention_weights[0, 1], attention_weights[0, 2]], axis=1
    )
    stacked_down_maps = jnp.concatenate(
        [adapter_down_weight[0, 0], adapter_down_weight[0, 1]], axis=1
    )

    def forward_relay(rows, group_starts):
        normalized_rows = layer_norm(rows, norm_gains[0, 0], norm_biases[0, 0]).astype(jnp.bfloat16)
        gathered = lax.all_gather(normalized_rows, "tensor", axis=0, tiled=True)
        joined = jnp.dot(gathered, w_cat, preferred_element_type=jnp.float32)
        apply_adapter = jnp.dot(
            gathered, stacked_down_maps, preferred_element_type=jnp.float32
        ).astype(jnp.bfloat16)
        query_rows = (
            joined[:, :head_cols]
            + query_value_bias[0, 0]
            + adapter_scale
            * jnp.dot(
                apply_adapter[:, :ADAPTER_RANK],
                adapter_up_weight[0, 0],
                preferred_element_type=jnp.float32,
            )
        ).astype(jnp.bfloat16)
        keys = joined[:, head_cols : 2 * head_cols].astype(jnp.bfloat16)
        value_rows = (
            joined[:, 2 * head_cols :]
            + query_value_bias[0, 1]
            + adapter_scale
            * jnp.dot(
                apply_adapter[:, ADAPTER_RANK:],
                adapter_up_weight[0, 1],
                preferred_element_type=jnp.float32,
            )
        ).astype(jnp.bfloat16)
        mixed, log_totals = lax.map(
            attend,
            (
                query_rows.reshape(shaped),
                keys.reshape(shaped),
                value_rows.reshape(shaped),
                group_starts,
            ),
        )
        mixed = mixed.reshape(-1, head_cols)
        middle = (
            rows
            + lax.psum_scatter(
                jnp.dot(mixed, projection_weight[0], preferred_element_type=jnp.float32),
                "tensor",
                scatter_dimension=0,
                tiled=True,
            )
            + output_biases[0, 0]
        )
        normed_two = layer_norm(middle, norm_gains[0, 1], norm_biases[0, 1]).astype(jnp.bfloat16)
        hidden = (
            jnp.dot(
                lax.all_gather(normed_two, "tensor", axis=0, tiled=True),
                feedforward_weight[0],
                preferred_element_type=jnp.float32,
            )
            + feedforward_bias[0]
        )
        active = gelu_tanh(hidden).astype(jnp.bfloat16)
        output = (
            middle
            + lax.psum_scatter(
                jnp.dot(active, output_weight[0], preferred_element_type=jnp.float32).astype(
                    jnp.bfloat16
                ),
                "tensor",
                scatter_dimension=0,
                tiled=True,
            ).astype(jnp.float32)
            + output_biases[0, 1]
        )
        return (
            output,
            (
                rows,
                middle,
                gathered,
                apply_adapter,
                query_rows,
                keys,
                value_rows,
                log_totals,
                hidden,
            ),
        )

    def backward_relay(grad_rows, cache, group_starts):
        rows, middle, gathered, apply_adapter, query_rows, keys, value_rows, log_totals, hidden = (
            cache
        )
        grad_active = contract_axes(
            lax.all_gather(grad_rows.astype(jnp.bfloat16), "tensor", axis=0, tiled=True),
            output_weight[0],
            1,
            1,
        )
        _, gelu_back = jax.vjp(gelu_tanh, hidden)
        grad_hidden = gelu_back(grad_active)[0].astype(jnp.bfloat16)
        grad_normed_two = lax.psum_scatter(
            contract_axes(grad_hidden, feedforward_weight[0], 1, 1).astype(jnp.bfloat16),
            "tensor",
            scatter_dimension=0,
            tiled=True,
        ).astype(jnp.float32)
        _, norm_two_back = jax.vjp(
            lambda inner_rows: layer_norm(inner_rows, norm_gains[0, 1], norm_biases[0, 1]), middle
        )
        grad_middle = grad_rows + norm_two_back(grad_normed_two)[0]
        grad_mixed = contract_axes(
            lax.all_gather(grad_middle.astype(jnp.bfloat16), "tensor", axis=0, tiled=True),
            projection_weight[0],
            1,
            1,
        ).astype(jnp.bfloat16)
        query_gradient, grad_k, value_gradient = lax.map(
            attend_back,
            (
                query_rows.reshape(shaped),
                keys.reshape(shaped),
                value_rows.reshape(shaped),
                group_starts,
                log_totals,
                grad_mixed.reshape(shaped),
            ),
        )
        query_gradient = query_gradient.reshape(-1, head_cols)
        grad_k = grad_k.reshape(-1, head_cols)
        value_gradient = value_gradient.reshape(-1, head_cols)
        grad_low = jnp.concatenate(
            [
                adapter_scale * contract_axes(query_gradient, adapter_up_weight[0, 0], 1, 1),
                adapter_scale * contract_axes(value_gradient, adapter_up_weight[0, 1], 1, 1),
            ],
            axis=1,
        ).astype(jnp.bfloat16)
        grad_joined = jnp.concatenate([query_gradient, grad_k, value_gradient], axis=1)
        grad_normed = lax.psum_scatter(
            (
                contract_axes(grad_joined, w_cat, 1, 1)
                + contract_axes(grad_low, stacked_down_maps, 1, 1)
            ).astype(jnp.bfloat16),
            "tensor",
            scatter_dimension=0,
            tiled=True,
        ).astype(jnp.float32)
        _, norm_back = jax.vjp(
            lambda inner_rows: layer_norm(inner_rows, norm_gains[0, 0], norm_biases[0, 0]), rows
        )
        grad_in = grad_middle + norm_back(grad_normed)[0]
        grad_down = contract_axes(gathered, grad_low, 0, 0)
        part_a = jnp.stack([grad_down[:, :ADAPTER_RANK], grad_down[:, ADAPTER_RANK:]])
        second_portion = adapter_scale * jnp.stack(
            [
                contract_axes(apply_adapter[:, :ADAPTER_RANK], query_gradient, 0, 0),
                contract_axes(apply_adapter[:, ADAPTER_RANK:], value_gradient, 0, 0),
            ]
        )
        return (grad_in, part_a, second_portion)

    received = jnp.zeros((own_rows, width), jnp.bfloat16)
    finals = []
    stored = []
    for tick in range(batches + 1):
        batch_index = jnp.clip(tick - section, 0, batches - 1)
        own = lax.dynamic_index_in_dim(activations[0], batch_index, 0, keepdims=False)
        rows = jnp.where(first, own, received).astype(jnp.float32)
        group_starts = lax.dynamic_index_in_dim(starts, batch_index, 0, keepdims=False)
        output, cache = forward_relay(rows, group_starts)
        finals.append(output)
        stored.append(rows)
        if tick < batches:
            received = from_behind(output.astype(jnp.bfloat16), "section", 1)
    stacked = jax.tree.map(lambda *items: jnp.stack(items), *stored)
    returned = jnp.zeros((own_rows, width), jnp.bfloat16)
    totals_a = jnp.zeros((2, width, ADAPTER_RANK), jnp.float32)
    totals_b = jnp.zeros((2, ADAPTER_RANK, head_cols), jnp.float32)
    grads_in = []
    for tick in range(batches + 1):
        position = tick - 1 + section
        batch_index = jnp.clip(position, 0, batches - 1)
        valid = ((position >= 0) & (position < batches)).astype(jnp.float32)
        own = lax.dynamic_index_in_dim(activations[0], batch_index, 0, keepdims=False)
        grad_rows = jnp.where(first, returned, own).astype(jnp.float32) * valid
        group_starts = lax.dynamic_index_in_dim(starts, batch_index, 0, keepdims=False)
        slot_index = jnp.clip(tick - 1 + 2 * section, 0, batches)
        picked = lax.dynamic_index_in_dim(stacked, slot_index, 0, keepdims=False)
        _, cache = forward_relay(picked, group_starts)
        grad_in, part_a, second_portion = backward_relay(grad_rows, cache, group_starts)
        grads_in.append(grad_in)
        if tick < batches:
            returned = from_behind(grad_in.astype(jnp.bfloat16), "section", -1)
        part_a, second_portion = reduce_adapters(part_a, second_portion)
        totals_a = totals_a + part_a
        totals_b = totals_b + second_portion
    combined = jnp.stack(
        [jnp.where(first, grads_in[index + 1], finals[index + 1]) for index in range(batches)]
    )
    return (combined[None], totals_a[None], totals_b[None])


LOW = 2 * ADAPTER_RANK
VMEM_SPACE = pl.BlockSpec(memory_space=pltpu.VMEM)
SMEM_SPACE = pl.BlockSpec(memory_space=pltpu.SMEM)
HBM_SPACE = pl.BlockSpec(memory_space=pltpu.HBM)
BLOCK = 256
CHUNK = 2 * BLOCK


def send(block, route):
    pairs = []
    for s in range(2):
        for t in range(4):
            to = route(s, t)
            if to is not None:
                pairs.append((s * 4 + t, to[0] * 4 + to[1]))
    return lax.ppermute(block, ("section", "tensor"), pairs)


def other_core(block):
    return send(block, lambda s, t: (1 - s, t))


def x_swap(block):
    return send(block, lambda s, t: (s, t ^ 1))


def y_swap(block):
    return send(block, lambda s, t: (s, t ^ 2))


def after(value, *others):
    return lax.optimization_barrier((value, others))[0]


def cross_send(block, source=0):
    return send(block, lambda s, t: (t >> 1, t ^ 2) if s == source else None)


def collect(target, same_chip, cross_chip):
    return (
        send(same_chip, lambda s, t: (target, t) if s == t & 1 and s != target else None),
        send(cross_chip, lambda s, t: (target, t ^ 2) if s == t & 1 else None),
    )


def mm(left, right):
    return jnp.dot(left, right, preferred_element_type=jnp.float32)


def mm_nt(left, right):
    return contract_axes(left, right, 1, 1)


def norm_back(rows, gain, grad):
    mean = jnp.mean(rows, axis=-1, keepdims=True)
    centered = rows - mean
    scale = lax.rsqrt(jnp.mean(centered * centered, axis=-1, keepdims=True) + 1e-05)
    unit = centered * scale
    scaled = grad * gain
    return scale * (
        scaled
        - jnp.mean(scaled, axis=-1, keepdims=True)
        - unit * jnp.mean(scaled * unit, axis=-1, keepdims=True)
    )


def gelu_both(value):
    square = value * value
    bent = jnp.tanh(0.7978845608028654 * value * (1.0 + 0.044715 * square))
    half = 0.5 * (1.0 + bent)
    slope = half + 0.5 * value * (1.0 - bent * bent) * (
        0.7978845608028654 * (1.0 + 3.0 * 0.044715 * square)
    )
    return value * half, slope


def cost(flops, read):
    return pl.CostEstimate(flops=1000, bytes_accessed=1000, transcendentals=0)


def kernel_params(mib):
    return pltpu.CompilerParams(vmem_limit_bytes=mib * 1024 * 1024)


def position_mask(meta, query_block, key_block):
    shape = (BLOCK, BLOCK)
    key_pos = key_block * BLOCK + lax.broadcasted_iota(jnp.int32, shape, 0)
    query_pos = query_block * BLOCK + lax.broadcasted_iota(jnp.int32, (1, BLOCK), 1)
    low = jnp.zeros((1, BLOCK), jnp.int32)
    for c in range(4):
        first = meta[4 + c]
        low = jnp.where(first <= query_pos, jnp.maximum(low, first), low)
    valid = key_pos >= low
    if query_block == key_block:
        valid = valid & (key_pos <= query_pos)
    return valid


def lay_mask(meta, chunk, target):
    for i in range(2):
        for j in range(2 * chunk + i + 1):
            target[tile(chunk, i, j)] = jnp.where(
                position_mask(meta, 2 * chunk + i, j), 0.0, -1e30
            )


def tile(chunk, i, j):
    return i * (2 * chunk + 1) + j


def head_lanes(half):
    return (lax.broadcasted_iota(jnp.int32, (1, 2 * HEAD), 1) // HEAD) == half


def start_pick(choices, target, sem):
    for condition, source in choices:

        @pl.when(condition)
        def _(source=source):
            pltpu.make_async_copy(source, target, sem).start()


def load_qkv_weight(layer, meta, pieces, w_buf, sem):
    own, other, lead, trail = pieces
    s, y, w = meta[0], meta[2], meta[8]
    start_pick(
        (((s == y) & (s == layer), own), ((s == y) & (s != layer), other)), w_buf, sem
    )

    @pl.when(s != y)
    def _():
        for part, side in ((lead, w), (trail, 1 - w)):
            pltpu.make_async_copy(part, w_buf.at[pl.ds(2 * side, 2)], sem).start()

    return pltpu.make_async_copy(own, w_buf, sem)


def half_rows(core):
    return pl.ds(pl.multiple_of(core * BLOCK, BLOCK), BLOCK)


def lay_out(meta, own, near, target):
    s = meta[0]
    target[half_rows(s), :] = own[...]
    target[half_rows(1 - s), :] = near[...]


def share_out(meta, source, keep, give):
    s = meta[0]
    keep[...] = source[half_rows(s), :]
    give[...] = source[half_rows(1 - s), :]


def attend_kernel(layer, chunk, meta, shared, varied, own, near, *rest):
    before, rest = rest[: 2 * chunk], rest[2 * chunk :]
    q_out, k_out, v_out, lse_out, mixed_out, keep, give = rest[4:11]
    (
        n_buf, w_buf, score_buf, mask_buf, vt_buf, q_ref, k_ref, v_ref, lse_ref, mixed_ref, sem,
        out_sems,
    ) = rest[11:]
    loaded = load_qkv_weight(layer, meta, rest[:4], w_buf, sem)
    down = shared[layer, 8:16, :].astype(jnp.bfloat16)
    bias = varied[layer, 1:2, :]
    up = varied[layer, 8:16, 0:512].astype(jnp.bfloat16)
    lay_out(meta, own, near, n_buf)
    lay_mask(meta, chunk, mask_buf)
    keys = [k_ref] if chunk == 0 else [before[0], k_ref]
    if chunk == 1:
        for b in range(2):
            span = slice(b * BLOCK, (b + 1) * BLOCK)
            vt_buf[:, span] = before[1][span, :].T
    loaded.wait()
    normed = n_buf[...]
    low = mm_nt(normed, down).astype(jnp.bfloat16)
    lifted = adapter_scale * mm(low, up)
    q_ref[...] = (mm(normed, w_buf[0]) + bias[:, 0:256] + lifted[:, 0:256]).astype(jnp.bfloat16)
    k_ref[...] = mm(normed, w_buf[1]).astype(jnp.bfloat16)
    v_ref[...] = (mm(normed, w_buf[2]) + bias[:, 256:512] + lifted[:, 256:512]).astype(jnp.bfloat16)
    saved = [
        pltpu.make_async_copy(source, target, out_sems.at[i])
        for i, (source, target) in enumerate(
            (
                (q_ref, q_out), (k_ref, k_out), (v_ref, v_out), (lse_ref, lse_out),
                (mixed_ref, mixed_out),
            )
        )
    ]
    for copy in saved[:3]:
        copy.start()
    for b in range(2):
        span = slice(b * BLOCK, (b + 1) * BLOCK)
        vt_buf[:, chunk * CHUNK + b * BLOCK : chunk * CHUNK + (b + 1) * BLOCK] = v_ref[span, :].T

    def one_head(head, carry):
        lanes = pl.ds(pl.multiple_of((head // 2) * 128, 128), 128)
        chosen = head_lanes(head % 2)
        deep = pl.ds(pl.multiple_of(head * HEAD, HEAD), HEAD)
        for i in range(2):
            span = slice(i * BLOCK, (i + 1) * BLOCK)
            place = 2 * chunk + i
            query = jnp.where(chosen, q_ref[span, lanes] * HEAD ** (-0.5), 0.0).astype(jnp.bfloat16)
            top = jnp.full((1, BLOCK), -1e30, jnp.float32)
            for j in range(place + 1):
                rows = slice((j % 2) * BLOCK, (j % 2 + 1) * BLOCK)
                scores = mm_nt(keys[j // 2][rows, lanes], query) + mask_buf[tile(chunk, i, j)]
                score_buf[j] = scores
                top = jnp.maximum(top, jnp.max(scores, axis=0, keepdims=True))
            total = jnp.zeros((1, BLOCK), jnp.float32)
            mixed = jnp.zeros((HEAD, BLOCK), jnp.float32)
            for j in range(place + 1):
                weights = jnp.exp(score_buf[j] - top)
                total = total + jnp.sum(weights, axis=0, keepdims=True)
                mixed = mixed + mm(
                    vt_buf[deep, j * BLOCK : (j + 1) * BLOCK], weights.astype(jnp.bfloat16)
                )
            mixed_ref[deep, span] = mixed / total
            lse_ref[pl.ds(head, 1), span] = top + jnp.log(total)
        return carry

    lax.fori_loop(0, 4, one_head, 0, unroll=4)
    for copy in saved[3:]:
        copy.start()
    for b in range(2):
        span = slice(b * BLOCK, (b + 1) * BLOCK)
        n_buf[span, :] = mm_nt(
            mixed_ref[:, span].T.astype(jnp.bfloat16), w_buf[3]
        ).astype(jnp.bfloat16)
    share_out(meta, n_buf, keep, give)
    for copy in saved:
        copy.wait()


def attend_call(layer, chunk, meta, blocks, before, shared, varied, weight):
    bf, f32 = jnp.bfloat16, jnp.float32
    wide = jax.ShapeDtypeStruct((CHUNK, 256), bf)
    piece = jax.ShapeDtypeStruct((BLOCK, 1024), bf)
    *saved, keep, give = pl.pallas_call(
        functools.partial(attend_kernel, layer, chunk),
        in_specs=[SMEM_SPACE] + [VMEM_SPACE] * (4 + 2 * chunk) + [HBM_SPACE] * 4,
        out_specs=[HBM_SPACE] * 5 + [VMEM_SPACE] * 2,
        out_shape=[wide, wide, wide, jax.ShapeDtypeStruct((8, CHUNK), f32),
                   jax.ShapeDtypeStruct((256, CHUNK), f32), piece, piece],
        scratch_shapes=[
            pltpu.VMEM((CHUNK, 1024), bf),
            pltpu.VMEM((4, 1024, 256), bf),
            pltpu.VMEM((2 + 2 * chunk, BLOCK, BLOCK), f32),
            pltpu.VMEM((3 + 4 * chunk, BLOCK, BLOCK), f32),
            pltpu.VMEM((256, CHUNK * (1 + chunk)), bf),
            pltpu.VMEM((CHUNK, 256), bf),
            pltpu.VMEM((CHUNK, 256), bf),
            pltpu.VMEM((CHUNK, 256), bf),
            pltpu.VMEM((8, CHUNK), f32),
            pltpu.VMEM((256, CHUNK), f32),
            pltpu.SemaphoreType.DMA,
            pltpu.SemaphoreType.DMA((5,)),
        ],
        compiler_params=kernel_params(24),
        cost_estimate=cost(3.5e9, 8e6),
        name="attention_forward_%d" % chunk,
    )(meta, shared, varied, *blocks, *(before if chunk else ()), *weight)
    return saved, keep, give


def attend_back_kernel(layer, chunk, meta, shared, varied, n_own, n_near, g_own, g_near, *rest):
    n_saved = 5 + 2 * chunk
    saved, rest = rest[:n_saved], rest[n_saved:]
    saved_sems, rest = rest[-1], rest[:-1]
    bufs, rest = rest[-n_saved:], rest[:-n_saved]
    fetches = [
        pltpu.make_async_copy(source, target, saved_sems.at[i])
        for i, (source, target) in enumerate(zip(saved, bufs))
    ]
    for fetch in fetches:
        fetch.start()
    q_ref, lse_ref, mixed_ref = bufs[:3]
    keys, values = bufs[3 : 4 + chunk], bufs[4 + chunk :]
    if chunk == 0:
        dk_in, dv_in, down_in, up_in = rest[:4]
        keep, give, down_ref, up_ref = rest[8:12]
        weight, scratch = rest[4:8], rest[12:]
    else:
        keep, give, down_ref, up_ref, dk_out, dv_out = rest[4:10]
        weight, scratch = rest[:4], rest[10:]
    (
        n_buf, g_buf, w_buf, mask_buf, kt_buf, do_buf, delta_buf, dqt_buf, dk_buf, dv_buf, dq_buf,
        sem,
    ) = scratch
    loaded = load_qkv_weight(layer, meta, weight, w_buf, sem)
    lay_out(meta, g_own, g_near, g_buf)
    lay_out(meta, n_own, n_near, n_buf)
    lay_mask(meta, chunk, mask_buf)
    for fetch in fetches:
        fetch.wait()
    for j in range(2 + 2 * chunk):
        rows = slice((j % 2) * BLOCK, (j % 2 + 1) * BLOCK)
        kt_buf[:, j * BLOCK : (j + 1) * BLOCK] = keys[j // 2][rows, :].T
    if chunk == 0:
        dk_buf[...] = dk_in[...]
        dv_buf[...] = dv_in[...]
    else:
        dk_buf[...] = jnp.zeros_like(dk_buf)
        dv_buf[...] = jnp.zeros_like(dv_buf)
    loaded.wait()
    do_buf[...] = mm(g_buf[...], w_buf[3]).astype(jnp.bfloat16)
    for b in range(2):
        span = slice(b * BLOCK, (b + 1) * BLOCK)
        product = do_buf[span, :].astype(jnp.float32).T * mixed_ref[:, span]
        for head in range(4):
            delta_buf[head : head + 1, span] = jnp.sum(
                product[head * HEAD : (head + 1) * HEAD], axis=0, keepdims=True
            )

    def one_head(head, carry):
        lanes = pl.ds(pl.multiple_of((head // 2) * 128, 128), 128)
        chosen = head_lanes(head % 2)
        deep = pl.ds(pl.multiple_of(head * HEAD, HEAD), HEAD)
        for i in range(2):
            span = slice(i * BLOCK, (i + 1) * BLOCK)
            place = 2 * chunk + i
            query = jnp.where(chosen, q_ref[span, lanes] * HEAD ** (-0.5), 0.0).astype(jnp.bfloat16)
            grad_mixed = jnp.where(chosen, do_buf[span, lanes], 0.0).astype(jnp.bfloat16)
            lse = lse_ref[pl.ds(head, 1), span]
            delta = delta_buf[pl.ds(head, 1), span]
            grad_query = jnp.zeros((HEAD, BLOCK), jnp.float32)
            for j in range(place + 1):
                rows = slice((j % 2) * BLOCK, (j % 2 + 1) * BLOCK)
                all_rows = slice(j * BLOCK, (j + 1) * BLOCK)
                scores = mm_nt(keys[j // 2][rows, lanes], query) + mask_buf[tile(chunk, i, j)]
                probs = jnp.exp(scores - lse)
                grad_probs = mm_nt(values[j // 2][rows, lanes], grad_mixed)
                grad_scores = (probs * (grad_probs - delta)).astype(jnp.bfloat16)
                dv_buf[all_rows, lanes] += mm(probs.astype(jnp.bfloat16), grad_mixed)
                dk_buf[all_rows, lanes] += mm(grad_scores, query)
                grad_query = grad_query + mm(kt_buf[deep, all_rows], grad_scores)
            dqt_buf[deep, span] = grad_query * HEAD ** (-0.5)
        return carry

    lax.fori_loop(0, 4, one_head, 0, unroll=4)
    down = shared[layer, 8:16, :].astype(jnp.bfloat16)
    up = varied[layer, 8:16, 0:512].astype(jnp.bfloat16)
    for b in range(2):
        span = slice(b * BLOCK, (b + 1) * BLOCK)
        dq_buf[span, :] = dqt_buf[:, span].T.astype(jnp.bfloat16)
    done = slice(chunk * CHUNK, (chunk + 1) * CHUNK)
    normed = n_buf[...]
    grad_q = dq_buf[...]
    grad_k = dk_buf[done, :].astype(jnp.bfloat16)
    grad_v = dv_buf[done, :].astype(jnp.bfloat16)
    both = jnp.concatenate([grad_q, grad_v], axis=1)
    low_grad = (adapter_scale * mm_nt(both, up)).astype(jnp.bfloat16)
    low_grad_t = (adapter_scale * mm_nt(up, both)).astype(jnp.bfloat16)
    low_t = mm_nt(down, normed).astype(jnp.bfloat16)
    g_buf[...] = (
        mm_nt(grad_q, w_buf[0]) + mm_nt(grad_k, w_buf[1]) + mm_nt(grad_v, w_buf[2])
        + mm(low_grad, down)
    ).astype(jnp.bfloat16)
    share_out(meta, g_buf, keep, give)
    total_down = mm(low_grad_t, normed)
    total_up = adapter_scale * mm(low_t, both)
    if chunk == 0:
        total_down = total_down + down_in[...]
        total_up = total_up + up_in[...]
    else:
        dk_out[...] = dk_buf[0:CHUNK, :]
        dv_out[...] = dv_buf[0:CHUNK, :]
    down_ref[...] = total_down
    up_ref[...] = total_up


def attend_back_call(layer, chunk, meta, blocks, grads, saved, carried, shared, varied, weight):
    bf, f32 = jnp.bfloat16, jnp.float32
    piece = jax.ShapeDtypeStruct((BLOCK, 1024), bf)
    tall = jax.ShapeDtypeStruct((CHUNK, 256), f32)
    spans = CHUNK * (1 + chunk)
    q, _, _, lse, mixed = saved[chunk]
    keys = [one[1] for one in saved[: chunk + 1]]
    values = [one[2] for one in saved[: chunk + 1]]
    held = (q, lse, mixed, *keys, *values)
    inputs = (shared, varied, *blocks, *grads, *held, *carried)
    return pl.pallas_call(
        functools.partial(attend_back_kernel, layer, chunk),
        in_specs=[SMEM_SPACE] + [VMEM_SPACE] * 6 + [HBM_SPACE] * len(held)
        + [VMEM_SPACE] * len(carried) + [HBM_SPACE] * 4,
        out_specs=[VMEM_SPACE] * (4 + 2 * chunk),
        out_shape=[piece, piece, jax.ShapeDtypeStruct((LOW, 1024), f32),
                   jax.ShapeDtypeStruct((LOW, 512), f32)] + [tall] * (2 * chunk),
        scratch_shapes=[
            pltpu.VMEM((CHUNK, 1024), bf),
            pltpu.VMEM((CHUNK, 1024), bf),
            pltpu.VMEM((4, 1024, 256), bf),
            pltpu.VMEM((3 + 4 * chunk, BLOCK, BLOCK), f32),
            pltpu.VMEM((256, spans), bf),
            pltpu.VMEM((CHUNK, 256), bf),
            pltpu.VMEM((8, CHUNK), f32),
            pltpu.VMEM((256, CHUNK), f32),
            pltpu.VMEM((spans, 256), f32),
            pltpu.VMEM((spans, 256), f32),
            pltpu.VMEM((CHUNK, 256), bf),
            pltpu.SemaphoreType.DMA,
            *[pltpu.VMEM(one.shape, one.dtype) for one in held],
            pltpu.SemaphoreType.DMA((len(held),)),
        ],
        compiler_params=kernel_params(24),
        cost_estimate=cost(6e9, 12e6),
        name="attention_backward_%d" % chunk,
    )(meta, *inputs, *weight)


def summed(passed, far):
    return passed[...].astype(jnp.float32) + far[...].astype(jnp.float32)


def rows_middle_kernel(layer, h_ref, passed, far, shared, middle_ref, normed_ref):
    middle = h_ref[...].astype(jnp.float32) + summed(passed, far) + shared[layer, 4:5, :]
    middle_ref[...] = middle
    normed_ref[...] = layer_norm(middle, shared[layer, 1:2, :], shared[layer, 3:4, :]).astype(
        jnp.bfloat16
    )


def load_units(layer, meta, pieces, w1, w2, sems):
    own, other, (lead, trail) = pieces[0:2], pieces[2:4], pieces[4:6]
    s, y, w = meta[0], meta[2], meta[8]
    copies = []
    for m, matrix in enumerate((w1, w2)):
        start_pick(
            (
                ((s == y) & (s == layer), own[m]),
                ((s == y) & (s != layer), other[m]),
                ((s != y) & (w == m), lead),
                ((s != y) & (w != m), trail),
            ),
            matrix,
            sems.at[m],
        )
        copies.append(pltpu.make_async_copy(own[m], matrix, sems.at[m]))
    return copies


def stack_rows(blocks, target):
    for i, block in enumerate(blocks):
        target[i * BLOCK : (i + 1) * BLOCK, :] = block[...]


def halve(total, keep, give):
    keep[...] = total[:BLOCK].astype(jnp.bfloat16)
    give[...] = total[BLOCK:].astype(jnp.bfloat16)


def units_kernel(layer, meta, n0, n1, bias, *rest):
    keep, give, slope_out, w1, w2, sems, n_buf, slope_buf, out_sem = rest[6:]
    waits = load_units(layer, meta, rest[:6], w1, w2, sems)
    stack_rows((n0, n1), n_buf)
    waits[0].wait()
    active, slope = gelu_both(mm(n_buf[...], w1[...]) + bias[layer, 0:1, :])
    slope_buf[...] = slope.astype(jnp.bfloat16)
    saving = pltpu.make_async_copy(slope_buf, slope_out, out_sem)
    saving.start()
    waits[1].wait()
    halve(mm(active.astype(jnp.bfloat16), w2[...]), keep, give)
    saving.wait()


def units_turn_kernel(layer, meta, n0, n1, g0, g1, bias, *rest):
    keep, give, out_keep, out_give, w1, w2, sems, n_buf, g_buf = rest[6:]
    waits = load_units(layer, meta, rest[:6], w1, w2, sems)
    stack_rows((n0, n1), n_buf)
    stack_rows((g0, g1), g_buf)
    for copy in waits:
        copy.wait()
    active, slope = gelu_both(mm(n_buf[...], w1[...]) + bias[layer, 0:1, :])
    grad_hidden = (mm_nt(g_buf[...], w2[...]) * slope).astype(jnp.bfloat16)
    halve(mm_nt(grad_hidden, w1[...]), keep, give)
    halve(mm(active.astype(jnp.bfloat16), w2[...]), out_keep, out_give)


def units_back_kernel(layer, meta, g0, g1, slope_in, *rest):
    keep, give, w1, w2, sems, g_buf, slope_buf, in_sem = rest[6:]
    waits = load_units(layer, meta, rest[:6], w1, w2, sems)
    fetch = pltpu.make_async_copy(slope_in, slope_buf, in_sem)
    fetch.start()
    stack_rows((g0, g1), g_buf)
    waits[1].wait()
    fetch.wait()
    grad = (mm_nt(g_buf[...], w2[...]) * slope_buf[...].astype(jnp.float32)).astype(jnp.bfloat16)
    waits[0].wait()
    halve(mm_nt(grad, w1[...]), keep, give)


def rows_first_kernel(meta, mine, crossed, far_mine, far_crossed, shared, *outs):
    holder = meta[0] == meta[1]
    upper = meta[2] == 0
    first = jnp.where(holder, mine[...], far_mine[...])
    second = jnp.where(holder, crossed[...], far_crossed[...])
    for c, (one, other) in enumerate(((first, second), (second, first))):
        rows = jnp.where(upper, one, other)
        outs[c][...] = rows
        outs[2 + c][...] = layer_norm(
            rows.astype(jnp.float32), shared[0, 0:1, :], shared[0, 2:3, :]
        ).astype(jnp.bfloat16)


def rows_next_kernel(middle, passed, far, shared, between_ref, normed_ref):
    between = (middle[...] + summed(passed, far) + shared[0, 5:6, :]).astype(jnp.bfloat16)
    between_ref[...] = between
    normed_ref[...] = layer_norm(
        between.astype(jnp.float32), shared[1, 0:1, :], shared[1, 2:3, :]
    ).astype(jnp.bfloat16)


def rows_turn_kernel(layer, middle, g_ref, passed, far, shared, grad_ref, sent_ref):
    grad_middle = g_ref[...].astype(jnp.float32) + norm_back(
        middle[...], shared[layer, 1:2, :], summed(passed, far)
    )
    grad_ref[...] = grad_middle
    sent_ref[...] = grad_middle.astype(jnp.bfloat16)


def rows_before_kernel(gm_ref, passed, far, between_ref, shared, grad_ref):
    grad_rows = gm_ref[...] + norm_back(
        between_ref[...].astype(jnp.float32), shared[1, 0:1, :], summed(passed, far)
    )
    grad_ref[...] = grad_rows.astype(jnp.bfloat16)


def rows_output_kernel(middle, passed, far, shared, wide_ref, narrow_ref):
    total = middle[...] + summed(passed, far) + shared[1, 5:6, :]
    wide_ref[...] = total
    narrow_ref[...] = total.astype(jnp.bfloat16)


def rows_final_kernel(gm_ref, passed, far, h_ref, shared, wide_ref, narrow_ref):
    grad_in = gm_ref[...] + norm_back(
        h_ref[...].astype(jnp.float32), shared[0, 0:1, :], summed(passed, far)
    )
    wide_ref[...] = grad_in
    narrow_ref[...] = grad_in.astype(jnp.bfloat16)


def units_call(kernel, meta, small, saved, weights, outs, saving, scratch, name):
    return pl.pallas_call(
        kernel,
        in_specs=[SMEM_SPACE] + [VMEM_SPACE] * len(small) + [HBM_SPACE] * (len(saved) + len(weights)),
        out_specs=[VMEM_SPACE] * len(outs) + [HBM_SPACE] * len(saving),
        out_shape=[*outs, *saving],
        scratch_shapes=scratch,
        compiler_params=kernel_params(24),
        cost_estimate=cost(2e9, 8e6),
        name=name,
    )(meta, *small, *saved, *weights)


def plain_call(kernel, scalar, small, large, outs, scratch, flops, name):
    specs = [VMEM_SPACE] * len(small) + [HBM_SPACE] * len(large)
    operands = (*small, *large)
    if scalar is not None:
        specs, operands = [SMEM_SPACE] + specs, (scalar, *operands)
    return pl.pallas_call(
        kernel,
        in_specs=specs,
        out_specs=[VMEM_SPACE] * len(outs),
        out_shape=outs,
        scratch_shapes=scratch,
        compiler_params=kernel_params(24),
        cost_estimate=cost(flops, 8e6),
        name=name,
    )(*operands)


def deal_rows(source, slots, section, y):
    same = lax.dynamic_index_in_dim(slots, y, 0, keepdims=False)
    cross = lax.dynamic_index_in_dim(slots, 1 - y, 0, keepdims=False)
    moved = send(same, lambda s, t: (t & 1, t) if s == source and s != t & 1 else None)
    crossed = send(cross, lambda s, t: (t & 1, t ^ 2) if s == source else None)
    mine = jnp.where(section == source, same, moved)
    return mine, crossed


def to_x(block):
    return send(block, lambda s, t: (s, t ^ 1) if s == t & 1 else None)


def from_x(block):
    return send(block, lambda s, t: (s, t ^ 1) if s != t & 1 else None)


def z_swap(block):
    size = lax.axis_size("dp")
    pairs = [
        ((s * size + z) * 4 + t, (s * size + (z ^ 1)) * 4 + t)
        for s in range(2) for z in range(size) for t in range(4) if s != t >> 1
    ]
    return lax.ppermute(block, ("section", "dp", "tensor"), pairs)


def chip_sum(keep, give, last, swap=x_swap):
    take = other_core(after(give, last))
    passed = (keep.astype(jnp.float32) + take.astype(jnp.float32)).astype(jnp.bfloat16)
    return passed, swap(passed)


def total_over_z(downs, ups):
    both = jnp.concatenate([jnp.concatenate(downs), jnp.concatenate(ups)], axis=1)
    size = lax.axis_size("dp")
    step = 1
    while step < size:
        both = both + lax.ppermute(both, "dp", [(i, i ^ step) for i in range(size)])
        step *= 2
    return both


def total_over_cores(both, section, y):
    both = both + y_swap(both)
    moved = other_core(both)
    down = both[:, :1024] + moved[:, :1024]
    down = jnp.where(section == 0, down[:LOW], down[LOW:])
    up = jnp.where(section == y, both[:, 1024:], moved[:, 1024:])
    return down + x_swap(down), jnp.where(section == 0, up[:LOW], up[LOW:])


def relay_body(
    activations, starts, attention_weights, projection_weight, feedforward_weight, output_weight,
    norm_gains, norm_biases, output_biases, query_value_bias, feedforward_bias,
    adapter_down_weight, adapter_up_weight,
):
    bf, f32 = jnp.bfloat16, jnp.float32
    section = lax.axis_index("section")
    place = lax.axis_index("tensor")
    y, x = place // 2, place % 2
    first = section == 0

    mine, crossed = deal_rows(0, activations[0], section, y)
    down_rows = adapter_down_weight[0].astype(f32).transpose(0, 2, 1).reshape(LOW, 1024)
    up0 = adapter_up_weight[0, 0].astype(f32)
    up1 = adapter_up_weight[0, 1].astype(f32)
    zero = jnp.zeros((ADAPTER_RANK, 256), f32)
    common = jnp.concatenate(
        [norm_gains[0], norm_biases[0], output_biases[0], jnp.zeros((2, 1024), f32), down_rows]
    )
    own_part = jnp.concatenate(
        [
            feedforward_bias,
            jnp.pad(query_value_bias[0].reshape(1, 512), ((0, 0), (0, 512))),
            jnp.zeros((6, 1024), f32),
            jnp.concatenate([up0, zero, jnp.zeros((ADAPTER_RANK, 512), f32)], axis=1),
            jnp.concatenate([zero, up1, jnp.zeros((ADAPTER_RANK, 512), f32)], axis=1),
        ]
    )
    partner = other_core(common)
    partner_part = other_core(own_part)
    parts = jnp.where(
        first, jnp.stack([own_part, partner_part]), jnp.stack([partner_part, own_part])
    )
    near_varied = jnp.where(section == y, parts, y_swap(parts))
    shared = jnp.where(first, jnp.stack([common, partner]), jnp.stack([partner, common]))
    meta = jnp.concatenate(
        [
            jnp.stack([section, x, y, place]).astype(jnp.int32),
            lax.dynamic_index_in_dim(starts, y, 0, keepdims=False).reshape(4),
            (lax.axis_index("dp") % 2).astype(jnp.int32)[None],
        ]
    )
    even = lax.axis_index("dp") % 2 == 0
    own_a = jnp.concatenate([attention_weights[0], projection_weight[0].T[None]])
    w1_own, w2_own = feedforward_weight[0], output_weight[0]
    other_a = other_core(own_a)
    g_mine, g_crossed = deal_rows(1, activations[0], section, y)
    mine, crossed, shared, g_mine, g_crossed = lax.optimization_barrier(
        (mine, crossed, shared, g_mine, g_crossed)
    )
    lead_a0 = cross_send(after(jnp.where(even, own_a[:2], own_a[2:]), crossed, near_varied))
    far_mine, far_crossed = to_x(mine), to_x(crossed)
    trail_a0 = z_swap(after(lead_a0, far_mine, far_crossed))

    sheet = jax.ShapeDtypeStruct((BLOCK, 1024), f32)
    thin = jax.ShapeDtypeStruct((BLOCK, 1024), bf)
    slope_shape = jax.ShapeDtypeStruct((CHUNK, 1024), bf)
    matrices = [
        pltpu.VMEM((1024, 1024), bf), pltpu.VMEM((1024, 1024), bf), pltpu.SemaphoreType.DMA((2,))
    ]
    group = pltpu.VMEM((CHUNK, 1024), bf)

    def small(kernel, *operands, outs, name):
        return plain_call(kernel, None, operands, (), outs, [], 1e7, name)

    def attend(layer, chunk, normed, before, weight, near=None):
        near = other_core(normed) if near is None else near
        return attend_call(
            layer, chunk, meta, (normed, near), before, shared, near_varied, weight
        )

    def units(layer, normed, weight):
        return units_call(
            functools.partial(units_kernel, layer), meta, (normed, other_core(normed), near_varied),
            (), weight, [thin, thin], [slope_shape],
            [*matrices, group, group, pltpu.SemaphoreType.DMA], "units",
        )

    def units_turn(layer, normed, grad, near_grad, weight):
        return units_call(
            functools.partial(units_turn_kernel, layer), meta,
            (normed, other_core(normed), grad, near_grad, near_varied), (), weight,
            [thin] * 4, [], [*matrices, group, group], "units_turn",
        )

    def units_back(layer, grad, slope, weight):
        return units_call(
            functools.partial(units_back_kernel, layer), meta, (grad, other_core(grad)), (slope,),
            weight, [thin, thin], [], [*matrices, group, group, pltpu.SemaphoreType.DMA],
            "units_back",
        )

    def middle(layer, rows, sums):
        return small(
            functools.partial(rows_middle_kernel, layer), rows, *sums, shared, outs=[sheet, thin],
            name="rows_middle",
        )

    def turn(layer, middle_rows, grad, sums):
        return small(
            functools.partial(rows_turn_kernel, layer), middle_rows, grad, *sums, shared,
            outs=[sheet, thin], name="rows_turn",
        )

    row0, row1, n0, n1 = plain_call(
        rows_first_kernel, meta, (mine, crossed, far_mine, far_crossed, shared), (), [thin] * 4,
        [], 1e7, "rows_first",
    )
    g_far = [to_x(one) for one in (g_mine, g_crossed)]
    weights_a0 = (own_a, other_a, lead_a0, trail_a0)
    near_n0 = other_core(n0)
    lead_b0 = cross_send(jnp.where(even, *after((w1_own, w2_own), near_n0)))
    n00, n01 = n0, n1
    saved00, keep, give = attend(0, 0, n0, (), weights_a0, near_n0)
    keep, give, g_far = lax.optimization_barrier((keep, give, g_far))
    sum0 = chip_sum(keep, give, lead_a0)
    other_w1, other_w2 = (other_core(after(one, sum0[0])) for one in (w1_own, w2_own))
    trail_b0 = z_swap(after(lead_b0, sum0[0]))
    weights_b0 = (w1_own, w2_own, other_w1, other_w2, lead_b0, trail_b0)
    saved01, keep, give = attend(0, 1, n1, saved00[1:3], weights_a0)
    sum1 = chip_sum(keep, give, sum0[1])
    lead_a1 = cross_send(jnp.where(even, *after((other_a[:2], other_a[2:]), sum0[0])))
    middle00, n0 = middle(0, row0, sum0)
    keep, give, slope0 = units(0, n0, weights_b0)
    sum2 = chip_sum(keep, give, sum1[1])
    sum1, lead_a1 = lax.optimization_barrier((sum1, lead_a1))
    trail_a1 = z_swap(lead_a1)
    lead_b1 = cross_send(jnp.where(even, *after((other_w1, other_w2), lead_a1)))
    middle01, n1 = middle(0, row1, sum1)
    keep, give, slope1 = units(0, n1, weights_b0)
    sum3 = chip_sum(keep, give, sum2[1])
    sum2, trail_a1 = lax.optimization_barrier((sum2, trail_a1))
    weights_a1 = (own_a, other_a, lead_a1, trail_a1)
    between0, n10 = small(rows_next_kernel, middle00, *sum2, shared, outs=[thin, thin], name="rows_next")
    saved10, keep, give = attend(1, 0, n10, (), weights_a1)
    sum4 = chip_sum(keep, give, sum3[1])
    sum3, lead_b1 = lax.optimization_barrier((sum3, lead_b1))
    trail_b1 = z_swap(lead_b1)
    weights_b1 = (w1_own, w2_own, other_w1, other_w2, lead_b1, trail_b1)
    between1, n11 = small(rows_next_kernel, middle01, *sum3, shared, outs=[thin, thin], name="rows_next")
    saved11, keep, give = attend(1, 1, n11, saved10[1:3], weights_a1)
    sum5 = chip_sum(keep, give, sum4[1])
    holder, upper = section == x, y == 0
    mine, crossed = (
        jnp.where(holder, one, two) for one, two in zip((g_mine, g_crossed), after(g_far, sum4[0]))
    )
    grad_outs = (jnp.where(upper, mine, crossed), jnp.where(upper, crossed, mine))
    near_outs = [other_core(one) for one in grad_outs]
    middle10, m0 = middle(1, between0, sum4)
    keep, give, out_keep0, out_give0 = units_turn(1, m0, grad_outs[0], near_outs[0], weights_b1)
    sum6 = chip_sum(keep, give, sum5[1])
    middle11, m1 = middle(1, between1, sum5)
    keep, give, out_keep1, out_give1 = units_turn(1, m1, grad_outs[1], near_outs[1], weights_b1)
    sum7 = chip_sum(keep, give, sum6[1])
    grad_middle10, g0 = turn(1, middle10, grad_outs[0], sum6)
    grad_middle11, g1 = turn(1, middle11, grad_outs[1], sum7)
    keep, give, down1, up1, dk, dv = attend_back_call(
        1, 1, meta, (n11, other_core(n11)), (g1, other_core(g1)), (saved10, saved11), (), shared,
        near_varied, weights_a1,
    )
    out_sums = [
        chip_sum(*after(one, g1), sum7[1], from_x)
        for one in ((out_keep0, out_give0), (out_keep1, out_give1))
    ]
    keep, give, out_sums = lax.optimization_barrier((keep, give, out_sums))
    sum8 = chip_sum(keep, give, sum7[1])
    keep, give, down1, up1 = attend_back_call(
        1, 0, meta, (n10, other_core(n10)), (g0, other_core(g0)), (saved10, saved11),
        (dk, dv, down1, up1), shared, near_varied, weights_a1,
    )
    sum9 = chip_sum(keep, give, sum8[1])
    before1 = small(
        rows_before_kernel, grad_middle11, *after(sum8, keep), between1, shared, outs=[thin], name="rows_before"
    )[0]
    keep, give = units_back(0, before1, slope1, weights_b0)
    sum10 = chip_sum(keep, give, sum9[1])
    before0 = small(
        rows_before_kernel, grad_middle10, *sum9, between0, shared, outs=[thin], name="rows_before"
    )[0]
    keep, give = units_back(0, before0, slope0, weights_b0)
    sum11 = chip_sum(keep, give, sum10[1])
    grad_middle01, h1 = turn(0, middle01, before1, sum10)
    keep, give, down0, up0, dk, dv = attend_back_call(
        0, 1, meta, (n01, other_core(n01)), (h1, other_core(h1)), (saved00, saved01), (), shared,
        near_varied, weights_a0,
    )
    sum12 = chip_sum(keep, give, sum11[1], from_x)
    grad_middle00, h0 = turn(0, middle00, before0, sum11)
    keep, give, down0, up0 = attend_back_call(
        0, 0, meta, (n00, other_core(n00)), (h0, other_core(h0)), (saved00, saved01),
        (dk, dv, down0, up0), shared, near_varied, weights_a0,
    )
    sum13 = chip_sum(keep, give, sum12[1], from_x)
    outs = [
        small(rows_output_kernel, one, *after(two, sum13[0]), shared, outs=[sheet, thin],
              name="rows_output")
        for one, two in zip((middle10, middle11), out_sums)
    ]
    out_wide = jnp.where(upper, outs[0][0], outs[1][0])
    out_same, out_cross = collect(1, out_wide, jnp.where(upper, outs[1][1], outs[0][1]))
    totals = total_over_z((down0, down1), after((up0, up1), sum13[0]))
    sum13, totals = lax.optimization_barrier((sum13, totals))
    ends = [
        small(rows_final_kernel, one, *two, three, shared, outs=[sheet, thin], name="rows_final")
        for one, two, three in ((grad_middle00, sum13, row0), (grad_middle01, sum12, row1))
    ]
    wide = jnp.where(upper, ends[0][0], ends[1][0])
    in_same, in_cross = collect(0, wide, jnp.where(upper, ends[1][1], ends[0][1]))
    grad_down, grad_up = total_over_cores(totals, section, y)
    same = jnp.where(
        first, jnp.where(x == 0, wide, in_same), jnp.where(x == 1, out_wide, out_same)
    )
    cross = jnp.where(first, in_cross, out_cross).astype(f32)
    combined = jnp.where(y == 0, jnp.stack([same, cross]), jnp.stack([cross, same]))
    return (
        combined[None],
        grad_down.reshape(1, 2, ADAPTER_RANK, 1024).transpose(0, 1, 3, 2),
        jnp.stack([grad_up[:ADAPTER_RANK, :256], grad_up[ADAPTER_RANK:, 256:]])[None],
    )


def body(*arrays):
    dp = lax.axis_size("dp")
    known = (
        arrays[0].shape == (1, 2, BLOCK, 1024)
        and lax.axis_size("tensor") == 4
        and lax.axis_size("section") == 2
        and arrays[3].shape == (1, 256, 1024)
        and arrays[5].shape == (1, 1024, 1024)
        and dp & (dp - 1) == 0
    )
    return relay_body(*arrays) if known else plain_body(*arrays)


def solution(mesh):
    placed = (
        P("section", None, ("dp", "tensor"), None),
        P(None, "dp", None),
        P("section", None, None, "tensor"),
        P("section", "tensor", None),
        P("section", None, "tensor"),
        P("section", "tensor", None),
        P("section", None, None),
        P("section", None, None),
        P("section", None, None),
        P("section", None, "tensor"),
        P("section", "tensor"),
        P("section", None, None, None),
        P("section", None, None, "tensor"),
    )
    return jax.shard_map(
        body,
        mesh=mesh,
        in_specs=placed,
        out_specs=(
            P("section", None, ("dp", "tensor"), None),
            P("section", None, None, None),
            P("section", None, None, "tensor"),
        ),
        check_vma=False,
    )
```

```python
import functools

import jax
import jax.numpy as jnp
from jax import lax
from jax.experimental import pallas as pl
from jax.experimental.pallas import tpu as pltpu
from jax.sharding import PartitionSpec as P

HEAD = 64
ADAPTER_RANK = 4
SEQ_LEN = 1024


adapter_scale = 8.0


def from_behind(block, axis, distance):
    devices = range(lax.axis_size(axis))
    route = [(i - distance, i) for i in devices if i - distance in devices]
    return lax.ppermute(block, axis, route)


def contract_axes(left, right, left_dim, right_dim):
    return lax.dot_general(
        left, right, (((left_dim,), (right_dim,)), ((), ())), preferred_element_type=jnp.float32
    )


def layer_norm(rows, gain, shift):
    mean = jnp.mean(rows, axis=-1, keepdims=True)
    centered = rows - mean
    spread = jnp.mean(centered * centered, axis=-1, keepdims=True)
    return centered * lax.rsqrt(spread + 1e-05) * gain + shift


def gelu_tanh(value):
    return (
        0.5
        * value
        * (1.0 + jnp.tanh(0.7978845608028654 * (value + 0.044715 * value * value * value)))
    )


def doc_mask(doc_starts):
    positions = jnp.arange(SEQ_LEN, dtype=jnp.int32)
    labels = jnp.sum((doc_starts[None, :] <= positions[:, None]).astype(jnp.int32), axis=1)
    return (positions[None, :] <= positions[:, None]) & (labels[:, None] == labels[None, :])


def masked_scores(query_rows, keys, doc_starts):
    scores = jnp.einsum(
        "qhd,khd->hqk", query_rows, keys, preferred_element_type=jnp.float32
    ) * HEAD ** (-0.5)
    return jnp.where(doc_mask(doc_starts)[None], scores, -1e30)


def attend(items):
    query_rows, keys, value_rows, doc_starts = items
    scores = masked_scores(query_rows, keys, doc_starts)
    top = jnp.max(scores, axis=-1, keepdims=True)
    weights = jnp.exp(scores - top)
    total = jnp.sum(weights, axis=-1, keepdims=True)
    mixed = jnp.einsum(
        "hqk,khd->qhd",
        (weights / total).astype(jnp.bfloat16),
        value_rows,
        preferred_element_type=jnp.float32,
    )
    return (mixed.astype(jnp.bfloat16), (top + jnp.log(total))[:, :, 0])


def attend_back(items):
    query_rows, keys, value_rows, doc_starts, log_totals, grad_mixed = items
    scores = masked_scores(query_rows, keys, doc_starts)
    probs = jnp.exp(scores - log_totals[:, :, None])
    grad_probs = jnp.einsum(
        "qhd,khd->hqk", grad_mixed, value_rows, preferred_element_type=jnp.float32
    )
    inner = jnp.sum(probs * grad_probs, axis=-1, keepdims=True)
    grad_scores = (probs * (grad_probs - inner)).astype(jnp.bfloat16)
    query_gradient = jnp.einsum(
        "hqk,khd->qhd", grad_scores, keys, preferred_element_type=jnp.float32
    ) * HEAD ** (-0.5)
    grad_k = jnp.einsum(
        "hqk,qhd->khd", grad_scores, query_rows, preferred_element_type=jnp.float32
    ) * HEAD ** (-0.5)
    value_gradient = jnp.einsum(
        "hqk,qhd->khd", probs.astype(jnp.bfloat16), grad_mixed, preferred_element_type=jnp.float32
    )
    return (
        query_gradient.astype(jnp.bfloat16),
        grad_k.astype(jnp.bfloat16),
        value_gradient.astype(jnp.bfloat16),
    )


def reduce_adapters(part_a, second_portion):
    return (lax.psum(part_a, ("dp", "tensor")), lax.psum(second_portion, "dp"))


def plain_body(
    activations,
    starts,
    attention_weights,
    projection_weight,
    feedforward_weight,
    output_weight,
    norm_gains,
    norm_biases,
    output_biases,
    query_value_bias,
    feedforward_bias,
    adapter_down_weight,
    adapter_up_weight,
):
    section = lax.axis_index("section")
    first = section == 0
    batches = activations.shape[1]
    own_rows = activations.shape[2]
    width = activations.shape[3]
    head_cols = projection_weight.shape[1]
    local_heads = head_cols // HEAD
    shaped = (-1, SEQ_LEN, local_heads, HEAD)
    w_cat = jnp.concatenate(
        [attention_weights[0, 0], attention_weights[0, 1], attention_weights[0, 2]], axis=1
    )
    stacked_down_maps = jnp.concatenate(
        [adapter_down_weight[0, 0], adapter_down_weight[0, 1]], axis=1
    )

    def forward_relay(rows, group_starts):
        normalized_rows = layer_norm(rows, norm_gains[0, 0], norm_biases[0, 0]).astype(jnp.bfloat16)
        gathered = lax.all_gather(normalized_rows, "tensor", axis=0, tiled=True)
        joined = jnp.dot(gathered, w_cat, preferred_element_type=jnp.float32)
        apply_adapter = jnp.dot(
            gathered, stacked_down_maps, preferred_element_type=jnp.float32
        ).astype(jnp.bfloat16)
        query_rows = (
            joined[:, :head_cols]
            + query_value_bias[0, 0]
            + adapter_scale
            * jnp.dot(
                apply_adapter[:, :ADAPTER_RANK],
                adapter_up_weight[0, 0],
                preferred_element_type=jnp.float32,
            )
        ).astype(jnp.bfloat16)
        keys = joined[:, head_cols : 2 * head_cols].astype(jnp.bfloat16)
        value_rows = (
            joined[:, 2 * head_cols :]
            + query_value_bias[0, 1]
            + adapter_scale
            * jnp.dot(
                apply_adapter[:, ADAPTER_RANK:],
                adapter_up_weight[0, 1],
                preferred_element_type=jnp.float32,
            )
        ).astype(jnp.bfloat16)
        mixed, log_totals = lax.map(
            attend,
            (
                query_rows.reshape(shaped),
                keys.reshape(shaped),
                value_rows.reshape(shaped),
                group_starts,
            ),
        )
        mixed = mixed.reshape(-1, head_cols)
        middle = (
            rows
            + lax.psum_scatter(
                jnp.dot(mixed, projection_weight[0], preferred_element_type=jnp.float32),
                "tensor",
                scatter_dimension=0,
                tiled=True,
            )
            + output_biases[0, 0]
        )
        normed_two = layer_norm(middle, norm_gains[0, 1], norm_biases[0, 1]).astype(jnp.bfloat16)
        hidden = (
            jnp.dot(
                lax.all_gather(normed_two, "tensor", axis=0, tiled=True),
                feedforward_weight[0],
                preferred_element_type=jnp.float32,
            )
            + feedforward_bias[0]
        )
        active = gelu_tanh(hidden).astype(jnp.bfloat16)
        output = (
            middle
            + lax.psum_scatter(
                jnp.dot(active, output_weight[0], preferred_element_type=jnp.float32).astype(
                    jnp.bfloat16
                ),
                "tensor",
                scatter_dimension=0,
                tiled=True,
            ).astype(jnp.float32)
            + output_biases[0, 1]
        )
        return (
            output,
            (
                rows,
                middle,
                gathered,
                apply_adapter,
                query_rows,
                keys,
                value_rows,
                log_totals,
                hidden,
            ),
        )

    def backward_relay(grad_rows, cache, group_starts):
        rows, middle, gathered, apply_adapter, query_rows, keys, value_rows, log_totals, hidden = (
            cache
        )
        grad_active = contract_axes(
            lax.all_gather(grad_rows.astype(jnp.bfloat16), "tensor", axis=0, tiled=True),
            output_weight[0],
            1,
            1,
        )
        _, gelu_back = jax.vjp(gelu_tanh, hidden)
        grad_hidden = gelu_back(grad_active)[0].astype(jnp.bfloat16)
        grad_normed_two = lax.psum_scatter(
            contract_axes(grad_hidden, feedforward_weight[0], 1, 1).astype(jnp.bfloat16),
            "tensor",
            scatter_dimension=0,
            tiled=True,
        ).astype(jnp.float32)
        _, norm_two_back = jax.vjp(
            lambda inner_rows: layer_norm(inner_rows, norm_gains[0, 1], norm_biases[0, 1]), middle
        )
        grad_middle = grad_rows + norm_two_back(grad_normed_two)[0]
        grad_mixed = contract_axes(
            lax.all_gather(grad_middle.astype(jnp.bfloat16), "tensor", axis=0, tiled=True),
            projection_weight[0],
            1,
            1,
        ).astype(jnp.bfloat16)
        query_gradient, grad_k, value_gradient = lax.map(
            attend_back,
            (
                query_rows.reshape(shaped),
                keys.reshape(shaped),
                value_rows.reshape(shaped),
                group_starts,
                log_totals,
                grad_mixed.reshape(shaped),
            ),
        )
        query_gradient = query_gradient.reshape(-1, head_cols)
        grad_k = grad_k.reshape(-1, head_cols)
        value_gradient = value_gradient.reshape(-1, head_cols)
        grad_low = jnp.concatenate(
            [
                adapter_scale * contract_axes(query_gradient, adapter_up_weight[0, 0], 1, 1),
                adapter_scale * contract_axes(value_gradient, adapter_up_weight[0, 1], 1, 1),
            ],
            axis=1,
        ).astype(jnp.bfloat16)
        grad_joined = jnp.concatenate([query_gradient, grad_k, value_gradient], axis=1)
        grad_normed = lax.psum_scatter(
            (
                contract_axes(grad_joined, w_cat, 1, 1)
                + contract_axes(grad_low, stacked_down_maps, 1, 1)
            ).astype(jnp.bfloat16),
            "tensor",
            scatter_dimension=0,
            tiled=True,
        ).astype(jnp.float32)
        _, norm_back = jax.vjp(
            lambda inner_rows: layer_norm(inner_rows, norm_gains[0, 0], norm_biases[0, 0]), rows
        )
        grad_in = grad_middle + norm_back(grad_normed)[0]
        grad_down = contract_axes(gathered, grad_low, 0, 0)
        part_a = jnp.stack([grad_down[:, :ADAPTER_RANK], grad_down[:, ADAPTER_RANK:]])
        second_portion = adapter_scale * jnp.stack(
            [
                contract_axes(apply_adapter[:, :ADAPTER_RANK], query_gradient, 0, 0),
                contract_axes(apply_adapter[:, ADAPTER_RANK:], value_gradient, 0, 0),
            ]
        )
        return (grad_in, part_a, second_portion)

    received = jnp.zeros((own_rows, width), jnp.bfloat16)
    finals = []
    stored = []
    for tick in range(batches + 1):
        batch_index = jnp.clip(tick - section, 0, batches - 1)
        own = lax.dynamic_index_in_dim(activations[0], batch_index, 0, keepdims=False)
        rows = jnp.where(first, own, received).astype(jnp.float32)
        group_starts = lax.dynamic_index_in_dim(starts, batch_index, 0, keepdims=False)
        output, cache = forward_relay(rows, group_starts)
        finals.append(output)
        stored.append(rows)
        if tick < batches:
            received = from_behind(output.astype(jnp.bfloat16), "section", 1)
    stacked = jax.tree.map(lambda *items: jnp.stack(items), *stored)
    returned = jnp.zeros((own_rows, width), jnp.bfloat16)
    totals_a = jnp.zeros((2, width, ADAPTER_RANK), jnp.float32)
    totals_b = jnp.zeros((2, ADAPTER_RANK, head_cols), jnp.float32)
    grads_in = []
    for tick in range(batches + 1):
        position = tick - 1 + section
        batch_index = jnp.clip(position, 0, batches - 1)
        valid = ((position >= 0) & (position < batches)).astype(jnp.float32)
        own = lax.dynamic_index_in_dim(activations[0], batch_index, 0, keepdims=False)
        grad_rows = jnp.where(first, returned, own).astype(jnp.float32) * valid
        group_starts = lax.dynamic_index_in_dim(starts, batch_index, 0, keepdims=False)
        slot_index = jnp.clip(tick - 1 + 2 * section, 0, batches)
        picked = lax.dynamic_index_in_dim(stacked, slot_index, 0, keepdims=False)
        _, cache = forward_relay(picked, group_starts)
        grad_in, part_a, second_portion = backward_relay(grad_rows, cache, group_starts)
        grads_in.append(grad_in)
        if tick < batches:
            returned = from_behind(grad_in.astype(jnp.bfloat16), "section", -1)
        part_a, second_portion = reduce_adapters(part_a, second_portion)
        totals_a = totals_a + part_a
        totals_b = totals_b + second_portion
    combined = jnp.stack(
        [jnp.where(first, grads_in[index + 1], finals[index + 1]) for index in range(batches)]
    )
    return (combined[None], totals_a[None], totals_b[None])


LOW = 2 * ADAPTER_RANK
VMEM_SPACE = pl.BlockSpec(memory_space=pltpu.VMEM)
SMEM_SPACE = pl.BlockSpec(memory_space=pltpu.SMEM)
HBM_SPACE = pl.BlockSpec(memory_space=pltpu.HBM)
BLOCK = 256
CHUNK = 2 * BLOCK


def send(block, route):
    pairs = []
    for s in range(2):
        for t in range(4):
            to = route(s, t)
            if to is not None:
                pairs.append((s * 4 + t, to[0] * 4 + to[1]))
    return lax.ppermute(block, ("section", "tensor"), pairs)


def other_core(block):
    return send(block, lambda s, t: (1 - s, t))


def x_swap(block):
    return send(block, lambda s, t: (s, t ^ 1))


def y_swap(block):
    return send(block, lambda s, t: (s, t ^ 2))


def after(value, *others):
    return lax.optimization_barrier((value, others))[0]


def cross_send(block, source=0):
    return send(block, lambda s, t: (t >> 1, t ^ 2) if s == source else None)


def collect(target, same_chip, cross_chip):
    return (
        send(same_chip, lambda s, t: (target, t) if s == t & 1 and s != target else None),
        send(cross_chip, lambda s, t: (target, t ^ 2) if s == t & 1 else None),
    )


def mm(left, right):
    return jnp.dot(left, right, preferred_element_type=jnp.float32)


def mm_nt(left, right):
    return contract_axes(left, right, 1, 1)


def norm_back(rows, gain, grad):
    mean = jnp.mean(rows, axis=-1, keepdims=True)
    centered = rows - mean
    scale = lax.rsqrt(jnp.mean(centered * centered, axis=-1, keepdims=True) + 1e-05)
    unit = centered * scale
    scaled = grad * gain
    return scale * (
        scaled
        - jnp.mean(scaled, axis=-1, keepdims=True)
        - unit * jnp.mean(scaled * unit, axis=-1, keepdims=True)
    )


def gelu_both(value):
    square = value * value
    bent = jnp.tanh(0.7978845608028654 * value * (1.0 + 0.044715 * square))
    half = 0.5 * (1.0 + bent)
    slope = half + 0.5 * value * (1.0 - bent * bent) * (
        0.7978845608028654 * (1.0 + 3.0 * 0.044715 * square)
    )
    return value * half, slope


def cost(flops, read):
    return pl.CostEstimate(flops=1000, bytes_accessed=1000, transcendentals=0)


def kernel_params(mib):
    return pltpu.CompilerParams(vmem_limit_bytes=mib * 1024 * 1024)


def position_mask(meta, query_block, key_block):
    shape = (BLOCK, BLOCK)
    key_pos = key_block * BLOCK + lax.broadcasted_iota(jnp.int32, shape, 0)
    query_pos = query_block * BLOCK + lax.broadcasted_iota(jnp.int32, (1, BLOCK), 1)
    low = jnp.zeros((1, BLOCK), jnp.int32)
    for c in range(4):
        first = meta[4 + c]
        low = jnp.where(first <= query_pos, jnp.maximum(low, first), low)
    valid = key_pos >= low
    if query_block == key_block:
        valid = valid & (key_pos <= query_pos)
    return valid


def lay_mask(meta, chunk, target):
    for i in range(2):
        for j in range(2 * chunk + i + 1):
            target[tile(chunk, i, j)] = jnp.where(
                position_mask(meta, 2 * chunk + i, j), 0.0, -1e30
            )


def tile(chunk, i, j):
    return i * (2 * chunk + 1) + j


def head_lanes(half):
    return (lax.broadcasted_iota(jnp.int32, (1, 2 * HEAD), 1) // HEAD) == half


def start_pick(choices, target, sem):
    for condition, source in choices:

        @pl.when(condition)
        def _(source=source):
            pltpu.make_async_copy(source, target, sem).start()


def load_qkv_weight(layer, meta, pieces, w_buf, sem):
    own, other, lead, trail = pieces
    s, y, w = meta[0], meta[2], meta[8]
    start_pick(
        (((s == y) & (s == layer), own), ((s == y) & (s != layer), other)), w_buf, sem
    )

    @pl.when(s != y)
    def _():
        for part, side in ((lead, w), (trail, 1 - w)):
            pltpu.make_async_copy(part, w_buf.at[pl.ds(2 * side, 2)], sem).start()

    return pltpu.make_async_copy(own, w_buf, sem)


def half_rows(core):
    return pl.ds(pl.multiple_of(core * BLOCK, BLOCK), BLOCK)


def lay_out(meta, own, near, target):
    s = meta[0]
    target[half_rows(s), :] = own[...]
    target[half_rows(1 - s), :] = near[...]


def share_out(meta, source, keep, give):
    s = meta[0]
    keep[...] = source[half_rows(s), :]
    give[...] = source[half_rows(1 - s), :]


def attend_kernel(layer, chunk, meta, shared, varied, own, near, *rest):
    before, rest = rest[: 2 * chunk], rest[2 * chunk :]
    q_out, k_out, v_out, lse_out, mixed_out, keep, give = rest[4:11]
    (
        n_buf, w_buf, score_buf, mask_buf, vt_buf, q_ref, k_ref, v_ref, lse_ref, mixed_ref, sem,
        out_sems,
    ) = rest[11:]
    loaded = load_qkv_weight(layer, meta, rest[:4], w_buf, sem)
    down = shared[layer, 8:16, :].astype(jnp.bfloat16)
    bias = varied[layer, 1:2, :]
    up = varied[layer, 8:16, 0:512].astype(jnp.bfloat16)
    lay_out(meta, own, near, n_buf)
    lay_mask(meta, chunk, mask_buf)
    keys = [k_ref] if chunk == 0 else [before[0], k_ref]
    if chunk == 1:
        for b in range(2):
            span = slice(b * BLOCK, (b + 1) * BLOCK)
            vt_buf[:, span] = before[1][span, :].T
    loaded.wait()
    normed = n_buf[...]
    low = mm_nt(normed, down).astype(jnp.bfloat16)
    lifted = adapter_scale * mm(low, up)
    q_ref[...] = (mm(normed, w_buf[0]) + bias[:, 0:256] + lifted[:, 0:256]).astype(jnp.bfloat16)
    k_ref[...] = mm(normed, w_buf[1]).astype(jnp.bfloat16)
    v_ref[...] = (mm(normed, w_buf[2]) + bias[:, 256:512] + lifted[:, 256:512]).astype(jnp.bfloat16)
    saved = [
        pltpu.make_async_copy(source, target, out_sems.at[i])
        for i, (source, target) in enumerate(
            (
                (q_ref, q_out), (k_ref, k_out), (v_ref, v_out), (lse_ref, lse_out),
                (mixed_ref, mixed_out),
            )
        )
    ]
    for copy in saved[:3]:
        copy.start()
    for b in range(2):
        span = slice(b * BLOCK, (b + 1) * BLOCK)
        vt_buf[:, chunk * CHUNK + b * BLOCK : chunk * CHUNK + (b + 1) * BLOCK] = v_ref[span, :].T

    def one_head(head, carry):
        lanes = pl.ds(pl.multiple_of((head // 2) * 128, 128), 128)
        chosen = head_lanes(head % 2)
        deep = pl.ds(pl.multiple_of(head * HEAD, HEAD), HEAD)
        for i in range(2):
            span = slice(i * BLOCK, (i + 1) * BLOCK)
            place = 2 * chunk + i
            query = jnp.where(chosen, q_ref[span, lanes] * HEAD ** (-0.5), 0.0).astype(jnp.bfloat16)
            top = jnp.full((1, BLOCK), -1e30, jnp.float32)
            for j in range(place + 1):
                rows = slice((j % 2) * BLOCK, (j % 2 + 1) * BLOCK)
                scores = mm_nt(keys[j // 2][rows, lanes], query) + mask_buf[tile(chunk, i, j)]
                score_buf[j] = scores
                top = jnp.maximum(top, jnp.max(scores, axis=0, keepdims=True))
            total = jnp.zeros((1, BLOCK), jnp.float32)
            mixed = jnp.zeros((HEAD, BLOCK), jnp.float32)
            for j in range(place + 1):
                weights = jnp.exp(score_buf[j] - top)
                total = total + jnp.sum(weights, axis=0, keepdims=True)
                mixed = mixed + mm(
                    vt_buf[deep, j * BLOCK : (j + 1) * BLOCK], weights.astype(jnp.bfloat16)
                )
            mixed_ref[deep, span] = mixed / total
            lse_ref[pl.ds(head, 1), span] = top + jnp.log(total)
        return carry

    lax.fori_loop(0, 4, one_head, 0, unroll=4)
    for copy in saved[3:]:
        copy.start()
    for b in range(2):
        span = slice(b * BLOCK, (b + 1) * BLOCK)
        n_buf[span, :] = mm_nt(
            mixed_ref[:, span].T.astype(jnp.bfloat16), w_buf[3]
        ).astype(jnp.bfloat16)
    share_out(meta, n_buf, keep, give)
    for copy in saved:
        copy.wait()


def attend_call(layer, chunk, meta, blocks, before, shared, varied, weight):
    bf, f32 = jnp.bfloat16, jnp.float32
    wide = jax.ShapeDtypeStruct((CHUNK, 256), bf)
    piece = jax.ShapeDtypeStruct((BLOCK, 1024), bf)
    *saved, keep, give = pl.pallas_call(
        functools.partial(attend_kernel, layer, chunk),
        in_specs=[SMEM_SPACE] + [VMEM_SPACE] * (4 + 2 * chunk) + [HBM_SPACE] * 4,
        out_specs=[HBM_SPACE] * 5 + [VMEM_SPACE] * 2,
        out_shape=[wide, wide, wide, jax.ShapeDtypeStruct((8, CHUNK), f32),
                   jax.ShapeDtypeStruct((256, CHUNK), f32), piece, piece],
        scratch_shapes=[
            pltpu.VMEM((CHUNK, 1024), bf),
            pltpu.VMEM((4, 1024, 256), bf),
            pltpu.VMEM((2 + 2 * chunk, BLOCK, BLOCK), f32),
            pltpu.VMEM((3 + 4 * chunk, BLOCK, BLOCK), f32),
            pltpu.VMEM((256, CHUNK * (1 + chunk)), bf),
            pltpu.VMEM((CHUNK, 256), bf),
            pltpu.VMEM((CHUNK, 256), bf),
            pltpu.VMEM((CHUNK, 256), bf),
            pltpu.VMEM((8, CHUNK), f32),
            pltpu.VMEM((256, CHUNK), f32),
            pltpu.SemaphoreType.DMA,
            pltpu.SemaphoreType.DMA((5,)),
        ],
        compiler_params=kernel_params(24),
        cost_estimate=cost(3.5e9, 8e6),
        name="attention_forward_%d" % chunk,
    )(meta, shared, varied, *blocks, *(before if chunk else ()), *weight)
    return saved, keep, give


def attend_back_kernel(layer, chunk, meta, shared, varied, n_own, n_near, g_own, g_near, *rest):
    n_saved = 5 + 2 * chunk
    saved, rest = rest[:n_saved], rest[n_saved:]
    saved_sems, rest = rest[-1], rest[:-1]
    bufs, rest = rest[-n_saved:], rest[:-n_saved]
    fetches = [
        pltpu.make_async_copy(source, target, saved_sems.at[i])
        for i, (source, target) in enumerate(zip(saved, bufs))
    ]
    for fetch in fetches:
        fetch.start()
    q_ref, lse_ref, mixed_ref = bufs[:3]
    keys, values = bufs[3 : 4 + chunk], bufs[4 + chunk :]
    if chunk == 0:
        dk_in, dv_in, down_in, up_in = rest[:4]
        keep, give, down_ref, up_ref = rest[8:12]
        weight, scratch = rest[4:8], rest[12:]
    else:
        keep, give, down_ref, up_ref, dk_out, dv_out = rest[4:10]
        weight, scratch = rest[:4], rest[10:]
    (
        n_buf, g_buf, w_buf, mask_buf, kt_buf, do_buf, delta_buf, dqt_buf, dk_buf, dv_buf, dq_buf,
        sem,
    ) = scratch
    loaded = load_qkv_weight(layer, meta, weight, w_buf, sem)
    lay_out(meta, g_own, g_near, g_buf)
    lay_out(meta, n_own, n_near, n_buf)
    lay_mask(meta, chunk, mask_buf)
    for fetch in fetches:
        fetch.wait()
    for j in range(2 + 2 * chunk):
        rows = slice((j % 2) * BLOCK, (j % 2 + 1) * BLOCK)
        kt_buf[:, j * BLOCK : (j + 1) * BLOCK] = keys[j // 2][rows, :].T
    if chunk == 0:
        dk_buf[...] = dk_in[...]
        dv_buf[...] = dv_in[...]
    else:
        dk_buf[...] = jnp.zeros_like(dk_buf)
        dv_buf[...] = jnp.zeros_like(dv_buf)
    loaded.wait()
    do_buf[...] = mm(g_buf[...], w_buf[3]).astype(jnp.bfloat16)
    for b in range(2):
        span = slice(b * BLOCK, (b + 1) * BLOCK)
        product = do_buf[span, :].astype(jnp.float32).T * mixed_ref[:, span]
        for head in range(4):
            delta_buf[head : head + 1, span] = jnp.sum(
                product[head * HEAD : (head + 1) * HEAD], axis=0, keepdims=True
            )

    def one_head(head, carry):
        lanes = pl.ds(pl.multiple_of((head // 2) * 128, 128), 128)
        chosen = head_lanes(head % 2)
        deep = pl.ds(pl.multiple_of(head * HEAD, HEAD), HEAD)
        for i in range(2):
            span = slice(i * BLOCK, (i + 1) * BLOCK)
            place = 2 * chunk + i
            query = jnp.where(chosen, q_ref[span, lanes] * HEAD ** (-0.5), 0.0).astype(jnp.bfloat16)
            grad_mixed = jnp.where(chosen, do_buf[span, lanes], 0.0).astype(jnp.bfloat16)
            lse = lse_ref[pl.ds(head, 1), span]
            delta = delta_buf[pl.ds(head, 1), span]
            grad_query = jnp.zeros((HEAD, BLOCK), jnp.float32)
            for j in range(place + 1):
                rows = slice((j % 2) * BLOCK, (j % 2 + 1) * BLOCK)
                all_rows = slice(j * BLOCK, (j + 1) * BLOCK)
                scores = mm_nt(keys[j // 2][rows, lanes], query) + mask_buf[tile(chunk, i, j)]
                probs = jnp.exp(scores - lse)
                grad_probs = mm_nt(values[j // 2][rows, lanes], grad_mixed)
                grad_scores = (probs * (grad_probs - delta)).astype(jnp.bfloat16)
                dv_buf[all_rows, lanes] += mm(probs.astype(jnp.bfloat16), grad_mixed)
                dk_buf[all_rows, lanes] += mm(grad_scores, query)
                grad_query = grad_query + mm(kt_buf[deep, all_rows], grad_scores)
            dqt_buf[deep, span] = grad_query * HEAD ** (-0.5)
        return carry

    lax.fori_loop(0, 4, one_head, 0, unroll=4)
    down = shared[layer, 8:16, :].astype(jnp.bfloat16)
    up = varied[layer, 8:16, 0:512].astype(jnp.bfloat16)
    for b in range(2):
        span = slice(b * BLOCK, (b + 1) * BLOCK)
        dq_buf[span, :] = dqt_buf[:, span].T.astype(jnp.bfloat16)
    done = slice(chunk * CHUNK, (chunk + 1) * CHUNK)
    normed = n_buf[...]
    grad_q = dq_buf[...]
    grad_k = dk_buf[done, :].astype(jnp.bfloat16)
    grad_v = dv_buf[done, :].astype(jnp.bfloat16)
    both = jnp.concatenate([grad_q, grad_v], axis=1)
    low_grad = (adapter_scale * mm_nt(both, up)).astype(jnp.bfloat16)
    low_grad_t = (adapter_scale * mm_nt(up, both)).astype(jnp.bfloat16)
    low_t = mm_nt(down, normed).astype(jnp.bfloat16)
    g_buf[...] = (
        mm_nt(grad_q, w_buf[0]) + mm_nt(grad_k, w_buf[1]) + mm_nt(grad_v, w_buf[2])
        + mm(low_grad, down)
    ).astype(jnp.bfloat16)
    share_out(meta, g_buf, keep, give)
    total_down = mm(low_grad_t, normed)
    total_up = adapter_scale * mm(low_t, both)
    if chunk == 0:
        total_down = total_down + down_in[...]
        total_up = total_up + up_in[...]
    else:
        dk_out[...] = dk_buf[0:CHUNK, :]
        dv_out[...] = dv_buf[0:CHUNK, :]
    down_ref[...] = total_down
    up_ref[...] = total_up


def attend_back_call(layer, chunk, meta, blocks, grads, saved, carried, shared, varied, weight):
    bf, f32 = jnp.bfloat16, jnp.float32
    piece = jax.ShapeDtypeStruct((BLOCK, 1024), bf)
    tall = jax.ShapeDtypeStruct((CHUNK, 256), f32)
    spans = CHUNK * (1 + chunk)
    q, _, _, lse, mixed = saved[chunk]
    keys = [one[1] for one in saved[: chunk + 1]]
    values = [one[2] for one in saved[: chunk + 1]]
    held = (q, lse, mixed, *keys, *values)
    inputs = (shared, varied, *blocks, *grads, *held, *carried)
    return pl.pallas_call(
        functools.partial(attend_back_kernel, layer, chunk),
        in_specs=[SMEM_SPACE] + [VMEM_SPACE] * 6 + [HBM_SPACE] * len(held)
        + [VMEM_SPACE] * len(carried) + [HBM_SPACE] * 4,
        out_specs=[VMEM_SPACE] * (4 + 2 * chunk),
        out_shape=[piece, piece, jax.ShapeDtypeStruct((LOW, 1024), f32),
                   jax.ShapeDtypeStruct((LOW, 512), f32)] + [tall] * (2 * chunk),
        scratch_shapes=[
            pltpu.VMEM((CHUNK, 1024), bf),
            pltpu.VMEM((CHUNK, 1024), bf),
            pltpu.VMEM((4, 1024, 256), bf),
            pltpu.VMEM((3 + 4 * chunk, BLOCK, BLOCK), f32),
            pltpu.VMEM((256, spans), bf),
            pltpu.VMEM((CHUNK, 256), bf),
            pltpu.VMEM((8, CHUNK), f32),
            pltpu.VMEM((256, CHUNK), f32),
            pltpu.VMEM((spans, 256), f32),
            pltpu.VMEM((spans, 256), f32),
            pltpu.VMEM((CHUNK, 256), bf),
            pltpu.SemaphoreType.DMA,
            *[pltpu.VMEM(one.shape, one.dtype) for one in held],
            pltpu.SemaphoreType.DMA((len(held),)),
        ],
        compiler_params=kernel_params(24),
        cost_estimate=cost(6e9, 12e6),
        name="attention_backward_%d" % chunk,
    )(meta, *inputs, *weight)


def summed(passed, far):
    return passed[...].astype(jnp.float32) + far[...].astype(jnp.float32)


def rows_middle_kernel(layer, h_ref, passed, far, shared, middle_ref, normed_ref):
    middle = h_ref[...].astype(jnp.float32) + summed(passed, far) + shared[layer, 4:5, :]
    middle_ref[...] = middle
    normed_ref[...] = layer_norm(middle, shared[layer, 1:2, :], shared[layer, 3:4, :]).astype(
        jnp.bfloat16
    )


def load_units(layer, meta, pieces, w1, w2, sems):
    own, other, (lead, trail) = pieces[0:2], pieces[2:4], pieces[4:6]
    s, y, w = meta[0], meta[2], meta[8]
    copies = []
    for m, matrix in enumerate((w1, w2)):
        start_pick(
            (
                ((s == y) & (s == layer), own[m]),
                ((s == y) & (s != layer), other[m]),
                ((s != y) & (w == m), lead),
                ((s != y) & (w != m), trail),
            ),
            matrix,
            sems.at[m],
        )
        copies.append(pltpu.make_async_copy(own[m], matrix, sems.at[m]))
    return copies


def stack_rows(blocks, target):
    for i, block in enumerate(blocks):
        target[i * BLOCK : (i + 1) * BLOCK, :] = block[...]


def halve(total, keep, give):
    keep[...] = total[:BLOCK].astype(jnp.bfloat16)
    give[...] = total[BLOCK:].astype(jnp.bfloat16)


def units_kernel(layer, meta, n0, n1, bias, *rest):
    keep, give, slope_out, w1, w2, sems, n_buf, slope_buf, out_sem = rest[6:]
    waits = load_units(layer, meta, rest[:6], w1, w2, sems)
    stack_rows((n0, n1), n_buf)
    waits[0].wait()
    active, slope = gelu_both(mm(n_buf[...], w1[...]) + bias[layer, 0:1, :])
    slope_buf[...] = slope.astype(jnp.bfloat16)
    saving = pltpu.make_async_copy(slope_buf, slope_out, out_sem)
    saving.start()
    waits[1].wait()
    halve(mm(active.astype(jnp.bfloat16), w2[...]), keep, give)
    saving.wait()


def units_turn_kernel(layer, meta, n0, n1, g0, g1, bias, *rest):
    keep, give, out_keep, out_give, w1, w2, sems, n_buf, g_buf = rest[6:]
    waits = load_units(layer, meta, rest[:6], w1, w2, sems)
    stack_rows((n0, n1), n_buf)
    stack_rows((g0, g1), g_buf)
    for copy in waits:
        copy.wait()
    active, slope = gelu_both(mm(n_buf[...], w1[...]) + bias[layer, 0:1, :])
    grad_hidden = (mm_nt(g_buf[...], w2[...]) * slope).astype(jnp.bfloat16)
    halve(mm_nt(grad_hidden, w1[...]), keep, give)
    halve(mm(active.astype(jnp.bfloat16), w2[...]), out_keep, out_give)


def units_back_kernel(layer, meta, g0, g1, slope_in, *rest):
    keep, give, w1, w2, sems, g_buf, slope_buf, in_sem = rest[6:]
    waits = load_units(layer, meta, rest[:6], w1, w2, sems)
    fetch = pltpu.make_async_copy(slope_in, slope_buf, in_sem)
    fetch.start()
    stack_rows((g0, g1), g_buf)
    waits[1].wait()
    fetch.wait()
    grad = (mm_nt(g_buf[...], w2[...]) * slope_buf[...].astype(jnp.float32)).astype(jnp.bfloat16)
    waits[0].wait()
    halve(mm_nt(grad, w1[...]), keep, give)


def rows_first_kernel(meta, mine, crossed, far_mine, far_crossed, shared, *outs):
    holder = meta[0] == meta[1]
    upper = meta[2] == 0
    first = jnp.where(holder, mine[...], far_mine[...])
    second = jnp.where(holder, crossed[...], far_crossed[...])
    for c, (one, other) in enumerate(((first, second), (second, first))):
        rows = jnp.where(upper, one, other)
        outs[c][...] = rows
        outs[2 + c][...] = layer_norm(
            rows.astype(jnp.float32), shared[0, 0:1, :], shared[0, 2:3, :]
        ).astype(jnp.bfloat16)


def rows_next_kernel(middle, passed, far, shared, between_ref, normed_ref):
    between = (middle[...] + summed(passed, far) + shared[0, 5:6, :]).astype(jnp.bfloat16)
    between_ref[...] = between
    normed_ref[...] = layer_norm(
        between.astype(jnp.float32), shared[1, 0:1, :], shared[1, 2:3, :]
    ).astype(jnp.bfloat16)


def rows_turn_kernel(layer, middle, g_ref, passed, far, shared, grad_ref, sent_ref):
    grad_middle = g_ref[...].astype(jnp.float32) + norm_back(
        middle[...], shared[layer, 1:2, :], summed(passed, far)
    )
    grad_ref[...] = grad_middle
    sent_ref[...] = grad_middle.astype(jnp.bfloat16)


def rows_before_kernel(gm_ref, passed, far, between_ref, shared, grad_ref):
    grad_rows = gm_ref[...] + norm_back(
        between_ref[...].astype(jnp.float32), shared[1, 0:1, :], summed(passed, far)
    )
    grad_ref[...] = grad_rows.astype(jnp.bfloat16)


def rows_output_kernel(middle, passed, far, shared, wide_ref, narrow_ref):
    total = middle[...] + summed(passed, far) + shared[1, 5:6, :]
    wide_ref[...] = total
    narrow_ref[...] = total.astype(jnp.bfloat16)


def rows_final_kernel(gm_ref, passed, far, h_ref, shared, wide_ref, narrow_ref):
    grad_in = gm_ref[...] + norm_back(
        h_ref[...].astype(jnp.float32), shared[0, 0:1, :], summed(passed, far)
    )
    wide_ref[...] = grad_in
    narrow_ref[...] = grad_in.astype(jnp.bfloat16)


def units_call(kernel, meta, small, saved, weights, outs, saving, scratch, name):
    return pl.pallas_call(
        kernel,
        in_specs=[SMEM_SPACE] + [VMEM_SPACE] * len(small) + [HBM_SPACE] * (len(saved) + len(weights)),
        out_specs=[VMEM_SPACE] * len(outs) + [HBM_SPACE] * len(saving),
        out_shape=[*outs, *saving],
        scratch_shapes=scratch,
        compiler_params=kernel_params(24),
        cost_estimate=cost(2e9, 8e6),
        name=name,
    )(meta, *small, *saved, *weights)


def plain_call(kernel, scalar, small, large, outs, scratch, flops, name):
    specs = [VMEM_SPACE] * len(small) + [HBM_SPACE] * len(large)
    operands = (*small, *large)
    if scalar is not None:
        specs, operands = [SMEM_SPACE] + specs, (scalar, *operands)
    return pl.pallas_call(
        kernel,
        in_specs=specs,
        out_specs=[VMEM_SPACE] * len(outs),
        out_shape=outs,
        scratch_shapes=scratch,
        compiler_params=kernel_params(24),
        cost_estimate=cost(flops, 8e6),
        name=name,
    )(*operands)


def deal_rows(source, slots, section, y):
    same = lax.dynamic_index_in_dim(slots, y, 0, keepdims=False)
    cross = lax.dynamic_index_in_dim(slots, 1 - y, 0, keepdims=False)
    moved = send(same, lambda s, t: (t & 1, t) if s == source and s != t & 1 else None)
    crossed = send(cross, lambda s, t: (t & 1, t ^ 2) if s == source else None)
    mine = jnp.where(section == source, same, moved)
    return mine, crossed


def to_x(block):
    return send(block, lambda s, t: (s, t ^ 1) if s == t & 1 else None)


def from_x(block):
    return send(block, lambda s, t: (s, t ^ 1) if s != t & 1 else None)


def z_swap(block):
    size = lax.axis_size("dp")
    pairs = [
        ((s * size + z) * 4 + t, (s * size + (z ^ 1)) * 4 + t)
        for s in range(2) for z in range(size) for t in range(4) if s != t >> 1
    ]
    return lax.ppermute(block, ("section", "dp", "tensor"), pairs)


def early_sum(keep, give, swap=x_swap):
    half = BLOCK // 2
    take = jnp.concatenate([other_core(give[:half]), other_core(give[half:])])
    passed = (keep.astype(jnp.float32) + take.astype(jnp.float32)).astype(jnp.bfloat16)
    return passed, swap(passed)


def chip_sum(keep, give, last, swap=x_swap):
    take = other_core(after(give, last))
    passed = (keep.astype(jnp.float32) + take.astype(jnp.float32)).astype(jnp.bfloat16)
    return passed, swap(passed)


def total_over_z(downs, ups):
    both = jnp.concatenate([jnp.concatenate(downs), jnp.concatenate(ups)], axis=1)
    size = lax.axis_size("dp")
    step = 1
    while step < size:
        both = both + lax.ppermute(both, "dp", [(i, i ^ step) for i in range(size)])
        step *= 2
    return both


def total_over_cores(both, section, y):
    both = both + y_swap(both)
    moved = other_core(both)
    down = both[:, :1024] + moved[:, :1024]
    down = jnp.where(section == 0, down[:LOW], down[LOW:])
    up = jnp.where(section == y, both[:, 1024:], moved[:, 1024:])
    return down + x_swap(down), jnp.where(section == 0, up[:LOW], up[LOW:])


def relay_body(
    activations, starts, attention_weights, projection_weight, feedforward_weight, output_weight,
    norm_gains, norm_biases, output_biases, query_value_bias, feedforward_bias,
    adapter_down_weight, adapter_up_weight,
):
    bf, f32 = jnp.bfloat16, jnp.float32
    section = lax.axis_index("section")
    place = lax.axis_index("tensor")
    y, x = place // 2, place % 2
    first = section == 0

    mine, crossed = deal_rows(0, activations[0], section, y)
    down_rows = adapter_down_weight[0].astype(f32).transpose(0, 2, 1).reshape(LOW, 1024)
    up0 = adapter_up_weight[0, 0].astype(f32)
    up1 = adapter_up_weight[0, 1].astype(f32)
    zero = jnp.zeros((ADAPTER_RANK, 256), f32)
    common = jnp.concatenate(
        [norm_gains[0], norm_biases[0], output_biases[0], jnp.zeros((2, 1024), f32), down_rows]
    )
    own_part = jnp.concatenate(
        [
            feedforward_bias,
            jnp.pad(query_value_bias[0].reshape(1, 512), ((0, 0), (0, 512))),
            jnp.zeros((6, 1024), f32),
            jnp.concatenate([up0, zero, jnp.zeros((ADAPTER_RANK, 512), f32)], axis=1),
            jnp.concatenate([zero, up1, jnp.zeros((ADAPTER_RANK, 512), f32)], axis=1),
        ]
    )
    partner = other_core(common)
    partner_part = other_core(own_part)
    parts = jnp.where(
        first, jnp.stack([own_part, partner_part]), jnp.stack([partner_part, own_part])
    )
    near_varied = jnp.where(section == y, parts, y_swap(parts))
    shared = jnp.where(first, jnp.stack([common, partner]), jnp.stack([partner, common]))
    meta = jnp.concatenate(
        [
            jnp.stack([section, x, y, place]).astype(jnp.int32),
            lax.dynamic_index_in_dim(starts, y, 0, keepdims=False).reshape(4),
            (lax.axis_index("dp") % 2).astype(jnp.int32)[None],
        ]
    )
    even = lax.axis_index("dp") % 2 == 0
    own_a = jnp.concatenate([attention_weights[0], projection_weight[0].T[None]])
    w1_own, w2_own = feedforward_weight[0], output_weight[0]
    other_a = other_core(own_a)
    g_mine, g_crossed = deal_rows(1, activations[0], section, y)
    mine, crossed, shared, g_mine, g_crossed = lax.optimization_barrier(
        (mine, crossed, shared, g_mine, g_crossed)
    )
    lead_a0 = cross_send(after(jnp.where(even, own_a[:2], own_a[2:]), crossed, near_varied))
    far_mine, far_crossed = to_x(mine), to_x(crossed)
    trail_a0 = z_swap(after(lead_a0, far_mine, far_crossed))

    sheet = jax.ShapeDtypeStruct((BLOCK, 1024), f32)
    thin = jax.ShapeDtypeStruct((BLOCK, 1024), bf)
    slope_shape = jax.ShapeDtypeStruct((CHUNK, 1024), bf)
    matrices = [
        pltpu.VMEM((1024, 1024), bf), pltpu.VMEM((1024, 1024), bf), pltpu.SemaphoreType.DMA((2,))
    ]
    group = pltpu.VMEM((CHUNK, 1024), bf)

    def small(kernel, *operands, outs, name):
        return plain_call(kernel, None, operands, (), outs, [], 1e7, name)

    def attend(layer, chunk, normed, before, weight, near=None):
        near = other_core(normed) if near is None else near
        return attend_call(
            layer, chunk, meta, (normed, near), before, shared, near_varied, weight
        )

    def units(layer, normed, weight):
        return units_call(
            functools.partial(units_kernel, layer), meta, (normed, other_core(normed), near_varied),
            (), weight, [thin, thin], [slope_shape],
            [*matrices, group, group, pltpu.SemaphoreType.DMA], "units",
        )

    def units_turn(layer, normed, grad, near_grad, weight):
        return units_call(
            functools.partial(units_turn_kernel, layer), meta,
            (normed, other_core(normed), grad, near_grad, near_varied), (), weight,
            [thin] * 4, [], [*matrices, group, group], "units_turn",
        )

    def units_back(layer, grad, slope, weight):
        return units_call(
            functools.partial(units_back_kernel, layer), meta, (grad, other_core(grad)), (slope,),
            weight, [thin, thin], [], [*matrices, group, group, pltpu.SemaphoreType.DMA],
            "units_back",
        )

    def middle(layer, rows, sums):
        return small(
            functools.partial(rows_middle_kernel, layer), rows, *sums, shared, outs=[sheet, thin],
            name="rows_middle",
        )

    def turn(layer, middle_rows, grad, sums):
        return small(
            functools.partial(rows_turn_kernel, layer), middle_rows, grad, *sums, shared,
            outs=[sheet, thin], name="rows_turn",
        )

    row0, row1, n0, n1 = plain_call(
        rows_first_kernel, meta, (mine, crossed, far_mine, far_crossed, shared), (), [thin] * 4,
        [], 1e7, "rows_first",
    )
    g_far = [to_x(one) for one in (g_mine, g_crossed)]
    weights_a0 = (own_a, other_a, lead_a0, trail_a0)
    near_n0 = other_core(n0)
    lead_b0 = cross_send(jnp.where(even, *after((w1_own, w2_own), near_n0)))
    n00, n01 = n0, n1
    saved00, keep, give = attend(0, 0, n0, (), weights_a0, near_n0)
    keep, give, g_far = lax.optimization_barrier((keep, give, g_far))
    sum0 = chip_sum(keep, give, lead_a0)
    other_w1, other_w2 = (other_core(after(one, sum0[0])) for one in (w1_own, w2_own))
    trail_b0 = z_swap(after(lead_b0, sum0[0]))
    weights_b0 = (w1_own, w2_own, other_w1, other_w2, lead_b0, trail_b0)
    saved01, keep, give = attend(0, 1, n1, saved00[1:3], weights_a0)
    sum1 = chip_sum(keep, give, sum0[1])
    lead_a1 = cross_send(jnp.where(even, *after((other_a[:2], other_a[2:]), sum0[0])))
    middle00, n0 = middle(0, row0, sum0)
    keep, give, slope0 = units(0, n0, weights_b0)
    sum2 = chip_sum(keep, give, sum1[1])
    sum1, lead_a1 = lax.optimization_barrier((sum1, lead_a1))
    trail_a1 = z_swap(lead_a1)
    lead_b1 = cross_send(jnp.where(even, *after((other_w1, other_w2), lead_a1)))
    middle01, n1 = middle(0, row1, sum1)
    keep, give, slope1 = units(0, n1, weights_b0)
    sum3 = chip_sum(keep, give, sum2[1])
    sum2, trail_a1 = lax.optimization_barrier((sum2, trail_a1))
    weights_a1 = (own_a, other_a, lead_a1, trail_a1)
    between0, n10 = small(rows_next_kernel, middle00, *sum2, shared, outs=[thin, thin], name="rows_next")
    saved10, keep, give = attend(1, 0, n10, (), weights_a1)
    sum4 = chip_sum(keep, give, sum3[1])
    sum3, lead_b1 = lax.optimization_barrier((sum3, lead_b1))
    trail_b1 = z_swap(lead_b1)
    weights_b1 = (w1_own, w2_own, other_w1, other_w2, lead_b1, trail_b1)
    between1, n11 = small(rows_next_kernel, middle01, *sum3, shared, outs=[thin, thin], name="rows_next")
    saved11, keep, give = attend(1, 1, n11, saved10[1:3], weights_a1)
    sum5 = chip_sum(keep, give, sum4[1])
    holder, upper = section == x, y == 0
    mine, crossed = (
        jnp.where(holder, one, two) for one, two in zip((g_mine, g_crossed), after(g_far, sum4[0]))
    )
    grad_outs = (jnp.where(upper, mine, crossed), jnp.where(upper, crossed, mine))
    near_outs = [other_core(one) for one in grad_outs]
    middle10, m0 = middle(1, between0, sum4)
    keep, give, out_keep0, out_give0 = units_turn(1, m0, grad_outs[0], near_outs[0], weights_b1)
    sum6 = chip_sum(keep, give, sum5[1])
    middle11, m1 = middle(1, between1, sum5)
    keep, give, out_keep1, out_give1 = units_turn(1, m1, grad_outs[1], near_outs[1], weights_b1)
    sum7 = chip_sum(keep, give, sum6[1])
    grad_middle10, g0 = turn(1, middle10, grad_outs[0], sum6)
    grad_middle11, g1 = turn(1, middle11, grad_outs[1], sum7)
    keep, give, down1, up1, dk, dv = attend_back_call(
        1, 1, meta, (n11, other_core(n11)), (g1, other_core(g1)), (saved10, saved11), (), shared,
        near_varied, weights_a1,
    )
    out_sums = [
        chip_sum(*after(one, g1), sum7[1], from_x)
        for one in ((out_keep0, out_give0), (out_keep1, out_give1))
    ]
    keep, give, out_sums = lax.optimization_barrier((keep, give, out_sums))
    sum8 = chip_sum(keep, give, sum7[1])
    keep, give, down1, up1 = attend_back_call(
        1, 0, meta, (n10, other_core(n10)), (g0, other_core(g0)), (saved10, saved11),
        (dk, dv, down1, up1), shared, near_varied, weights_a1,
    )
    sum9 = chip_sum(keep, give, sum8[1])
    before1 = small(
        rows_before_kernel, grad_middle11, *after(sum8, keep), between1, shared, outs=[thin], name="rows_before"
    )[0]
    keep, give = units_back(0, before1, slope1, weights_b0)
    sum10 = early_sum(keep, give)
    sum9 = (sum9[0], after(sum9[1], sum10[0]))
    before0 = small(
        rows_before_kernel, grad_middle10, *sum9, between0, shared, outs=[thin], name="rows_before"
    )[0]
    keep, give = units_back(0, before0, slope0, weights_b0)
    sum11 = early_sum(keep, give)
    sum10 = (sum10[0], after(sum10[1], sum11[0]))
    grad_middle01, h1 = turn(0, middle01, before1, sum10)
    keep, give, down0, up0, dk, dv = attend_back_call(
        0, 1, meta, (n01, other_core(n01)), (h1, other_core(h1)), (saved00, saved01), (), shared,
        near_varied, weights_a0,
    )
    sum12 = early_sum(keep, give, from_x)
    sum11 = (sum11[0], after(sum11[1], sum12[0]))
    grad_middle00, h0 = turn(0, middle00, before0, sum11)
    keep, give, down0, up0 = attend_back_call(
        0, 0, meta, (n00, other_core(n00)), (h0, other_core(h0)), (saved00, saved01),
        (dk, dv, down0, up0), shared, near_varied, weights_a0,
    )
    sum13 = early_sum(keep, give, from_x)
    sum12 = (sum12[0], after(sum12[1], sum13[0]))
    outs = [
        small(rows_output_kernel, one, *after(two, sum13[0]), shared, outs=[sheet, thin],
              name="rows_output")
        for one, two in zip((middle10, middle11), out_sums)
    ]
    out_wide = jnp.where(upper, outs[0][0], outs[1][0])
    out_same, out_cross = collect(1, out_wide, jnp.where(upper, outs[1][1], outs[0][1]))
    totals = total_over_z((down0, down1), after((up0, up1), sum13[0]))
    sum13, totals = lax.optimization_barrier((sum13, totals))
    ends = [
        small(rows_final_kernel, one, *two, three, shared, outs=[sheet, thin], name="rows_final")
        for one, two, three in ((grad_middle00, sum13, row0), (grad_middle01, sum12, row1))
    ]
    wide = jnp.where(upper, ends[0][0], ends[1][0])
    in_same, in_cross = collect(0, wide, jnp.where(upper, ends[1][1], ends[0][1]))
    grad_down, grad_up = total_over_cores(totals, section, y)
    same = jnp.where(
        first, jnp.where(x == 0, wide, in_same), jnp.where(x == 1, out_wide, out_same)
    )
    cross = jnp.where(first, in_cross, out_cross).astype(f32)
    combined = jnp.where(y == 0, jnp.stack([same, cross]), jnp.stack([cross, same]))
    return (
        combined[None],
        grad_down.reshape(1, 2, ADAPTER_RANK, 1024).transpose(0, 1, 3, 2),
        jnp.stack([grad_up[:ADAPTER_RANK, :256], grad_up[ADAPTER_RANK:, 256:]])[None],
    )


def body(*arrays):
    dp = lax.axis_size("dp")
    known = (
        arrays[0].shape == (1, 2, BLOCK, 1024)
        and lax.axis_size("tensor") == 4
        and lax.axis_size("section") == 2
        and arrays[3].shape == (1, 256, 1024)
        and arrays[5].shape == (1, 1024, 1024)
        and dp & (dp - 1) == 0
    )
    return relay_body(*arrays) if known else plain_body(*arrays)


def solution(mesh):
    placed = (
        P("section", None, ("dp", "tensor"), None),
        P(None, "dp", None),
        P("section", None, None, "tensor"),
        P("section", "tensor", None),
        P("section", None, "tensor"),
        P("section", "tensor", None),
        P("section", None, None),
        P("section", None, None),
        P("section", None, None),
        P("section", None, "tensor"),
        P("section", "tensor"),
        P("section", None, None, None),
        P("section", None, None, "tensor"),
    )
    return jax.shard_map(
        body,
        mesh=mesh,
        in_specs=placed,
        out_specs=(
            P("section", None, ("dp", "tensor"), None),
            P("section", None, None, None),
            P("section", None, None, "tensor"),
        ),
        check_vma=False,
    )
```

```python
import functools

import jax
import jax.numpy as jnp
from jax import lax
from jax.experimental import pallas as pl
from jax.experimental.pallas import tpu as pltpu
from jax.sharding import PartitionSpec as P

HEAD = 64
ADAPTER_RANK = 4
SEQ_LEN = 1024


adapter_scale = 8.0


def from_behind(block, axis, distance):
    devices = range(lax.axis_size(axis))
    route = [(i - distance, i) for i in devices if i - distance in devices]
    return lax.ppermute(block, axis, route)


def contract_axes(left, right, left_dim, right_dim):
    return lax.dot_general(
        left, right, (((left_dim,), (right_dim,)), ((), ())), preferred_element_type=jnp.float32
    )


def layer_norm(rows, gain, shift):
    mean = jnp.mean(rows, axis=-1, keepdims=True)
    centered = rows - mean
    spread = jnp.mean(centered * centered, axis=-1, keepdims=True)
    return centered * lax.rsqrt(spread + 1e-05) * gain + shift


def gelu_tanh(value):
    return (
        0.5
        * value
        * (1.0 + jnp.tanh(0.7978845608028654 * (value + 0.044715 * value * value * value)))
    )


def doc_mask(doc_starts):
    positions = jnp.arange(SEQ_LEN, dtype=jnp.int32)
    labels = jnp.sum((doc_starts[None, :] <= positions[:, None]).astype(jnp.int32), axis=1)
    return (positions[None, :] <= positions[:, None]) & (labels[:, None] == labels[None, :])


def masked_scores(query_rows, keys, doc_starts):
    scores = jnp.einsum(
        "qhd,khd->hqk", query_rows, keys, preferred_element_type=jnp.float32
    ) * HEAD ** (-0.5)
    return jnp.where(doc_mask(doc_starts)[None], scores, -1e30)


def attend(items):
    query_rows, keys, value_rows, doc_starts = items
    scores = masked_scores(query_rows, keys, doc_starts)
    top = jnp.max(scores, axis=-1, keepdims=True)
    weights = jnp.exp(scores - top)
    total = jnp.sum(weights, axis=-1, keepdims=True)
    mixed = jnp.einsum(
        "hqk,khd->qhd",
        (weights / total).astype(jnp.bfloat16),
        value_rows,
        preferred_element_type=jnp.float32,
    )
    return (mixed.astype(jnp.bfloat16), (top + jnp.log(total))[:, :, 0])


def attend_back(items):
    query_rows, keys, value_rows, doc_starts, log_totals, grad_mixed = items
    scores = masked_scores(query_rows, keys, doc_starts)
    probs = jnp.exp(scores - log_totals[:, :, None])
    grad_probs = jnp.einsum(
        "qhd,khd->hqk", grad_mixed, value_rows, preferred_element_type=jnp.float32
    )
    inner = jnp.sum(probs * grad_probs, axis=-1, keepdims=True)
    grad_scores = (probs * (grad_probs - inner)).astype(jnp.bfloat16)
    query_gradient = jnp.einsum(
        "hqk,khd->qhd", grad_scores, keys, preferred_element_type=jnp.float32
    ) * HEAD ** (-0.5)
    grad_k = jnp.einsum(
        "hqk,qhd->khd", grad_scores, query_rows, preferred_element_type=jnp.float32
    ) * HEAD ** (-0.5)
    value_gradient = jnp.einsum(
        "hqk,qhd->khd", probs.astype(jnp.bfloat16), grad_mixed, preferred_element_type=jnp.float32
    )
    return (
        query_gradient.astype(jnp.bfloat16),
        grad_k.astype(jnp.bfloat16),
        value_gradient.astype(jnp.bfloat16),
    )


def reduce_adapters(part_a, second_portion):
    return (lax.psum(part_a, ("dp", "tensor")), lax.psum(second_portion, "dp"))


def plain_body(
    activations,
    starts,
    attention_weights,
    projection_weight,
    feedforward_weight,
    output_weight,
    norm_gains,
    norm_biases,
    output_biases,
    query_value_bias,
    feedforward_bias,
    adapter_down_weight,
    adapter_up_weight,
):
    section = lax.axis_index("section")
    first = section == 0
    batches = activations.shape[1]
    own_rows = activations.shape[2]
    width = activations.shape[3]
    head_cols = projection_weight.shape[1]
    local_heads = head_cols // HEAD
    shaped = (-1, SEQ_LEN, local_heads, HEAD)
    w_cat = jnp.concatenate(
        [attention_weights[0, 0], attention_weights[0, 1], attention_weights[0, 2]], axis=1
    )
    stacked_down_maps = jnp.concatenate(
        [adapter_down_weight[0, 0], adapter_down_weight[0, 1]], axis=1
    )

    def forward_relay(rows, group_starts):
        normalized_rows = layer_norm(rows, norm_gains[0, 0], norm_biases[0, 0]).astype(jnp.bfloat16)
        gathered = lax.all_gather(normalized_rows, "tensor", axis=0, tiled=True)
        joined = jnp.dot(gathered, w_cat, preferred_element_type=jnp.float32)
        apply_adapter = jnp.dot(
            gathered, stacked_down_maps, preferred_element_type=jnp.float32
        ).astype(jnp.bfloat16)
        query_rows = (
            joined[:, :head_cols]
            + query_value_bias[0, 0]
            + adapter_scale
            * jnp.dot(
                apply_adapter[:, :ADAPTER_RANK],
                adapter_up_weight[0, 0],
                preferred_element_type=jnp.float32,
            )
        ).astype(jnp.bfloat16)
        keys = joined[:, head_cols : 2 * head_cols].astype(jnp.bfloat16)
        value_rows = (
            joined[:, 2 * head_cols :]
            + query_value_bias[0, 1]
            + adapter_scale
            * jnp.dot(
                apply_adapter[:, ADAPTER_RANK:],
                adapter_up_weight[0, 1],
                preferred_element_type=jnp.float32,
            )
        ).astype(jnp.bfloat16)
        mixed, log_totals = lax.map(
            attend,
            (
                query_rows.reshape(shaped),
                keys.reshape(shaped),
                value_rows.reshape(shaped),
                group_starts,
            ),
        )
        mixed = mixed.reshape(-1, head_cols)
        middle = (
            rows
            + lax.psum_scatter(
                jnp.dot(mixed, projection_weight[0], preferred_element_type=jnp.float32),
                "tensor",
                scatter_dimension=0,
                tiled=True,
            )
            + output_biases[0, 0]
        )
        normed_two = layer_norm(middle, norm_gains[0, 1], norm_biases[0, 1]).astype(jnp.bfloat16)
        hidden = (
            jnp.dot(
                lax.all_gather(normed_two, "tensor", axis=0, tiled=True),
                feedforward_weight[0],
                preferred_element_type=jnp.float32,
            )
            + feedforward_bias[0]
        )
        active = gelu_tanh(hidden).astype(jnp.bfloat16)
        output = (
            middle
            + lax.psum_scatter(
                jnp.dot(active, output_weight[0], preferred_element_type=jnp.float32).astype(
                    jnp.bfloat16
                ),
                "tensor",
                scatter_dimension=0,
                tiled=True,
            ).astype(jnp.float32)
            + output_biases[0, 1]
        )
        return (
            output,
            (
                rows,
                middle,
                gathered,
                apply_adapter,
                query_rows,
                keys,
                value_rows,
                log_totals,
                hidden,
            ),
        )

    def backward_relay(grad_rows, cache, group_starts):
        rows, middle, gathered, apply_adapter, query_rows, keys, value_rows, log_totals, hidden = (
            cache
        )
        grad_active = contract_axes(
            lax.all_gather(grad_rows.astype(jnp.bfloat16), "tensor", axis=0, tiled=True),
            output_weight[0],
            1,
            1,
        )
        _, gelu_back = jax.vjp(gelu_tanh, hidden)
        grad_hidden = gelu_back(grad_active)[0].astype(jnp.bfloat16)
        grad_normed_two = lax.psum_scatter(
            contract_axes(grad_hidden, feedforward_weight[0], 1, 1).astype(jnp.bfloat16),
            "tensor",
            scatter_dimension=0,
            tiled=True,
        ).astype(jnp.float32)
        _, norm_two_back = jax.vjp(
            lambda inner_rows: layer_norm(inner_rows, norm_gains[0, 1], norm_biases[0, 1]), middle
        )
        grad_middle = grad_rows + norm_two_back(grad_normed_two)[0]
        grad_mixed = contract_axes(
            lax.all_gather(grad_middle.astype(jnp.bfloat16), "tensor", axis=0, tiled=True),
            projection_weight[0],
            1,
            1,
        ).astype(jnp.bfloat16)
        query_gradient, grad_k, value_gradient = lax.map(
            attend_back,
            (
                query_rows.reshape(shaped),
                keys.reshape(shaped),
                value_rows.reshape(shaped),
                group_starts,
                log_totals,
                grad_mixed.reshape(shaped),
            ),
        )
        query_gradient = query_gradient.reshape(-1, head_cols)
        grad_k = grad_k.reshape(-1, head_cols)
        value_gradient = value_gradient.reshape(-1, head_cols)
        grad_low = jnp.concatenate(
            [
                adapter_scale * contract_axes(query_gradient, adapter_up_weight[0, 0], 1, 1),
                adapter_scale * contract_axes(value_gradient, adapter_up_weight[0, 1], 1, 1),
            ],
            axis=1,
        ).astype(jnp.bfloat16)
        grad_joined = jnp.concatenate([query_gradient, grad_k, value_gradient], axis=1)
        grad_normed = lax.psum_scatter(
            (
                contract_axes(grad_joined, w_cat, 1, 1)
                + contract_axes(grad_low, stacked_down_maps, 1, 1)
            ).astype(jnp.bfloat16),
            "tensor",
            scatter_dimension=0,
            tiled=True,
        ).astype(jnp.float32)
        _, norm_back = jax.vjp(
            lambda inner_rows: layer_norm(inner_rows, norm_gains[0, 0], norm_biases[0, 0]), rows
        )
        grad_in = grad_middle + norm_back(grad_normed)[0]
        grad_down = contract_axes(gathered, grad_low, 0, 0)
        part_a = jnp.stack([grad_down[:, :ADAPTER_RANK], grad_down[:, ADAPTER_RANK:]])
        second_portion = adapter_scale * jnp.stack(
            [
                contract_axes(apply_adapter[:, :ADAPTER_RANK], query_gradient, 0, 0),
                contract_axes(apply_adapter[:, ADAPTER_RANK:], value_gradient, 0, 0),
            ]
        )
        return (grad_in, part_a, second_portion)

    received = jnp.zeros((own_rows, width), jnp.bfloat16)
    finals = []
    stored = []
    for tick in range(batches + 1):
        batch_index = jnp.clip(tick - section, 0, batches - 1)
        own = lax.dynamic_index_in_dim(activations[0], batch_index, 0, keepdims=False)
        rows = jnp.where(first, own, received).astype(jnp.float32)
        group_starts = lax.dynamic_index_in_dim(starts, batch_index, 0, keepdims=False)
        output, cache = forward_relay(rows, group_starts)
        finals.append(output)
        stored.append(rows)
        if tick < batches:
            received = from_behind(output.astype(jnp.bfloat16), "section", 1)
    stacked = jax.tree.map(lambda *items: jnp.stack(items), *stored)
    returned = jnp.zeros((own_rows, width), jnp.bfloat16)
    totals_a = jnp.zeros((2, width, ADAPTER_RANK), jnp.float32)
    totals_b = jnp.zeros((2, ADAPTER_RANK, head_cols), jnp.float32)
    grads_in = []
    for tick in range(batches + 1):
        position = tick - 1 + section
        batch_index = jnp.clip(position, 0, batches - 1)
        valid = ((position >= 0) & (position < batches)).astype(jnp.float32)
        own = lax.dynamic_index_in_dim(activations[0], batch_index, 0, keepdims=False)
        grad_rows = jnp.where(first, returned, own).astype(jnp.float32) * valid
        group_starts = lax.dynamic_index_in_dim(starts, batch_index, 0, keepdims=False)
        slot_index = jnp.clip(tick - 1 + 2 * section, 0, batches)
        picked = lax.dynamic_index_in_dim(stacked, slot_index, 0, keepdims=False)
        _, cache = forward_relay(picked, group_starts)
        grad_in, part_a, second_portion = backward_relay(grad_rows, cache, group_starts)
        grads_in.append(grad_in)
        if tick < batches:
            returned = from_behind(grad_in.astype(jnp.bfloat16), "section", -1)
        part_a, second_portion = reduce_adapters(part_a, second_portion)
        totals_a = totals_a + part_a
        totals_b = totals_b + second_portion
    combined = jnp.stack(
        [jnp.where(first, grads_in[index + 1], finals[index + 1]) for index in range(batches)]
    )
    return (combined[None], totals_a[None], totals_b[None])


LOW = 2 * ADAPTER_RANK
VMEM_SPACE = pl.BlockSpec(memory_space=pltpu.VMEM)
SMEM_SPACE = pl.BlockSpec(memory_space=pltpu.SMEM)
HBM_SPACE = pl.BlockSpec(memory_space=pltpu.HBM)
BLOCK = 256
CHUNK = 2 * BLOCK


def send(block, route):
    pairs = []
    for s in range(2):
        for t in range(4):
            to = route(s, t)
            if to is not None:
                pairs.append((s * 4 + t, to[0] * 4 + to[1]))
    return lax.ppermute(block, ("section", "tensor"), pairs)


def other_core(block):
    return send(block, lambda s, t: (1 - s, t))


def x_swap(block):
    return send(block, lambda s, t: (s, t ^ 1))


def y_swap(block):
    return send(block, lambda s, t: (s, t ^ 2))


def after(value, *others):
    return lax.optimization_barrier((value, others))[0]


def cross_send(block, source=0):
    return send(block, lambda s, t: (t >> 1, t ^ 2) if s == source else None)


def collect(target, same_chip, cross_chip):
    return (
        send(same_chip, lambda s, t: (target, t) if s == t & 1 and s != target else None),
        send(cross_chip, lambda s, t: (target, t ^ 2) if s == t & 1 else None),
    )


def mm(left, right):
    return jnp.dot(left, right, preferred_element_type=jnp.float32)


def mm_nt(left, right):
    return contract_axes(left, right, 1, 1)


def norm_back(rows, gain, grad):
    mean = jnp.mean(rows, axis=-1, keepdims=True)
    centered = rows - mean
    scale = lax.rsqrt(jnp.mean(centered * centered, axis=-1, keepdims=True) + 1e-05)
    unit = centered * scale
    scaled = grad * gain
    return scale * (
        scaled
        - jnp.mean(scaled, axis=-1, keepdims=True)
        - unit * jnp.mean(scaled * unit, axis=-1, keepdims=True)
    )


def gelu_both(value):
    square = value * value
    bent = jnp.tanh(0.7978845608028654 * value * (1.0 + 0.044715 * square))
    half = 0.5 * (1.0 + bent)
    slope = half + 0.5 * value * (1.0 - bent * bent) * (
        0.7978845608028654 * (1.0 + 3.0 * 0.044715 * square)
    )
    return value * half, slope


def cost(flops, read):
    return pl.CostEstimate(flops=1000, bytes_accessed=1000, transcendentals=0)


def kernel_params(mib):
    return pltpu.CompilerParams(vmem_limit_bytes=mib * 1024 * 1024)


def position_mask(meta, query_block, key_block):
    shape = (BLOCK, BLOCK)
    key_pos = key_block * BLOCK + lax.broadcasted_iota(jnp.int32, shape, 0)
    query_pos = query_block * BLOCK + lax.broadcasted_iota(jnp.int32, (1, BLOCK), 1)
    low = jnp.zeros((1, BLOCK), jnp.int32)
    for c in range(4):
        first = meta[4 + c]
        low = jnp.where(first <= query_pos, jnp.maximum(low, first), low)
    valid = key_pos >= low
    if query_block == key_block:
        valid = valid & (key_pos <= query_pos)
    return valid


def lay_mask(meta, chunk, target):
    for i in range(2):
        for j in range(2 * chunk + i + 1):
            target[tile(chunk, i, j)] = jnp.where(
                position_mask(meta, 2 * chunk + i, j), 0.0, -1e30
            )


def tile(chunk, i, j):
    return i * (2 * chunk + 1) + j


def head_lanes(half):
    return (lax.broadcasted_iota(jnp.int32, (1, 2 * HEAD), 1) // HEAD) == half


def start_pick(choices, target, sem):
    for condition, source in choices:

        @pl.when(condition)
        def _(source=source):
            pltpu.make_async_copy(source, target, sem).start()


def load_qkv_weight(layer, meta, pieces, w_buf, sem):
    own, other, lead, trail = pieces
    s, y, w = meta[0], meta[2], meta[8]
    start_pick(
        (((s == y) & (s == layer), own), ((s == y) & (s != layer), other)), w_buf, sem
    )

    @pl.when(s != y)
    def _():
        for part, side in ((lead, w), (trail, 1 - w)):
            pltpu.make_async_copy(part, w_buf.at[pl.ds(2 * side, 2)], sem).start()

    return pltpu.make_async_copy(own, w_buf, sem)


def half_rows(core):
    return pl.ds(pl.multiple_of(core * BLOCK, BLOCK), BLOCK)


def lay_out(meta, own, near, target):
    s = meta[0]
    target[half_rows(s), :] = own[...]
    target[half_rows(1 - s), :] = near[...]


def share_out(meta, source, keep, give):
    s = meta[0]
    keep[...] = source[half_rows(s), :]
    give[...] = source[half_rows(1 - s), :]


def attend_kernel(layer, chunk, meta, shared, varied, own, near, *rest):
    before, rest = rest[: 2 * chunk], rest[2 * chunk :]
    q_out, k_out, v_out, lse_out, mixed_out, keep, give = rest[4:11]
    (
        n_buf, w_buf, score_buf, mask_buf, vt_buf, q_ref, k_ref, v_ref, lse_ref, mixed_ref, sem,
        out_sems,
    ) = rest[11:]
    loaded = load_qkv_weight(layer, meta, rest[:4], w_buf, sem)
    down = shared[layer, 8:16, :].astype(jnp.bfloat16)
    bias = varied[layer, 1:2, :]
    up = varied[layer, 8:16, 0:512].astype(jnp.bfloat16)
    lay_out(meta, own, near, n_buf)
    lay_mask(meta, chunk, mask_buf)
    keys = [k_ref] if chunk == 0 else [before[0], k_ref]
    if chunk == 1:
        for b in range(2):
            span = slice(b * BLOCK, (b + 1) * BLOCK)
            vt_buf[:, span] = before[1][span, :].T
    loaded.wait()
    normed = n_buf[...]
    low = mm_nt(normed, down).astype(jnp.bfloat16)
    lifted = adapter_scale * mm(low, up)
    q_ref[...] = (mm(normed, w_buf[0]) + bias[:, 0:256] + lifted[:, 0:256]).astype(jnp.bfloat16)
    k_ref[...] = mm(normed, w_buf[1]).astype(jnp.bfloat16)
    v_ref[...] = (mm(normed, w_buf[2]) + bias[:, 256:512] + lifted[:, 256:512]).astype(jnp.bfloat16)
    saved = [
        pltpu.make_async_copy(source, target, out_sems.at[i])
        for i, (source, target) in enumerate(
            (
                (q_ref, q_out), (k_ref, k_out), (v_ref, v_out), (lse_ref, lse_out),
                (mixed_ref, mixed_out),
            )
        )
    ]
    for copy in saved[:3]:
        copy.start()
    for b in range(2):
        span = slice(b * BLOCK, (b + 1) * BLOCK)
        vt_buf[:, chunk * CHUNK + b * BLOCK : chunk * CHUNK + (b + 1) * BLOCK] = v_ref[span, :].T

    def one_head(head, carry):
        lanes = pl.ds(pl.multiple_of((head // 2) * 128, 128), 128)
        chosen = head_lanes(head % 2)
        deep = pl.ds(pl.multiple_of(head * HEAD, HEAD), HEAD)
        for i in range(2):
            span = slice(i * BLOCK, (i + 1) * BLOCK)
            place = 2 * chunk + i
            query = jnp.where(chosen, q_ref[span, lanes] * HEAD ** (-0.5), 0.0).astype(jnp.bfloat16)
            top = jnp.full((1, BLOCK), -1e30, jnp.float32)
            for j in range(place + 1):
                rows = slice((j % 2) * BLOCK, (j % 2 + 1) * BLOCK)
                scores = mm_nt(keys[j // 2][rows, lanes], query) + mask_buf[tile(chunk, i, j)]
                score_buf[j] = scores
                top = jnp.maximum(top, jnp.max(scores, axis=0, keepdims=True))
            total = jnp.zeros((1, BLOCK), jnp.float32)
            mixed = jnp.zeros((HEAD, BLOCK), jnp.float32)
            for j in range(place + 1):
                weights = jnp.exp(score_buf[j] - top)
                total = total + jnp.sum(weights, axis=0, keepdims=True)
                mixed = mixed + mm(
                    vt_buf[deep, j * BLOCK : (j + 1) * BLOCK], weights.astype(jnp.bfloat16)
                )
            mixed_ref[deep, span] = mixed / total
            lse_ref[pl.ds(head, 1), span] = top + jnp.log(total)
        return carry

    lax.fori_loop(0, 4, one_head, 0, unroll=4)
    for copy in saved[3:]:
        copy.start()
    for b in range(2):
        span = slice(b * BLOCK, (b + 1) * BLOCK)
        n_buf[span, :] = mm_nt(
            mixed_ref[:, span].T.astype(jnp.bfloat16), w_buf[3]
        ).astype(jnp.bfloat16)
    share_out(meta, n_buf, keep, give)
    for copy in saved:
        copy.wait()


def attend_call(layer, chunk, meta, blocks, before, shared, varied, weight):
    bf, f32 = jnp.bfloat16, jnp.float32
    wide = jax.ShapeDtypeStruct((CHUNK, 256), bf)
    piece = jax.ShapeDtypeStruct((BLOCK, 1024), bf)
    *saved, keep, give = pl.pallas_call(
        functools.partial(attend_kernel, layer, chunk),
        in_specs=[SMEM_SPACE] + [VMEM_SPACE] * (4 + 2 * chunk) + [HBM_SPACE] * 4,
        out_specs=[HBM_SPACE] * 5 + [VMEM_SPACE] * 2,
        out_shape=[wide, wide, wide, jax.ShapeDtypeStruct((8, CHUNK), f32),
                   jax.ShapeDtypeStruct((256, CHUNK), f32), piece, piece],
        scratch_shapes=[
            pltpu.VMEM((CHUNK, 1024), bf),
            pltpu.VMEM((4, 1024, 256), bf),
            pltpu.VMEM((2 + 2 * chunk, BLOCK, BLOCK), f32),
            pltpu.VMEM((3 + 4 * chunk, BLOCK, BLOCK), f32),
            pltpu.VMEM((256, CHUNK * (1 + chunk)), bf),
            pltpu.VMEM((CHUNK, 256), bf),
            pltpu.VMEM((CHUNK, 256), bf),
            pltpu.VMEM((CHUNK, 256), bf),
            pltpu.VMEM((8, CHUNK), f32),
            pltpu.VMEM((256, CHUNK), f32),
            pltpu.SemaphoreType.DMA,
            pltpu.SemaphoreType.DMA((5,)),
        ],
        compiler_params=kernel_params(24),
        cost_estimate=cost(3.5e9, 8e6),
        name="attention_forward_%d" % chunk,
    )(meta, shared, varied, *blocks, *(before if chunk else ()), *weight)
    return saved, keep, give


def attend_back_kernel(layer, chunk, meta, shared, varied, n_own, n_near, g_own, g_near, *rest):
    n_saved = 5 + 2 * chunk
    saved, rest = rest[:n_saved], rest[n_saved:]
    saved_sems, rest = rest[-1], rest[:-1]
    bufs, rest = rest[-n_saved:], rest[:-n_saved]
    fetches = [
        pltpu.make_async_copy(source, target, saved_sems.at[i])
        for i, (source, target) in enumerate(zip(saved, bufs))
    ]
    for fetch in fetches:
        fetch.start()
    q_ref, lse_ref, mixed_ref = bufs[:3]
    keys, values = bufs[3 : 4 + chunk], bufs[4 + chunk :]
    if chunk == 0:
        dk_in, dv_in, down_in, up_in = rest[:4]
        keep, give, down_ref, up_ref = rest[8:12]
        weight, scratch = rest[4:8], rest[12:]
    else:
        keep, give, down_ref, up_ref, dk_out, dv_out = rest[4:10]
        weight, scratch = rest[:4], rest[10:]
    (
        n_buf, g_buf, w_buf, mask_buf, kt_buf, do_buf, delta_buf, dqt_buf, dk_buf, dv_buf, dq_buf,
        sem,
    ) = scratch
    loaded = load_qkv_weight(layer, meta, weight, w_buf, sem)
    lay_out(meta, g_own, g_near, g_buf)
    lay_out(meta, n_own, n_near, n_buf)
    lay_mask(meta, chunk, mask_buf)
    for fetch in fetches:
        fetch.wait()
    for j in range(2 + 2 * chunk):
        rows = slice((j % 2) * BLOCK, (j % 2 + 1) * BLOCK)
        kt_buf[:, j * BLOCK : (j + 1) * BLOCK] = keys[j // 2][rows, :].T
    if chunk == 0:
        dk_buf[...] = dk_in[...]
        dv_buf[...] = dv_in[...]
    else:
        dk_buf[...] = jnp.zeros_like(dk_buf)
        dv_buf[...] = jnp.zeros_like(dv_buf)
    loaded.wait()
    do_buf[...] = mm(g_buf[...], w_buf[3]).astype(jnp.bfloat16)
    for b in range(2):
        span = slice(b * BLOCK, (b + 1) * BLOCK)
        product = do_buf[span, :].astype(jnp.float32).T * mixed_ref[:, span]
        for head in range(4):
            delta_buf[head : head + 1, span] = jnp.sum(
                product[head * HEAD : (head + 1) * HEAD], axis=0, keepdims=True
            )

    def one_head(head, carry):
        lanes = pl.ds(pl.multiple_of((head // 2) * 128, 128), 128)
        chosen = head_lanes(head % 2)
        deep = pl.ds(pl.multiple_of(head * HEAD, HEAD), HEAD)
        for i in range(2):
            span = slice(i * BLOCK, (i + 1) * BLOCK)
            place = 2 * chunk + i
            query = jnp.where(chosen, q_ref[span, lanes] * HEAD ** (-0.5), 0.0).astype(jnp.bfloat16)
            grad_mixed = jnp.where(chosen, do_buf[span, lanes], 0.0).astype(jnp.bfloat16)
            lse = lse_ref[pl.ds(head, 1), span]
            delta = delta_buf[pl.ds(head, 1), span]
            grad_query = jnp.zeros((HEAD, BLOCK), jnp.float32)
            for j in range(place + 1):
                rows = slice((j % 2) * BLOCK, (j % 2 + 1) * BLOCK)
                all_rows = slice(j * BLOCK, (j + 1) * BLOCK)
                scores = mm_nt(keys[j // 2][rows, lanes], query) + mask_buf[tile(chunk, i, j)]
                probs = jnp.exp(scores - lse)
                grad_probs = mm_nt(values[j // 2][rows, lanes], grad_mixed)
                grad_scores = (probs * (grad_probs - delta)).astype(jnp.bfloat16)
                dv_buf[all_rows, lanes] += mm(probs.astype(jnp.bfloat16), grad_mixed)
                dk_buf[all_rows, lanes] += mm(grad_scores, query)
                grad_query = grad_query + mm(kt_buf[deep, all_rows], grad_scores)
            dqt_buf[deep, span] = grad_query * HEAD ** (-0.5)
        return carry

    lax.fori_loop(0, 4, one_head, 0, unroll=4)
    down = shared[layer, 8:16, :].astype(jnp.bfloat16)
    up = varied[layer, 8:16, 0:512].astype(jnp.bfloat16)
    for b in range(2):
        span = slice(b * BLOCK, (b + 1) * BLOCK)
        dq_buf[span, :] = dqt_buf[:, span].T.astype(jnp.bfloat16)
    done = slice(chunk * CHUNK, (chunk + 1) * CHUNK)
    normed = n_buf[...]
    grad_q = dq_buf[...]
    grad_k = dk_buf[done, :].astype(jnp.bfloat16)
    grad_v = dv_buf[done, :].astype(jnp.bfloat16)
    both = jnp.concatenate([grad_q, grad_v], axis=1)
    low_grad = (adapter_scale * mm_nt(both, up)).astype(jnp.bfloat16)
    low_grad_t = (adapter_scale * mm_nt(up, both)).astype(jnp.bfloat16)
    low_t = mm_nt(down, normed).astype(jnp.bfloat16)
    g_buf[...] = (
        mm_nt(grad_q, w_buf[0]) + mm_nt(grad_k, w_buf[1]) + mm_nt(grad_v, w_buf[2])
        + mm(low_grad, down)
    ).astype(jnp.bfloat16)
    share_out(meta, g_buf, keep, give)
    total_down = mm(low_grad_t, normed)
    total_up = adapter_scale * mm(low_t, both)
    if chunk == 0:
        total_down = total_down + down_in[...]
        total_up = total_up + up_in[...]
    else:
        dk_out[...] = dk_buf[0:CHUNK, :]
        dv_out[...] = dv_buf[0:CHUNK, :]
    down_ref[...] = total_down
    up_ref[...] = total_up


def attend_back_call(layer, chunk, meta, blocks, grads, saved, carried, shared, varied, weight):
    bf, f32 = jnp.bfloat16, jnp.float32
    piece = jax.ShapeDtypeStruct((BLOCK, 1024), bf)
    tall = jax.ShapeDtypeStruct((CHUNK, 256), f32)
    spans = CHUNK * (1 + chunk)
    q, _, _, lse, mixed = saved[chunk]
    keys = [one[1] for one in saved[: chunk + 1]]
    values = [one[2] for one in saved[: chunk + 1]]
    held = (q, lse, mixed, *keys, *values)
    inputs = (shared, varied, *blocks, *grads, *held, *carried)
    return pl.pallas_call(
        functools.partial(attend_back_kernel, layer, chunk),
        in_specs=[SMEM_SPACE] + [VMEM_SPACE] * 6 + [HBM_SPACE] * len(held)
        + [VMEM_SPACE] * len(carried) + [HBM_SPACE] * 4,
        out_specs=[VMEM_SPACE] * (4 + 2 * chunk),
        out_shape=[piece, piece, jax.ShapeDtypeStruct((LOW, 1024), f32),
                   jax.ShapeDtypeStruct((LOW, 512), f32)] + [tall] * (2 * chunk),
        scratch_shapes=[
            pltpu.VMEM((CHUNK, 1024), bf),
            pltpu.VMEM((CHUNK, 1024), bf),
            pltpu.VMEM((4, 1024, 256), bf),
            pltpu.VMEM((3 + 4 * chunk, BLOCK, BLOCK), f32),
            pltpu.VMEM((256, spans), bf),
            pltpu.VMEM((CHUNK, 256), bf),
            pltpu.VMEM((8, CHUNK), f32),
            pltpu.VMEM((256, CHUNK), f32),
            pltpu.VMEM((spans, 256), f32),
            pltpu.VMEM((spans, 256), f32),
            pltpu.VMEM((CHUNK, 256), bf),
            pltpu.SemaphoreType.DMA,
            *[pltpu.VMEM(one.shape, one.dtype) for one in held],
            pltpu.SemaphoreType.DMA((len(held),)),
        ],
        compiler_params=kernel_params(24),
        cost_estimate=cost(6e9, 12e6),
        name="attention_backward_%d" % chunk,
    )(meta, *inputs, *weight)


def summed(passed, far):
    return passed[...].astype(jnp.float32) + far[...].astype(jnp.float32)


def rows_middle_kernel(layer, h_ref, passed, far, shared, middle_ref, normed_ref):
    middle = h_ref[...].astype(jnp.float32) + summed(passed, far) + shared[layer, 4:5, :]
    middle_ref[...] = middle
    normed_ref[...] = layer_norm(middle, shared[layer, 1:2, :], shared[layer, 3:4, :]).astype(
        jnp.bfloat16
    )


def load_units(layer, meta, pieces, w1, w2, sems):
    own, other, (lead, trail) = pieces[0:2], pieces[2:4], pieces[4:6]
    s, y, w = meta[0], meta[2], meta[8]
    copies = []
    for m, matrix in enumerate((w1, w2)):
        start_pick(
            (
                ((s == y) & (s == layer), own[m]),
                ((s == y) & (s != layer), other[m]),
                ((s != y) & (w == m), lead),
                ((s != y) & (w != m), trail),
            ),
            matrix,
            sems.at[m],
        )
        copies.append(pltpu.make_async_copy(own[m], matrix, sems.at[m]))
    return copies


def stack_rows(blocks, target):
    for i, block in enumerate(blocks):
        target[i * BLOCK : (i + 1) * BLOCK, :] = block[...]


def halve(total, keep, give):
    keep[...] = total[:BLOCK].astype(jnp.bfloat16)
    give[...] = total[BLOCK:].astype(jnp.bfloat16)


def units_kernel(layer, meta, n0, n1, bias, *rest):
    keep, give, slope_out, w1, w2, sems, n_buf, slope_buf, out_sem = rest[6:]
    waits = load_units(layer, meta, rest[:6], w1, w2, sems)
    stack_rows((n0, n1), n_buf)
    waits[0].wait()
    active, slope = gelu_both(mm(n_buf[...], w1[...]) + bias[layer, 0:1, :])
    slope_buf[...] = slope.astype(jnp.bfloat16)
    saving = pltpu.make_async_copy(slope_buf, slope_out, out_sem)
    saving.start()
    waits[1].wait()
    halve(mm(active.astype(jnp.bfloat16), w2[...]), keep, give)
    saving.wait()


def units_turn_kernel(layer, meta, n0, n1, g0, g1, bias, *rest):
    keep, give, out_keep, out_give, w1, w2, sems, n_buf, g_buf = rest[6:]
    waits = load_units(layer, meta, rest[:6], w1, w2, sems)
    stack_rows((n0, n1), n_buf)
    stack_rows((g0, g1), g_buf)
    for copy in waits:
        copy.wait()
    active, slope = gelu_both(mm(n_buf[...], w1[...]) + bias[layer, 0:1, :])
    grad_hidden = (mm_nt(g_buf[...], w2[...]) * slope).astype(jnp.bfloat16)
    halve(mm_nt(grad_hidden, w1[...]), keep, give)
    halve(mm(active.astype(jnp.bfloat16), w2[...]), out_keep, out_give)


def units_back_kernel(layer, meta, g0, g1, slope_in, *rest):
    keep, give, w1, w2, sems, g_buf, slope_buf, in_sem = rest[6:]
    waits = load_units(layer, meta, rest[:6], w1, w2, sems)
    fetch = pltpu.make_async_copy(slope_in, slope_buf, in_sem)
    fetch.start()
    stack_rows((g0, g1), g_buf)
    waits[1].wait()
    fetch.wait()
    grad = (mm_nt(g_buf[...], w2[...]) * slope_buf[...].astype(jnp.float32)).astype(jnp.bfloat16)
    waits[0].wait()
    halve(mm_nt(grad, w1[...]), keep, give)


def rows_first_kernel(meta, mine, crossed, far_mine, far_crossed, shared, *outs):
    holder = meta[0] == meta[1]
    upper = meta[2] == 0
    first = jnp.where(holder, mine[...], far_mine[...])
    second = jnp.where(holder, crossed[...], far_crossed[...])
    for c, (one, other) in enumerate(((first, second), (second, first))):
        rows = jnp.where(upper, one, other)
        outs[c][...] = rows
        outs[2 + c][...] = layer_norm(
            rows.astype(jnp.float32), shared[0, 0:1, :], shared[0, 2:3, :]
        ).astype(jnp.bfloat16)


def rows_next_kernel(middle, passed, far, shared, between_ref, normed_ref):
    between = (middle[...] + summed(passed, far) + shared[0, 5:6, :]).astype(jnp.bfloat16)
    between_ref[...] = between
    normed_ref[...] = layer_norm(
        between.astype(jnp.float32), shared[1, 0:1, :], shared[1, 2:3, :]
    ).astype(jnp.bfloat16)


def rows_turn_kernel(layer, middle, g_ref, passed, far, shared, grad_ref, sent_ref):
    grad_middle = g_ref[...].astype(jnp.float32) + norm_back(
        middle[...], shared[layer, 1:2, :], summed(passed, far)
    )
    grad_ref[...] = grad_middle
    sent_ref[...] = grad_middle.astype(jnp.bfloat16)


def rows_before_kernel(gm_ref, passed, far, between_ref, shared, grad_ref):
    grad_rows = gm_ref[...] + norm_back(
        between_ref[...].astype(jnp.float32), shared[1, 0:1, :], summed(passed, far)
    )
    grad_ref[...] = grad_rows.astype(jnp.bfloat16)


def rows_output_kernel(middle, passed, far, shared, wide_ref, narrow_ref):
    total = middle[...] + summed(passed, far) + shared[1, 5:6, :]
    wide_ref[...] = total
    narrow_ref[...] = total.astype(jnp.bfloat16)


def rows_final_kernel(gm_ref, passed, far, h_ref, shared, wide_ref, narrow_ref):
    grad_in = gm_ref[...] + norm_back(
        h_ref[...].astype(jnp.float32), shared[0, 0:1, :], summed(passed, far)
    )
    wide_ref[...] = grad_in
    narrow_ref[...] = grad_in.astype(jnp.bfloat16)


def units_call(kernel, meta, small, saved, weights, outs, saving, scratch, name):
    return pl.pallas_call(
        kernel,
        in_specs=[SMEM_SPACE] + [VMEM_SPACE] * len(small) + [HBM_SPACE] * (len(saved) + len(weights)),
        out_specs=[VMEM_SPACE] * len(outs) + [HBM_SPACE] * len(saving),
        out_shape=[*outs, *saving],
        scratch_shapes=scratch,
        compiler_params=kernel_params(24),
        cost_estimate=cost(2e9, 8e6),
        name=name,
    )(meta, *small, *saved, *weights)


def plain_call(kernel, scalar, small, large, outs, scratch, flops, name):
    specs = [VMEM_SPACE] * len(small) + [HBM_SPACE] * len(large)
    operands = (*small, *large)
    if scalar is not None:
        specs, operands = [SMEM_SPACE] + specs, (scalar, *operands)
    return pl.pallas_call(
        kernel,
        in_specs=specs,
        out_specs=[VMEM_SPACE] * len(outs),
        out_shape=outs,
        scratch_shapes=scratch,
        compiler_params=kernel_params(24),
        cost_estimate=cost(flops, 8e6),
        name=name,
    )(*operands)


def deal_rows(source, slots, section, y):
    same = lax.dynamic_index_in_dim(slots, y, 0, keepdims=False)
    cross = lax.dynamic_index_in_dim(slots, 1 - y, 0, keepdims=False)
    moved = send(same, lambda s, t: (t & 1, t) if s == source and s != t & 1 else None)
    crossed = send(cross, lambda s, t: (t & 1, t ^ 2) if s == source else None)
    mine = jnp.where(section == source, same, moved)
    return mine, crossed


def to_x(block):
    return send(block, lambda s, t: (s, t ^ 1) if s == t & 1 else None)


def from_x(block):
    return send(block, lambda s, t: (s, t ^ 1) if s != t & 1 else None)


def z_swap(block):
    size = lax.axis_size("dp")
    pairs = [
        ((s * size + z) * 4 + t, (s * size + (z ^ 1)) * 4 + t)
        for s in range(2) for z in range(size) for t in range(4) if s != t >> 1
    ]
    return lax.ppermute(block, ("section", "dp", "tensor"), pairs)


def early_sum(keep, give, swap=x_swap):
    take = jnp.concatenate([other_core(piece) for piece in jnp.split(give, 4)])
    passed = (keep.astype(jnp.float32) + take.astype(jnp.float32)).astype(jnp.bfloat16)
    return passed, swap(passed)


def chip_sum(keep, give, last, swap=x_swap):
    take = other_core(after(give, last))
    passed = (keep.astype(jnp.float32) + take.astype(jnp.float32)).astype(jnp.bfloat16)
    return passed, swap(passed)


def total_over_z(downs, ups):
    both = jnp.concatenate([jnp.concatenate(downs), jnp.concatenate(ups)], axis=1)
    size = lax.axis_size("dp")
    step = 1
    while step < size:
        both = both + lax.ppermute(both, "dp", [(i, i ^ step) for i in range(size)])
        step *= 2
    return both


def total_over_cores(both, section, y):
    both = both + y_swap(both)
    moved = other_core(both)
    down = both[:, :1024] + moved[:, :1024]
    down = jnp.where(section == 0, down[:LOW], down[LOW:])
    up = jnp.where(section == y, both[:, 1024:], moved[:, 1024:])
    return down + x_swap(down), jnp.where(section == 0, up[:LOW], up[LOW:])


def relay_body(
    activations, starts, attention_weights, projection_weight, feedforward_weight, output_weight,
    norm_gains, norm_biases, output_biases, query_value_bias, feedforward_bias,
    adapter_down_weight, adapter_up_weight,
):
    bf, f32 = jnp.bfloat16, jnp.float32
    section = lax.axis_index("section")
    place = lax.axis_index("tensor")
    y, x = place // 2, place % 2
    first = section == 0

    mine, crossed = deal_rows(0, activations[0], section, y)
    down_rows = adapter_down_weight[0].astype(f32).transpose(0, 2, 1).reshape(LOW, 1024)
    up0 = adapter_up_weight[0, 0].astype(f32)
    up1 = adapter_up_weight[0, 1].astype(f32)
    zero = jnp.zeros((ADAPTER_RANK, 256), f32)
    common = jnp.concatenate(
        [norm_gains[0], norm_biases[0], output_biases[0], jnp.zeros((2, 1024), f32), down_rows]
    )
    own_part = jnp.concatenate(
        [
            feedforward_bias,
            jnp.pad(query_value_bias[0].reshape(1, 512), ((0, 0), (0, 512))),
            jnp.zeros((6, 1024), f32),
            jnp.concatenate([up0, zero, jnp.zeros((ADAPTER_RANK, 512), f32)], axis=1),
            jnp.concatenate([zero, up1, jnp.zeros((ADAPTER_RANK, 512), f32)], axis=1),
        ]
    )
    partner = other_core(common)
    partner_part = other_core(own_part)
    parts = jnp.where(
        first, jnp.stack([own_part, partner_part]), jnp.stack([partner_part, own_part])
    )
    near_varied = jnp.where(section == y, parts, y_swap(parts))
    shared = jnp.where(first, jnp.stack([common, partner]), jnp.stack([partner, common]))
    meta = jnp.concatenate(
        [
            jnp.stack([section, x, y, place]).astype(jnp.int32),
            lax.dynamic_index_in_dim(starts, y, 0, keepdims=False).reshape(4),
            (lax.axis_index("dp") % 2).astype(jnp.int32)[None],
        ]
    )
    even = lax.axis_index("dp") % 2 == 0
    own_a = jnp.concatenate([attention_weights[0], projection_weight[0].T[None]])
    w1_own, w2_own = feedforward_weight[0], output_weight[0]
    other_a = other_core(own_a)
    g_mine, g_crossed = deal_rows(1, activations[0], section, y)
    mine, crossed, shared, g_mine, g_crossed = lax.optimization_barrier(
        (mine, crossed, shared, g_mine, g_crossed)
    )
    lead_a0 = cross_send(after(jnp.where(even, own_a[:2], own_a[2:]), crossed, near_varied))
    far_mine, far_crossed = to_x(mine), to_x(crossed)
    trail_a0 = z_swap(after(lead_a0, far_mine, far_crossed))

    sheet = jax.ShapeDtypeStruct((BLOCK, 1024), f32)
    thin = jax.ShapeDtypeStruct((BLOCK, 1024), bf)
    slope_shape = jax.ShapeDtypeStruct((CHUNK, 1024), bf)
    matrices = [
        pltpu.VMEM((1024, 1024), bf), pltpu.VMEM((1024, 1024), bf), pltpu.SemaphoreType.DMA((2,))
    ]
    group = pltpu.VMEM((CHUNK, 1024), bf)

    def small(kernel, *operands, outs, name):
        return plain_call(kernel, None, operands, (), outs, [], 1e7, name)

    def attend(layer, chunk, normed, before, weight, near=None):
        near = other_core(normed) if near is None else near
        return attend_call(
            layer, chunk, meta, (normed, near), before, shared, near_varied, weight
        )

    def units(layer, normed, weight):
        return units_call(
            functools.partial(units_kernel, layer), meta, (normed, other_core(normed), near_varied),
            (), weight, [thin, thin], [slope_shape],
            [*matrices, group, group, pltpu.SemaphoreType.DMA], "units",
        )

    def units_turn(layer, normed, grad, near_grad, weight):
        return units_call(
            functools.partial(units_turn_kernel, layer), meta,
            (normed, other_core(normed), grad, near_grad, near_varied), (), weight,
            [thin] * 4, [], [*matrices, group, group], "units_turn",
        )

    def units_back(layer, grad, slope, weight):
        return units_call(
            functools.partial(units_back_kernel, layer), meta, (grad, other_core(grad)), (slope,),
            weight, [thin, thin], [], [*matrices, group, group, pltpu.SemaphoreType.DMA],
            "units_back",
        )

    def middle(layer, rows, sums):
        return small(
            functools.partial(rows_middle_kernel, layer), rows, *sums, shared, outs=[sheet, thin],
            name="rows_middle",
        )

    def turn(layer, middle_rows, grad, sums):
        return small(
            functools.partial(rows_turn_kernel, layer), middle_rows, grad, *sums, shared,
            outs=[sheet, thin], name="rows_turn",
        )

    row0, row1, n0, n1 = plain_call(
        rows_first_kernel, meta, (mine, crossed, far_mine, far_crossed, shared), (), [thin] * 4,
        [], 1e7, "rows_first",
    )
    g_far = [to_x(one) for one in (g_mine, g_crossed)]
    weights_a0 = (own_a, other_a, lead_a0, trail_a0)
    near_n0 = other_core(n0)
    lead_b0 = cross_send(jnp.where(even, *after((w1_own, w2_own), near_n0)))
    n00, n01 = n0, n1
    saved00, keep, give = attend(0, 0, n0, (), weights_a0, near_n0)
    keep, give, g_far = lax.optimization_barrier((keep, give, g_far))
    sum0 = chip_sum(keep, give, lead_a0)
    other_w1, other_w2 = (other_core(after(one, sum0[0])) for one in (w1_own, w2_own))
    trail_b0 = z_swap(after(lead_b0, sum0[0]))
    weights_b0 = (w1_own, w2_own, other_w1, other_w2, lead_b0, trail_b0)
    saved01, keep, give = attend(0, 1, n1, saved00[1:3], weights_a0)
    sum1 = chip_sum(keep, give, sum0[1])
    lead_a1 = cross_send(jnp.where(even, *after((other_a[:2], other_a[2:]), sum0[0])))
    middle00, n0 = middle(0, row0, sum0)
    keep, give, slope0 = units(0, n0, weights_b0)
    sum2 = chip_sum(keep, give, sum1[1])
    sum1, lead_a1 = lax.optimization_barrier((sum1, lead_a1))
    trail_a1 = z_swap(lead_a1)
    lead_b1 = cross_send(jnp.where(even, *after((other_w1, other_w2), lead_a1)))
    middle01, n1 = middle(0, row1, sum1)
    keep, give, slope1 = units(0, n1, weights_b0)
    sum3 = chip_sum(keep, give, sum2[1])
    sum2, trail_a1 = lax.optimization_barrier((sum2, trail_a1))
    weights_a1 = (own_a, other_a, lead_a1, trail_a1)
    between0, n10 = small(rows_next_kernel, middle00, *sum2, shared, outs=[thin, thin], name="rows_next")
    saved10, keep, give = attend(1, 0, n10, (), weights_a1)
    sum4 = chip_sum(keep, give, sum3[1])
    sum3, lead_b1 = lax.optimization_barrier((sum3, lead_b1))
    trail_b1 = z_swap(lead_b1)
    weights_b1 = (w1_own, w2_own, other_w1, other_w2, lead_b1, trail_b1)
    between1, n11 = small(rows_next_kernel, middle01, *sum3, shared, outs=[thin, thin], name="rows_next")
    saved11, keep, give = attend(1, 1, n11, saved10[1:3], weights_a1)
    sum5 = chip_sum(keep, give, sum4[1])
    holder, upper = section == x, y == 0
    mine, crossed = (
        jnp.where(holder, one, two) for one, two in zip((g_mine, g_crossed), after(g_far, sum4[0]))
    )
    grad_outs = (jnp.where(upper, mine, crossed), jnp.where(upper, crossed, mine))
    near_outs = [other_core(one) for one in grad_outs]
    middle10, m0 = middle(1, between0, sum4)
    keep, give, out_keep0, out_give0 = units_turn(1, m0, grad_outs[0], near_outs[0], weights_b1)
    sum6 = chip_sum(keep, give, sum5[1])
    middle11, m1 = middle(1, between1, sum5)
    keep, give, out_keep1, out_give1 = units_turn(1, m1, grad_outs[1], near_outs[1], weights_b1)
    sum7 = chip_sum(keep, give, sum6[1])
    grad_middle10, g0 = turn(1, middle10, grad_outs[0], sum6)
    grad_middle11, g1 = turn(1, middle11, grad_outs[1], sum7)
    keep, give, down1, up1, dk, dv = attend_back_call(
        1, 1, meta, (n11, other_core(n11)), (g1, other_core(g1)), (saved10, saved11), (), shared,
        near_varied, weights_a1,
    )
    out_sums = [
        chip_sum(*after(one, g1), sum7[1], from_x)
        for one in ((out_keep0, out_give0), (out_keep1, out_give1))
    ]
    keep, give, out_sums = lax.optimization_barrier((keep, give, out_sums))
    sum8 = chip_sum(keep, give, sum7[1])
    keep, give, down1, up1 = attend_back_call(
        1, 0, meta, (n10, other_core(n10)), (g0, other_core(g0)), (saved10, saved11),
        (dk, dv, down1, up1), shared, near_varied, weights_a1,
    )
    sum9 = chip_sum(keep, give, sum8[1])
    before1 = small(
        rows_before_kernel, grad_middle11, *after(sum8, keep), between1, shared, outs=[thin], name="rows_before"
    )[0]
    keep, give = units_back(0, before1, slope1, weights_b0)
    sum10 = early_sum(keep, give)
    sum9 = (sum9[0], after(sum9[1], sum10[0]))
    before0 = small(
        rows_before_kernel, grad_middle10, *sum9, between0, shared, outs=[thin], name="rows_before"
    )[0]
    keep, give = units_back(0, before0, slope0, weights_b0)
    sum11 = early_sum(keep, give)
    sum10 = (sum10[0], after(sum10[1], sum11[0]))
    grad_middle01, h1 = turn(0, middle01, before1, sum10)
    keep, give, down0, up0, dk, dv = attend_back_call(
        0, 1, meta, (n01, other_core(n01)), (h1, other_core(h1)), (saved00, saved01), (), shared,
        near_varied, weights_a0,
    )
    sum12 = early_sum(keep, give, from_x)
    sum11 = (sum11[0], after(sum11[1], sum12[0]))
    grad_middle00, h0 = turn(0, middle00, before0, sum11)
    keep, give, down0, up0 = attend_back_call(
        0, 0, meta, (n00, other_core(n00)), (h0, other_core(h0)), (saved00, saved01),
        (dk, dv, down0, up0), shared, near_varied, weights_a0,
    )
    sum13 = early_sum(keep, give, from_x)
    sum12 = (sum12[0], after(sum12[1], sum13[0]))
    outs = [
        small(rows_output_kernel, one, *after(two, sum13[0]), shared, outs=[sheet, thin],
              name="rows_output")
        for one, two in zip((middle10, middle11), out_sums)
    ]
    out_wide = jnp.where(upper, outs[0][0], outs[1][0])
    out_same, out_cross = collect(1, out_wide, jnp.where(upper, outs[1][1], outs[0][1]))
    totals = total_over_z((down0, down1), after((up0, up1), sum13[0]))
    sum13, totals = lax.optimization_barrier((sum13, totals))
    ends = [
        small(rows_final_kernel, one, *two, three, shared, outs=[sheet, thin], name="rows_final")
        for one, two, three in ((grad_middle00, sum13, row0), (grad_middle01, sum12, row1))
    ]
    wide = jnp.where(upper, ends[0][0], ends[1][0])
    in_same, in_cross = collect(0, wide, jnp.where(upper, ends[1][1], ends[0][1]))
    grad_down, grad_up = total_over_cores(totals, section, y)
    same = jnp.where(
        first, jnp.where(x == 0, wide, in_same), jnp.where(x == 1, out_wide, out_same)
    )
    cross = jnp.where(first, in_cross, out_cross).astype(f32)
    combined = jnp.where(y == 0, jnp.stack([same, cross]), jnp.stack([cross, same]))
    return (
        combined[None],
        grad_down.reshape(1, 2, ADAPTER_RANK, 1024).transpose(0, 1, 3, 2),
        jnp.stack([grad_up[:ADAPTER_RANK, :256], grad_up[ADAPTER_RANK:, 256:]])[None],
    )


def body(*arrays):
    dp = lax.axis_size("dp")
    known = (
        arrays[0].shape == (1, 2, BLOCK, 1024)
        and lax.axis_size("tensor") == 4
        and lax.axis_size("section") == 2
        and arrays[3].shape == (1, 256, 1024)
        and arrays[5].shape == (1, 1024, 1024)
        and dp & (dp - 1) == 0
    )
    return relay_body(*arrays) if known else plain_body(*arrays)


def solution(mesh):
    placed = (
        P("section", None, ("dp", "tensor"), None),
        P(None, "dp", None),
        P("section", None, None, "tensor"),
        P("section", "tensor", None),
        P("section", None, "tensor"),
        P("section", "tensor", None),
        P("section", None, None),
        P("section", None, None),
        P("section", None, None),
        P("section", None, "tensor"),
        P("section", "tensor"),
        P("section", None, None, None),
        P("section", None, None, "tensor"),
    )
    return jax.shard_map(
        body,
        mesh=mesh,
        in_specs=placed,
        out_specs=(
            P("section", None, ("dp", "tensor"), None),
            P("section", None, None, None),
            P("section", None, None, "tensor"),
        ),
        check_vma=False,
    )
```
